128 devices in a mesh: row: 8 (over z_lo, y), col: 16 (over x, z_hi, core).
Axes of the slice: x: 4, y: 4, z: 4 (z_hi: 2, z_lo: 2; z = z_hi * 2 + z_lo), core: 2. Of those that a mesh axis runs over, the one named last changes fastest.
Arguments:
- moisture: float32 [4, 524288], P(None, ('row', 'col')), may hold values from 0.05 to 0.4
- conduct: float32 [4, 524288], P(None, ('row', 'col')), may hold values from 0.01 to 0.1
- rainfall: float32 [524288], P(('row', 'col')), may hold values from 0.2 to 1.5
- weights: float32 [100, 524288], P(None, ('row', 'col')), may hold values from 0.2 to 5
- land_tile: int32 [524288], P(('row', 'col')), may hold values from 0 to 127, as said below
- head: float32 [5120, 10240], P('row', 'col'), may hold values from 0 to 0.5
- rate: float32 [5120, 10240], P('row', 'col'), may hold values from 0.2 to 5
- flow_code: int32 [5120, 10240], P('row', 'col'), may hold values from 0 to 7
- lake_slot: int32 [5120, 10240], P('row', 'col'), may hold values from 0 to 64, as said below
- lake_table: int32 [8192], P(('row', 'col')), may hold values from 0 to 8191, as said below
- lake_phase: float32 [8192], P(('row', 'col')), may hold values from 0.5 to 2
- lake_area: float32 [8192], P(('row', 'col')), may hold values from 100 to 1000
- lake_crest: float32 [8192], P(('row', 'col')), may hold values from 0.5 to 3
Outputs:
- new_moisture: float32 [4, 524288], P(None, ('row', 'col'))
- surface: float32 [5120, 10240], P('row', 'col')
- level: float32 [8192], P(('row', 'col'))
- outflow: float32 [8192], P(('row', 'col'))
The draws below stay inside these ranges and needn't reach their ends.
Inputs may be any that keep to these rules, and one draw needn't show every extreme that they name: `land_tile`: the 4096 blocks of one device form aligned runs of 32 blocks; each run goes whole to one tile, different runs of a device to different tiles, and every tile receives each block position exactly once. `lake_slot`: the value 64 marks cells outside lakes; the cells of one slot lie within one rectangle of the tile. `lake_table`: lake k is owned by device k // 64 of the joined axis; a slot may name a lake of any owner.
All inputs are finite; a program needn't handle non-finite values.
Results may differ from the reference program's by a relative error of at most 0.00019.
Values sent between devices are 32-bit elements; how exact they have to be, the bound alone decides.
No kernel may reach another device: no remote copies, remote signals or barrier semaphores. Data moves between devices by JAX's collectives and lax.ppermute only.
A program may use at most 192 MiB of HBM per device.

```python
import math
import jax
import jax.numpy as jnp
from jax import lax

AGG = 10
LAYERS = 4
SUBSTEPS = 2
BX = 64
BY = 64
LLOC = 64
LAKE_DEV = 64
AGG2 = 100
BPD = 4096
NBLK = 524288
RX = 640
RY = 640
NX = 5120
NY = 10240
NLAKE = 8192
SLOTS = 8192
N_ROW = 8
N_COL = 16


def draw_land_tile(key, part):
    key = jax.random.fold_in(key, 11)
    blocks = BX * BY
    device_count = NBLK // blocks
    capacity = blocks // device_count
    first_key, second_key, third_key = jax.random.split(key, 3)
    perm_a = jax.random.permutation(first_key, device_count)
    perm_b = jax.random.permutation(second_key, device_count)
    shifts = jax.random.permutation(third_key, device_count)
    source = jnp.arange(device_count)[:, None]
    group = jnp.arange(blocks)[None, :] // capacity
    tiles_of = perm_b[(perm_a[source] + shifts[group]) % device_count]
    return tiles_of.reshape(-1).astype(jnp.int32)


def draw_lake_slot(key, part):
    key = jax.random.fold_in(key, 23)
    tiles_r = NX // RX
    tiles_c = NY // RY
    keys = jax.random.split(key, 4)
    shape = (tiles_r, tiles_c, LLOC)
    center_r = jax.random.randint(keys[0], shape, 0, RX)
    center_c = jax.random.randint(keys[1], shape, 0, RY)
    half_r = jax.random.randint(keys[2], shape, 4, 10)
    half_c = jax.random.randint(keys[3], shape, 4, 10)
    local_r = jnp.arange(RX, dtype=jnp.int32)[None, :, None, None]
    local_c = jnp.arange(RY, dtype=jnp.int32)[None, None, None, :]

    def paint(step, slots):
        slot = LLOC - 1 - step
        rows_in = jnp.abs(local_r - center_r[:, None, :, None, slot]) < half_r[:, None, :, None, slot]
        cols_in = jnp.abs(local_c - center_c[:, None, :, None, slot]) < half_c[:, None, :, None, slot]
        return jnp.where(rows_in & cols_in, slot, slots)
    start = jnp.full((tiles_r, RX, tiles_c, RY), LLOC, jnp.int32)
    slots = lax.fori_loop(0, LLOC, paint, start)
    return slots.reshape(NX, NY).astype(jnp.int32)


def draw_lake_table(key, part):
    key = jax.random.fold_in(key, 29)
    local_key, pick_key, owner_key = jax.random.split(key, 3)
    device_count = SLOTS // LLOC
    index = jnp.arange(SLOTS, dtype=jnp.int32)
    tile = index // LLOC
    slot = index % LLOC
    owner = jnp.where(slot == 1, (tile + 1) % device_count, tile)
    owner = jnp.where(slot == 2, (tile + device_count // 2) % device_count, owner)
    owner = jnp.where(slot == 3, (tile + device_count - 1) % device_count, owner)
    picked = (jax.random.randint(pick_key, (SLOTS,), 0, 4) == 0) & (slot >= 4) & (slot < LLOC - 1)
    anywhere = jax.random.randint(owner_key, (SLOTS,), 0, device_count)
    owner = jnp.where(picked, anywhere, owner)
    local = jax.random.randint(local_key, (SLOTS,), 0, LAKE_DEV)
    local = jnp.where(slot == 0, 0, jnp.where(slot == LLOC - 1, LAKE_DEV - 1, local))
    return (owner * LAKE_DEV + local).astype(jnp.int32)


def with_ends(result, own_key, low, top_value):
    spot = [jax.random.randint(jax.random.fold_in(own_key, axis), (), 0, length) for axis, length in enumerate(result.shape)]
    longest = result.shape.index(max(result.shape))
    next_to = spot[:longest] + [(spot[longest] + 1) % result.shape[longest]] + spot[longest + 1:]
    return result.at[tuple(spot)].set(low).at[tuple(next_to)].set(top_value)


def shard_levels(key, extent, cuts, low, largest):
    loudness = 1.0
    for position, blocks in cuts:
        steps = jax.random.uniform(jax.random.fold_in(jax.random.fold_in(key, 6), position), (blocks,), jnp.float32, low / len(cuts), largest / len(cuts))
        loudness = loudness * jnp.repeat(jnp.exp(steps), extent[position] // blocks).reshape((-1,) + (1,) * (len(extent) - 1 - position))
    return loudness


def setup_inputs(seed: int = 0) -> dict:
    seeds = jax.random.split(jax.random.key(seed), 14)
    moisture = jnp.clip(0.05 + 0.35 * jax.random.uniform(seeds[0], (LAYERS, NBLK), jnp.float32) ** shard_levels(seeds[0], (LAYERS, NBLK), ((1, 128),), -0.2, 0.2), 0.05, 0.4)
    conduct = jnp.clip(jnp.exp(math.log(0.1) - 2.3025851 * jax.random.uniform(seeds[1], (LAYERS, NBLK), jnp.float32) ** shard_levels(seeds[1], (LAYERS, NBLK), ((1, 128),), -0.2, 0.2)), 0.01, 0.1)
    rainfall = jnp.clip(0.2 + 1.3 * jax.random.uniform(seeds[2], (NBLK,), jnp.float32) ** shard_levels(seeds[2], (NBLK,), ((0, 128),), -0.2, 0.2), 0.2, 1.5)
    weights = jnp.clip(jnp.exp(math.log(5.0) - 3.218876 * jax.random.uniform(seeds[3], (AGG2, NBLK), jnp.float32) ** shard_levels(seeds[3], (AGG2, NBLK), ((1, 128),), -0.2, 0.2)), 0.2, 5.0)
    land_tile = draw_land_tile(jax.random.fold_in(seeds[13], 71), 0)
    head = jnp.clip(0.5 * jax.random.uniform(seeds[5], (NX, NY), jnp.float32) ** shard_levels(seeds[5], (NX, NY), ((0, 8), (1, 16)), -0.2, 0.2), 0.0, 0.5)
    rate = jnp.clip(jnp.exp(math.log(5.0) - 3.218876 * jax.random.uniform(seeds[6], (NX, NY), jnp.float32) ** shard_levels(seeds[6], (NX, NY), ((0, 8), (1, 16)), -0.2, 0.2)), 0.2, 5.0)
    flow_code = with_ends(jax.random.randint(seeds[7], (NX, NY), 0, 8), jax.random.fold_in(seeds[7], 1), 0, 7).astype(jnp.int32)
    lake_slot = draw_lake_slot(jax.random.fold_in(seeds[13], 71), 0)
    lake_table = draw_lake_table(jax.random.fold_in(seeds[13], 71), 0)
    lake_phase = jnp.clip(0.5 + 1.5 * jax.random.uniform(seeds[10], (NLAKE,), jnp.float32) ** shard_levels(seeds[10], (NLAKE,), ((0, 128),), -0.2, 0.2), 0.5, 2.0)
    lake_area = jnp.clip(jnp.exp(math.log(1000.0) - 2.3025851 * jax.random.uniform(seeds[11], (NLAKE,), jnp.float32) ** shard_levels(seeds[11], (NLAKE,), ((0, 128),), -0.2, 0.2)), 100.0, 1000.0)
    lake_crest = jnp.clip(0.5 + 2.5 * jax.random.uniform(seeds[12], (NLAKE,), jnp.float32) ** shard_levels(seeds[12], (NLAKE,), ((0, 128),), -0.2, 0.2), 0.5, 3.0)
    return {"moisture": moisture, "conduct": conduct, "rainfall": rainfall, "weights": weights, "land_tile": land_tile, "head": head, "rate": rate, "flow_code": flow_code, "lake_slot": lake_slot, "lake_table": lake_table, "lake_phase": lake_phase, "lake_area": lake_area, "lake_crest": lake_crest}


LAYER_DEPTHS = (0.1, 0.3, 0.6, 1.0)
POROSITY = 0.45
TIME_STEP = 0.05
OFFSETS = ((0, 1), (1, 1), (1, 0), (1, -1), (0, -1), (-1, -1), (-1, 0), (-1, 1))

def land_update(moisture, conduct, rainfall):
    saturation = moisture / POROSITY
    capacity = 10.0 * conduct[0] * (1.5 - saturation[0])
    infiltration = rainfall * capacity / (rainfall + capacity)
    drainage = conduct * saturation ** 4
    incoming = jnp.concatenate([infiltration[None, :], drainage[:-1]], axis=0)
    thickness = jnp.array(LAYER_DEPTHS, jnp.float32)[:, None]
    new_moisture = moisture + TIME_STEP * (incoming - drainage) / thickness
    return (new_moisture, rainfall - infiltration)

def route(surface, rate, padded_code):
    row_count, col_count = surface.shape
    conveyance = rate * surface ** (2.0 / 3.0)
    leaving = surface * conveyance / (1.0 + conveyance)
    padded = jnp.pad(leaving, 1)
    gained = jnp.zeros_like(surface)
    for direction, (delta_x, delta_y) in enumerate(OFFSETS):
        source = padded[1 - delta_x:1 - delta_x + row_count, 1 - delta_y:1 - delta_y + col_count]
        source_code = padded_code[1 - delta_x:1 - delta_x + row_count, 1 - delta_y:1 - delta_y + col_count]
        gained = gained + jnp.where(source_code == direction, source, 0.0)
    return surface - leaving + gained

def level_pool(lake_phase, inflow, lake_area, lake_crest):
    phase = lake_phase + inflow / lake_area
    excess = jnp.maximum(phase - lake_crest, 0.0)
    outflow = excess * jnp.sqrt(excess)
    return (phase - outflow / lake_area, outflow)

def reference(moisture, conduct, rainfall, weights, land_tile, head, rate, flow_code, lake_slot, lake_table, lake_phase, lake_area, lake_crest):
    new_moisture, runoff = land_update(moisture, conduct, rainfall)
    cell_depth = runoff[None, :] * weights / lax.optimization_barrier(jnp.mean(weights, axis=0, keepdims=True))
    slot_index = jnp.arange(NBLK, dtype=jnp.int32) % BPD
    target = land_tile * BPD + slot_index
    placed = jnp.zeros_like(cell_depth).at[:, target].set(cell_depth)
    relaid = placed.reshape(AGG, AGG, N_ROW, N_COL, BX, BY).transpose(2, 4, 0, 3, 5, 1).reshape(NX, NY)
    surface = head + relaid
    tile_row = (jnp.arange(NX, dtype=jnp.int32) // RX)[:, None]
    tile_col = (jnp.arange(NY, dtype=jnp.int32) // RY)[None, :]
    lake_here = lake_slot < LLOC
    flat_index = (tile_row * N_COL + tile_col) * LLOC + jnp.minimum(lake_slot, LLOC - 1)
    lake_id = jnp.where(lake_here, lake_table[flat_index], NLAKE).astype(jnp.int32)
    padded_code = jnp.pad(flow_code, 1)
    inflow = jnp.zeros((NLAKE,), jnp.float32)
    for substep in range(SUBSTEPS):
        surface = route(surface, rate, padded_code)
        inflow = inflow + jax.ops.segment_sum(surface.reshape(-1), lake_id.reshape(-1), NLAKE + 1)[:NLAKE]
        surface = jnp.where(lake_here, 0.0, surface)
    level, outflow = level_pool(lake_phase, inflow, lake_area, lake_crest)
    return (new_moisture, surface, level, outflow)
```

```python
import jax
import jax.numpy as jnp
import numpy as np
from jax import lax
from jax.experimental import pallas as pl
from jax.experimental.pallas import tpu as pltpu
from jax.sharding import PartitionSpec as P

AGG = 10
LLOC = 64
LANES = 128
RUNS = 128
RUN_ROWS = 26
SLABS = 6
ROWS = 672
FIRST = 16

LAYER_DEPTHS = (0.1, 0.3, 0.6, 1.0)
POROSITY = 0.45
TIME_STEP = 0.05
F32 = jnp.float32
BF16 = jnp.bfloat16
VMEM = pl.BlockSpec(memory_space=pltpu.VMEM)
SMEM = pl.BlockSpec(memory_space=pltpu.SMEM)


def params(mebibytes):
    return pltpu.CompilerParams(vmem_limit_bytes=mebibytes * 1024 * 1024)


def lanes_of(shape):
    return lax.broadcasted_iota(jnp.int32, shape, len(shape) - 1)


def rows_of(shape):
    return lax.broadcasted_iota(jnp.int32, shape, 0)


def split3(value):
    high = value.astype(BF16)
    rest = value - high.astype(F32)
    middle = rest.astype(BF16)
    low = (rest - middle.astype(F32)).astype(BF16)
    return high, middle, low


def select_dot(picks, value):
    return sum(jnp.dot(picks, part, preferred_element_type=F32) for part in split3(value))


def dot_select(value, picks):
    return sum(jnp.dot(part, picks, preferred_element_type=F32) for part in split3(value))


def quarter_transpose(arrays, quarter):
    rolled = []
    for d in range(4):
        skew = arrays[(3 + d) % 4]
        for m in range(3):
            skew = jnp.where(quarter == m, arrays[(m + d) % 4], skew)
        rolled.append(pltpu.roll(skew, 32 * d, 1) if d else skew)
    outs = []
    for r in range(4):
        out = rolled[(3 - r) % 4]
        for m in range(3):
            out = jnp.where(quarter == m, rolled[(m - r) % 4], out)
        outs.append(out)
    return outs


def send_kernel(tile_ref, moisture_ref, conduct_ref, rain_ref, weights_ref, out_ref, slab_ref, edge_ref, sems):
    count = slab_ref.shape[0]

    def fetch(i):
        start = pl.multiple_of(i * LANES, LANES)
        return pltpu.make_async_copy(weights_ref.at[:, pl.ds(start, LANES)], slab_ref.at[i], sems.at[i])

    def begin(i, carry):
        fetch(i).start()
        return carry

    lax.fori_loop(0, count, begin, 0)
    lane = lanes_of((1, LANES))
    quarter = lane >> 5

    def step(i, carry):
        edges, tiles = carry
        start = pl.multiple_of(i * LANES, LANES)
        conduct = conduct_ref[0:1, pl.ds(start, LANES)]
        moisture = moisture_ref[0:1, pl.ds(start, LANES)]
        rain = rain_ref[0:1, pl.ds(start, LANES)]
        capacity = 10.0 * conduct * (1.5 - moisture / POROSITY)
        runoff = rain - rain * capacity / (rain + capacity)
        fetch(i).wait()
        parts = [slab_ref[i, pl.ds(b, AGG, stride=AGG), :] for b in range(AGG)]
        total = sum(parts[1:], parts[0])
        mean = jnp.sum(total, axis=0, keepdims=True) * 0.01
        scale = runoff / mean
        parts = [part * scale for part in parts]
        tail = [slab_ref[i, pl.ds(first, 5, stride=AGG), :] * scale for first in (8, 9, 58, 59)]
        groups = (
            (0, AGG, quarter_transpose(parts[0:4], quarter)),
            (AGG, AGG, quarter_transpose(parts[4:8], quarter)),
            (2 * AGG, 5, quarter_transpose(tail, quarter)),
        )
        for r in range(4):
            tile = tile_ref[(4 * i + r) * 32]
            tiles = jnp.where(lane == 32 * r + i, tile, tiles)
            for offset, length, outs in groups:
                out_ref[pl.ds(tile * RUN_ROWS + offset, length), :] = outs[r]
        place = lane & 63
        new_edges = []
        for b in range(2):
            left = pltpu.roll(parts[b], i, 1)
            right = pltpu.roll(parts[8 + b], i + 97, 1)
            edge = jnp.where(place == i, left, edges[b])
            new_edges.append(jnp.where(place == i + 32, right, edge))
        return tuple(new_edges), tiles

    zeros = jnp.zeros((AGG, LANES), F32)
    edges, tiles = lax.fori_loop(0, count, step, ((zeros, zeros), jnp.zeros((1, LANES), jnp.int32)))
    edge_ref[...] = jnp.zeros((LANES, LANES), F32)
    edge_ref[0:AGG, :] = edges[0]
    edge_ref[16 : 16 + AGG, :] = edges[1]
    edge_ref[15:16, :] = (4 * (lane & 31) + (lane >> 5)).astype(F32)
    by_run = edge_ref[...].T
    square = (LANES, LANES)
    here = (rows_of(square) == tiles).astype(F32).astype(BF16)
    by_tile = select_dot(here, by_run)
    run = by_tile[:, 15:16].astype(jnp.int32)
    wide = lanes_of(square)
    cell = wide & 15
    odd = (run & 1) == 1
    no_edge = jnp.where(wide == 15, -1.0, 0.0)
    low = cell < 2
    high = (cell == 8) | (cell == 9)

    def moved(picked, down, across):
        value = pltpu.roll(picked, down % LANES, 0)
        return pltpu.roll(value, across, 1) if across else value

    def corner(number, cells):
        return jnp.where((run == number) & cells, by_tile, 0.0)

    row = moved(jnp.where(odd, by_tile, no_edge), 1, 0)
    row = row + moved(jnp.where(odd, no_edge, by_tile), -1, 32)
    row = row + moved(corner(127, high), 17, 64) + moved(corner(1, low), -15, 64)
    row = row + moved(corner(126, high), 15, 96) + moved(corner(0, low), -17, 96)
    row = row + jnp.where(wide == 127, run.astype(F32), 0.0)
    out_ref[pl.ds(25, RUNS, stride=RUN_ROWS), :] = row


def land_payload(land_tile, moisture, conduct, rainfall, weights):
    blocks = weights.shape[1]
    count = blocks // LANES
    return pl.pallas_call(
        send_kernel,
        out_shape=jax.ShapeDtypeStruct((RUNS * RUN_ROWS, LANES), F32),
        in_specs=[SMEM, VMEM, VMEM, VMEM, pl.BlockSpec(memory_space=pl.ANY)],
        out_specs=VMEM,
        scratch_shapes=[
            pltpu.VMEM((count, AGG * AGG, LANES), F32),
            pltpu.VMEM((LANES, LANES), F32),
            pltpu.SemaphoreType.DMA((count,)),
        ],
        compiler_params=params(12),
        name="land",
    )(land_tile, moisture, conduct, rainfall.reshape(1, blocks), weights)


def spread_columns():
    picks = np.zeros((SLABS * LANES, 640), np.float32)
    for half in range(2):
        for j in range(3):
            for k in range(4 if j < 2 else 2):
                for i in range(32):
                    picks[(half * 3 + j) * LANES + 32 * k + i, (half * 32 + i) * AGG + 4 * j + k] = 1.0
    return picks


def place_kernel(pay_ref, head_ref, side_ref, picks_ref, depth_ref, top_ref, bottom_ref, cells_ref, tag_ref, tags, sem):
    arrived = pay_ref[pl.ds(25, RUNS, stride=RUN_ROWS), :]
    by_lane = arrived.T
    tag_ref[...] = jnp.broadcast_to(by_lane[127:128, :].astype(jnp.int32), (8, LANES))
    copy = pltpu.make_async_copy(tag_ref, tags, sem)
    copy.start()
    copy.wait()

    def settle(s, carry):
        run = tags[0, s]
        slab = (run & 1) * 3
        row = (run >> 1) * AGG
        start = s * RUN_ROWS
        cells_ref[slab, pl.ds(row, AGG), :] = pay_ref[pl.ds(start, AGG), :]
        cells_ref[slab + 1, pl.ds(row, AGG), :] = pay_ref[pl.ds(start + AGG, AGG), :]
        last = pay_ref[pl.ds(start + 2 * AGG, 5), :]
        cells_ref[slab + 2, pl.ds(row, 5), :] = last
        cells_ref[slab + 2, pl.ds(row + 5, 5), :] = pltpu.roll(last, 64, 1)
        return carry

    lax.fori_loop(0, RUNS, settle, 0, unroll=4)
    picks = picks_ref[...]
    chunk = 160
    for m in range(0, 640, chunk):
        cells = jnp.concatenate([cells_ref[c, m : m + chunk, :] for c in range(SLABS)], axis=1)
        laid = dot_select(cells, picks)
        for c in range(SLABS - 1):
            columns = slice(c * LANES, (c + 1) * LANES)
            depth = laid[:, columns] + head_ref[m : m + chunk, columns]
            depth_ref[c, FIRST + m : FIRST + m + chunk, :] = depth
            if m == 0:
                top_ref[:, columns] = depth[0:8]
            if m == 640 - chunk:
                bottom_ref[:, columns] = depth[chunk - 8 :]

    tall = (640, LANES)
    row = rows_of(tall)
    block = (row * 6554) >> 16
    lane = lanes_of(tall)
    left = (by_lane[15:16, :].astype(jnp.int32) == 2 * block + 1).astype(F32).astype(BF16)
    right = (by_lane[47:48, :].astype(jnp.int32) == 2 * block).astype(F32).astype(BF16)
    square = (LANES, LANES)
    wide = lanes_of(square)
    strips = select_dot(left, jnp.where(wide < 32, arrived, 0.0))
    strips = strips + select_dot(right, jnp.where((wide >= 32) & (wide < 64), arrived, 0.0))
    strips = jnp.where((lane & 15) == row - AGG * block, strips, 0.0)
    corners = jnp.sum(arrived, axis=0, keepdims=True)
    flat = (8, LANES)
    cell = lanes_of(flat) & 15
    late = lanes_of(flat) >= 64
    above = jnp.where(late & (cell == rows_of(flat) + 2), corners, 0.0)
    below = jnp.where(late & (cell == rows_of(flat)), corners, 0.0)
    source = rows_of(square)
    group = source >> 4
    target = jnp.where((group & 2) == 0, 126, 0) + (group & 1)
    fold = (((source & 15) < AGG) & (target == wide)).astype(F32).astype(BF16)
    depth_ref[SLABS - 1, 8:FIRST, :] = dot_select(above, fold) + side_ref[0:8, :]
    depth_ref[SLABS - 1, FIRST : FIRST + 640, :] = dot_select(strips, fold) + side_ref[8:648, :]
    depth_ref[SLABS - 1, FIRST + 640 : FIRST + 648, :] = dot_select(below, fold) + side_ref[648:656, :]


def place(payload, head, side):
    picks = jnp.asarray(spread_columns(), BF16)
    strip = jax.ShapeDtypeStruct((8, 640), F32)
    return pl.pallas_call(
        place_kernel,
        out_shape=(jax.ShapeDtypeStruct((SLABS, ROWS, LANES), F32), strip, strip),
        in_specs=[VMEM] * 4,
        out_specs=(VMEM,) * 3,
        scratch_shapes=[
            pltpu.VMEM((SLABS, 640, LANES), F32),
            pltpu.VMEM((8, LANES), jnp.int32),
            pltpu.SMEM((8, LANES), jnp.int32),
            pltpu.SemaphoreType.DMA(()),
        ],
        compiler_params=params(24),
        name="place",
    )(payload, head, side, picks)


def rim_kernel(rate_ref, code_ref, slot_ref, head_ref, top_ref, bottom_ref, cols_ref):
    def four(rows, columns):
        code = code_ref[rows, columns].astype(F32)
        lake = (slot_ref[rows, columns] < LLOC).astype(F32)
        return rate_ref[rows, columns], code, lake, head_ref[rows, columns]

    for n, (first, last) in enumerate(zip(four(slice(0, 8), slice(None)), four(slice(632, 640), slice(None)))):
        top_ref[2 * n : 2 * n + 2, :] = first[0:2]
        bottom_ref[2 * n : 2 * n + 2, :] = last[6:8]
    lane = lanes_of((640, LANES))
    gathered = jnp.zeros((640, LANES), F32)
    for n, first in enumerate(four(slice(None), slice(0, LANES))):
        value = pltpu.roll(first, 2 * n, 1) if n else first
        gathered = jnp.where((lane >> 1) == n, value, gathered)
    for n, last in enumerate(four(slice(None), slice(640 - LANES, 640))):
        value = pltpu.roll(last, 2 * n + 10, 1)
        gathered = jnp.where((lane >> 1) == n + 4, value, gathered)
    cols_ref[...] = gathered.T[0:16, :]


def static_kernel(edge_ref, rate_ref, code_ref, slot_ref, up_ref, down_ref, left_ref, right_ref, rates_ref, codes_ref, side_ref, ranges_ref, turn_ref, bits_ref):
    def signed(rate, lake):
        return jnp.where(lake, -rate, rate)

    def center(g, carry):
        rows = pl.ds(pl.multiple_of(g * 8, 8), 8)
        into = pl.ds(pl.multiple_of(g * 8 + FIRST, 8), 8)
        low = jnp.zeros((8, LANES), jnp.int32)
        high = jnp.zeros((8, LANES), jnp.int32)
        for c in range(SLABS - 1):
            columns = slice(c * LANES, (c + 1) * LANES)
            slot = slot_ref[rows, columns]
            rates_ref[c, into, :] = signed(rate_ref[rows, columns], slot < LLOC)
            codes_ref[c, into, :] = code_ref[rows, columns]
            bit = jnp.left_shift(1, slot & 31)
            low = low | jnp.where(slot < 32, bit, 0)
            high = high | jnp.where((slot >= 32) & (slot < LLOC), bit, 0)
        for shift in (4, 2, 1):
            low = low | pltpu.roll(low, shift, 0)
            high = high | pltpu.roll(high, shift, 0)
        bits_ref[0, pl.ds(g, 1), :] = low[0:1]
        bits_ref[1, pl.ds(g, 1), :] = high[0:1]
        return carry

    lax.fori_loop(0, 80, center, 0)
    low, high = bits_ref[0], bits_ref[1]
    for shift in (64, 32, 16, 8, 4, 2, 1):
        low = low | pltpu.roll(low, shift, 1)
        high = high | pltpu.roll(high, shift, 1)
    shape = (80, LANES)
    lane = lanes_of(shape)
    found = (jnp.right_shift(jnp.where(lane < 32, low, high), lane & 31) & 1) == 1
    group = rows_of(shape)
    ranges_ref[...] = jnp.zeros((8, LANES), jnp.int32)
    ranges_ref[0:1, :] = jnp.min(jnp.where(found, group, 80), axis=0, keepdims=True)
    ranges_ref[1:2, :] = jnp.max(jnp.where(found, group + 1, 0), axis=0, keepdims=True)

    first_row, last_row, first_col, last_col = (edge_ref[n] == 1 for n in range(4))
    eight = (8, LANES)
    for c in range(SLABS - 1):
        columns = slice(c * LANES, (c + 1) * LANES)
        for ref, base, offset, outside in ((up_ref, 8, 6, first_row), (down_ref, FIRST + 640, 0, last_row)):
            four = ref[:, columns]
            rates_ref[c, base : base + 8, :] = jnp.zeros(eight, F32)
            codes_ref[c, base : base + 8, :] = jnp.full(eight, -1, jnp.int32)
            at = slice(base + offset, base + offset + 2)
            rates_ref[c, at, :] = signed(four[0:2], four[4:6] > 0.5)
            codes_ref[c, at, :] = jnp.where(outside, -1, four[2:4].astype(jnp.int32))

    turn_ref[...] = jnp.zeros(turn_ref.shape, F32)
    turn_ref[0:8, :] = right_ref[...]
    turn_ref[8:16, :] = left_ref[...]
    turned = turn_ref[...].T[0:656, :]
    lane = lanes_of((656, LANES))
    row = rows_of((656, LANES))
    rightmost = lane < 2
    leftmost = lane >= 126

    def slab(n):
        right = pltpu.roll(turned, LANES - 2 * n, 1) if n else turned
        left = pltpu.roll(turned, 118 - 2 * n, 1)
        return jnp.where(rightmost, right, jnp.where(leftmost, left, 0.0))

    beyond = ((row < 8) & first_row) | ((row >= 648) & last_row) | (leftmost & first_col) | (rightmost & last_col)
    inside = (rightmost | leftmost) & (row >= 6) & (row < 650) & jnp.logical_not(beyond)
    rates_ref[SLABS - 1, 8:664, :] = signed(slab(0), slab(2) > 0.5)
    codes_ref[SLABS - 1, 8:664, :] = jnp.where(inside, slab(1).astype(jnp.int32), -1)
    side_ref[...] = slab(3)


def ring(axis, step):
    count = lax.axis_size(axis)
    return [(i, (i + step) % count) for i in range(count)]


def statics(rate, flow_code, lake_slot, head):
    strip = jax.ShapeDtypeStruct((8, 640), F32)
    top, bottom, cols = pl.pallas_call(
        rim_kernel,
        out_shape=(strip, strip, jax.ShapeDtypeStruct((16, 640), F32)),
        in_specs=[VMEM] * 4,
        out_specs=(VMEM,) * 3,
        compiler_params=params(16),
        name="rim",
    )(rate, flow_code, lake_slot, head)
    up = lax.ppermute(bottom, "row", ring("row", 1))
    down = lax.ppermute(top, "row", ring("row", -1))

    def corner(strips, columns):
        return strips[:, columns].reshape(4, 2, 2).transpose(0, 2, 1).reshape(8, 2)

    def tall(own, columns):
        pad = jnp.zeros((8, 6), F32)
        rest = jnp.zeros((8, 768 - 650), F32)
        return jnp.concatenate([pad, corner(up, columns), own, corner(down, columns), rest], axis=1)

    left = lax.ppermute(tall(cols[8:16], slice(638, 640)), "col", ring("col", 1))
    right = lax.ppermute(tall(cols[0:8], slice(0, 2)), "col", ring("col", -1))
    at_row, at_col = lax.axis_index("row"), lax.axis_index("col")
    edges = jnp.stack(
        [at_row == 0, at_row == lax.axis_size("row") - 1, at_col == 0, at_col == lax.axis_size("col") - 1]
    ).astype(jnp.int32)
    slabs = (SLABS, ROWS, LANES)
    return pl.pallas_call(
        static_kernel,
        out_shape=(
            jax.ShapeDtypeStruct(slabs, F32),
            jax.ShapeDtypeStruct(slabs, jnp.int32),
            jax.ShapeDtypeStruct((656, LANES), F32),
            jax.ShapeDtypeStruct((8, LANES), jnp.int32),
        ),
        in_specs=[SMEM] + [VMEM] * 7,
        out_specs=(VMEM,) * 4,
        scratch_shapes=[pltpu.VMEM((LANES, 768), F32), pltpu.VMEM((2, 80, LANES), jnp.int32)],
        compiler_params=params(20),
        name="static",
    )(edges, rate, flow_code, lake_slot, up, down, left, right)


def leave(depth, rate):
    conveyance = rate * jnp.exp(jnp.log(depth) * (2.0 / 3.0))
    return depth * conveyance / (1.0 + conveyance)


def route_kernel(
    ranges, depth_ref, up_ref, down_ref, rates_ref, codes_ref, slot_ref, wide_table_ref, tall_table_ref,
    surface_ref, spread_ref, leave_ref, next_ref, stay_ref, lake_ref, sums_ref,
):
    lane = lanes_of((8, LANES))

    def at(g):
        return pl.ds(pl.multiple_of(g * 8, 8), 8)

    def start(c, rows, depth):
        leaving = leave(depth, jnp.abs(rates_ref[c, rows, :]))
        leave_ref[c, rows, :] = leaving
        stay_ref[c, rows, :] = depth - leaving

    for g, ref in ((1, up_ref), (82, down_ref)):
        rows = slice(g * 8, g * 8 + 8)
        for c in range(SLABS - 1):
            start(c, rows, ref[:, c * LANES : (c + 1) * LANES])
        start(SLABS - 1, rows, depth_ref[SLABS - 1, rows, :])

    def first(g, carry):
        rows = at(g)
        for c in range(SLABS):
            start(c, rows, depth_ref[c, rows, :])
        return carry

    lax.fori_loop(2, 82, first, 0)

    def gained(ref, g, slabs):
        east, middle, west = [], [], []
        base = g * 8
        for c in range(SLABS):
            here, above, below = (ref[c, pl.ds(base + d, 8), :] for d in (0, -1, 1))
            code, code_above, code_below = (codes_ref[c, pl.ds(base + d, 8), :] for d in (0, -1, 1))

            def pick(which, number, value):
                return jnp.where(which == number, value, 0.0)

            east.append(pick(code, 0, here) + pick(code_above, 1, above) + pick(code_below, 7, below))
            middle.append(pick(code_above, 2, above) + pick(code_below, 6, below))
            west.append(pick(code, 4, here) + pick(code_above, 3, above) + pick(code_below, 5, below))
        east = [pltpu.roll(value, 1, 1) for value in east]
        west = [pltpu.roll(value, LANES - 1, 1) for value in west]
        return [
            middle[c]
            + jnp.where(lane == 0, east[c - 1], east[c])
            + jnp.where(lane == LANES - 1, west[(c + 1) % SLABS], west[c])
            for c in range(slabs)
        ]

    def second(g, carry):
        rows = at(g)
        for c, gain in enumerate(gained(leave_ref, g, SLABS)):
            rate = rates_ref[c, rows, :]
            lake = rate < 0.0
            depth = stay_ref[c, rows, :] + gain
            kept = jnp.where(lake, 0.0, depth)
            leaving = leave(kept, jnp.abs(rate))
            next_ref[c, rows, :] = leaving
            stay_ref[c, rows, :] = kept - leaving
            if c < SLABS - 1:
                lake_ref[c, rows, :] = depth - kept
        return carry

    lax.fori_loop(1, 83, second, 0)

    def third(g, carry):
        rows = at(g)
        out = at(g - 2)
        for c, gain in enumerate(gained(next_ref, g, SLABS - 1)):
            depth = stay_ref[c, rows, :] + gain
            kept = jnp.where(rates_ref[c, rows, :] < 0.0, 0.0, depth)
            lake_ref[c, rows, :] += depth - kept
            surface_ref[out, c * LANES : (c + 1) * LANES] = kept
        return carry

    lax.fori_loop(2, 82, third, 0)

    def lake(slot, carry):
        def add(g, total):
            rows = at(g)
            from_rows = at(g + 2)
            for c in range(SLABS - 1):
                mine = slot_ref[rows, c * LANES : (c + 1) * LANES] == slot
                total = total + jnp.where(mine, lake_ref[c, from_rows, :], 0.0)
            return total

        total = lax.fori_loop(ranges[0, slot], ranges[1, slot], add, jnp.zeros((8, LANES), F32))
        sums_ref[pl.ds(slot, 1), :] = jnp.sum(total, axis=0, keepdims=True)
        return carry

    lax.fori_loop(0, LLOC, lake, 0)
    totals = jnp.sum(sums_ref[...], axis=1, keepdims=True)
    owner = (wide_table_ref[...] >> 6 == rows_of((LANES, LLOC))).astype(F32).astype(BF16)
    number = (tall_table_ref[...] & 63) == lanes_of((LLOC, LANES))
    spread_ref[...] = select_dot(owner, jnp.where(number, totals, 0.0))


def route(depth, up, down, rates, codes, ranges, lake_slot, lake_table):
    slabs = pltpu.VMEM((SLABS, ROWS, LANES), F32)
    return pl.pallas_call(
        route_kernel,
        out_shape=(jax.ShapeDtypeStruct(lake_slot.shape, F32), jax.ShapeDtypeStruct((LANES, LANES), F32)),
        in_specs=[SMEM] + [VMEM] * 8,
        out_specs=(VMEM,) * 2,
        scratch_shapes=[slabs, slabs, slabs, slabs, pltpu.VMEM((LLOC, LANES), F32)],
        compiler_params=params(28),
        name="route",
    )(ranges, depth, up, down, rates, codes, lake_slot, lake_table.reshape(1, LLOC), lake_table.reshape(LLOC, 1))


def pool_kernel(spread_ref, phase_ref, area_ref, crest_ref, level_ref, outflow_ref):
    inflow = jnp.sum(spread_ref[...], axis=0, keepdims=True)[:, :LLOC]
    area = area_ref[...]
    phase = phase_ref[...] + inflow / area
    excess = jnp.maximum(phase - crest_ref[...], 0.0)
    outflow = excess * jnp.sqrt(excess)
    level_ref[...] = phase - outflow / area
    outflow_ref[...] = outflow


def level_pool(spread, lake_phase, lake_area, lake_crest):
    row = jax.ShapeDtypeStruct((1, LLOC), F32)
    level, outflow = pl.pallas_call(
        pool_kernel,
        out_shape=(row, row),
        in_specs=[VMEM] * 4,
        out_specs=(VMEM,) * 2,
        name="pool",
    )(spread, *(value.reshape(1, LLOC) for value in (lake_phase, lake_area, lake_crest)))
    return level.reshape(LLOC), outflow.reshape(LLOC)


def new_moisture_of(moisture, conduct, rainfall):
    saturation = moisture / POROSITY
    capacity = 10.0 * conduct[0] * (1.5 - saturation[0])
    infiltration = rainfall * capacity / (rainfall + capacity)
    drainage = conduct * saturation**4
    incoming = jnp.concatenate([infiltration[None, :], drainage[:-1]], axis=0)
    thickness = jnp.array(LAYER_DEPTHS, F32)[:, None]
    return moisture + TIME_STEP * (incoming - drainage) / thickness


def body(
    moisture, conduct, rainfall, weights, land_tile, head, rate, flow_code, lake_slot, lake_table,
    lake_phase, lake_area, lake_crest,
):
    both = ("row", "col")
    payload = land_payload(land_tile, moisture, conduct, rainfall, weights)
    payload, rate, flow_code, lake_slot, head, moisture = lax.optimization_barrier(
        (payload, rate, flow_code, lake_slot, head, moisture)
    )
    arrived = lax.all_to_all(
        payload.reshape(RUNS, 1, RUN_ROWS * LANES), both, split_axis=0, concat_axis=0, tiled=True
    ).reshape(RUNS * RUN_ROWS, LANES)
    new_moisture = new_moisture_of(moisture, conduct, rainfall)
    rates, codes, side, ranges = statics(rate, flow_code, lake_slot, head)
    depth, top, bottom = place(arrived, head, side)
    up = lax.ppermute(bottom, "row", ring("row", 1))
    down = lax.ppermute(top, "row", ring("row", -1))
    surface, spread = route(depth, up, down, rates, codes, ranges, lake_slot, lake_table)
    spread = lax.all_to_all(
        spread.reshape(RUNS, 1, LANES), both, split_axis=0, concat_axis=0, tiled=True
    ).reshape(RUNS, LANES)
    level, outflow = level_pool(spread, lake_phase, lake_area, lake_crest)
    return (new_moisture, surface, level, outflow)


def solution(mesh):
    blocks = P(("row", "col"))
    layers = P(None, ("row", "col"))
    cells = P("row", "col")
    in_specs = (layers, layers, blocks, layers, blocks) + (cells,) * 4 + (blocks,) * 4
    out_specs = (layers, cells, blocks, blocks)
    return jax.shard_map(body, mesh=mesh, in_specs=in_specs, out_specs=out_specs, check_vma=False)
```

```python
import jax
import jax.numpy as jnp
import numpy as np
from jax import lax
from jax.experimental import pallas as pl
from jax.experimental.pallas import tpu as pltpu
from jax.sharding import PartitionSpec as P

AGG = 10
LLOC = 64
LANES = 128
RUNS = 128
RUN_ROWS = 26
SLABS = 6
ROWS = 672
FIRST = 16

LAYER_DEPTHS = (0.1, 0.3, 0.6, 1.0)
POROSITY = 0.45
TIME_STEP = 0.05
F32 = jnp.float32
BF16 = jnp.bfloat16
VMEM = pl.BlockSpec(memory_space=pltpu.VMEM)
HBM = pl.BlockSpec(memory_space=pltpu.HBM)
SMEM = pl.BlockSpec(memory_space=pltpu.SMEM)


def params(mebibytes=60):
    return pltpu.CompilerParams(vmem_limit_bytes=mebibytes * 1024 * 1024)


def lanes_of(shape):
    return lax.broadcasted_iota(jnp.int32, shape, len(shape) - 1)


def rows_of(shape):
    return lax.broadcasted_iota(jnp.int32, shape, 0)


def split3(value):
    high = value.astype(BF16)
    rest = value - high.astype(F32)
    middle = rest.astype(BF16)
    low = (rest - middle.astype(F32)).astype(BF16)
    return high, middle, low


def select_dot(picks, value):
    return sum(jnp.dot(picks, part, preferred_element_type=F32) for part in split3(value))


def signed(rate, lake):
    return jnp.where(lake, -rate, rate)


def ring(axis, step):
    count = lax.axis_size(axis)
    return [(i, (i + step) % count) for i in range(count)]


def dot_select(value, picks):
    return sum(jnp.dot(part, picks, preferred_element_type=F32) for part in split3(value))


def quarter_transpose(arrays, quarter):
    rolled = []
    for d in range(4):
        skew = arrays[(3 + d) % 4]
        for m in range(3):
            skew = jnp.where(quarter == m, arrays[(m + d) % 4], skew)
        rolled.append(pltpu.roll(skew, 32 * d, 1) if d else skew)
    outs = []
    for r in range(4):
        out = rolled[(3 - r) % 4]
        for m in range(3):
            out = jnp.where(quarter == m, rolled[(m - r) % 4], out)
        outs.append(out)
    return outs


def send_kernel(
    tile_hbm, moisture_hbm, conduct_hbm, rain_hbm, weights_hbm, out_ref,
    tile_ref, moisture_ref, conduct_ref, rain_ref, slab_ref, edge_ref, sems,
):
    count = slab_ref.shape[0]

    def fetch(i):
        start = pl.multiple_of(i * LANES, LANES)
        return pltpu.make_async_copy(weights_hbm.at[:, pl.ds(start, LANES)], slab_ref.at[i], sems.at[i])

    small = [
        pltpu.make_async_copy(source, into, sems.at[count + n])
        for n, (source, into) in enumerate(
            ((tile_hbm, tile_ref), (moisture_hbm, moisture_ref), (conduct_hbm, conduct_ref), (rain_hbm, rain_ref))
        )
    ]
    for copy in small:
        copy.start()

    def begin(i, carry):
        fetch(i).start()
        return carry

    lax.fori_loop(0, count, begin, 0, unroll=4)
    for copy in small:
        copy.wait()
    lane = lanes_of((1, LANES))
    quarter = lane >> 5

    def step(i, carry):
        edges, tiles = carry
        start = pl.multiple_of(i * LANES, LANES)
        conduct = conduct_ref[0:1, pl.ds(start, LANES)]
        moisture = moisture_ref[0:1, pl.ds(start, LANES)]
        rain = rain_ref[0:1, pl.ds(start, LANES)]
        capacity = 10.0 * conduct * (1.5 - moisture / POROSITY)
        runoff = rain - rain * capacity / (rain + capacity)
        fetch(i).wait()
        parts = [slab_ref[i, pl.ds(b, AGG, stride=AGG), :] for b in range(AGG)]
        total = sum(parts[1:], parts[0])
        mean = jnp.sum(total, axis=0, keepdims=True) * 0.01
        scale = runoff / mean
        parts = [part * scale for part in parts]
        tail = [slab_ref[i, pl.ds(first, 5, stride=AGG), :] * scale for first in (8, 9, 58, 59)]
        groups = (
            (0, AGG, quarter_transpose(parts[0:4], quarter)),
            (AGG, AGG, quarter_transpose(parts[4:8], quarter)),
            (2 * AGG, 5, quarter_transpose(tail, quarter)),
        )
        for r in range(4):
            tile = tile_ref[(4 * i + r) * 32]
            tiles = jnp.where(lane == 32 * r + i, tile, tiles)
            for offset, length, outs in groups:
                out_ref[pl.ds(tile * RUN_ROWS + offset, length), :] = outs[r]
        place = lane & 63
        new_edges = []
        for b in range(2):
            left = pltpu.roll(parts[b], i, 1)
            right = pltpu.roll(parts[8 + b], i + 97, 1)
            edge = jnp.where(place == i, left, edges[b])
            new_edges.append(jnp.where(place == i + 32, right, edge))
        return tuple(new_edges), tiles

    zeros = jnp.zeros((AGG, LANES), F32)
    edges, tiles = lax.fori_loop(0, count, step, ((zeros, zeros), jnp.zeros((1, LANES), jnp.int32)))
    edge_ref[...] = jnp.zeros((LANES, LANES), F32)
    edge_ref[0:AGG, :] = edges[0]
    edge_ref[16 : 16 + AGG, :] = edges[1]
    edge_ref[15:16, :] = (4 * (lane & 31) + (lane >> 5)).astype(F32)
    by_run = edge_ref[...].T
    square = (LANES, LANES)
    here = (rows_of(square) == tiles).astype(F32).astype(BF16)
    by_tile = select_dot(here, by_run)
    run = by_tile[:, 15:16].astype(jnp.int32)
    wide = lanes_of(square)
    odd = (run & 1) == 1
    no_edge = jnp.where(wide == 15, -1.0, 0.0)
    row = pltpu.roll(jnp.where(odd, by_tile, no_edge), 1, 0)
    row = row + pltpu.roll(pltpu.roll(jnp.where(odd, no_edge, by_tile), LANES - 1, 0), 32, 1)
    row = row + jnp.where(wide == 127, run.astype(F32), 0.0)
    out_ref[pl.ds(25, RUNS, stride=RUN_ROWS), :] = row


def land_payload(land_tile, moisture, conduct, rainfall, weights):
    blocks = weights.shape[1]
    count = blocks // LANES
    return pl.pallas_call(
        send_kernel,
        out_shape=jax.ShapeDtypeStruct((RUNS * RUN_ROWS, LANES), F32),
        in_specs=[HBM] * 5,
        out_specs=VMEM,
        scratch_shapes=[
            pltpu.SMEM((blocks,), jnp.int32),
            pltpu.VMEM(moisture.shape, F32),
            pltpu.VMEM(conduct.shape, F32),
            pltpu.VMEM((1, blocks), F32),
            pltpu.VMEM((count, AGG * AGG, LANES), F32),
            pltpu.VMEM((LANES, LANES), F32),
            pltpu.SemaphoreType.DMA((count + 4,)),
        ],
        compiler_params=params(),
        name="land",
    )(land_tile, moisture, conduct, rainfall.reshape(1, blocks), weights)


def spread_columns():
    picks = np.zeros((SLABS * LANES, 640), np.float32)
    for half in range(2):
        for j in range(3):
            for k in range(4 if j < 2 else 2):
                for i in range(32):
                    picks[(half * 3 + j) * LANES + 32 * k + i, (half * 32 + i) * AGG + 4 * j + k] = 1.0
    return picks


def place_kernel(
    edge_ref, left_ref, right_ref, top_in, bottom_in, pay_hbm, head_hbm, picks_hbm,
    depth_hbm, rate_hbm, code_hbm, top_ref, bottom_ref,
    pay_ref, head_ref, picks_ref, depth_ref, rate_ref, code_ref, turn_ref, cells_ref, tag_ref, tags, sems,
):
    fetches = [
        pltpu.make_async_copy(source, into, sems.at[n])
        for n, (source, into) in enumerate(((pay_hbm, pay_ref), (picks_hbm, picks_ref), (head_hbm, head_ref)))
    ]
    for copy in fetches:
        copy.start()
    top_ref[...] = top_in[...]
    bottom_ref[...] = bottom_in[...]
    turn_ref[...] = jnp.zeros(turn_ref.shape, F32)
    turn_ref[0:8, :] = right_ref[...]
    turn_ref[8:16, :] = left_ref[...]
    turned = turn_ref[...].T
    tall = (640, LANES)
    lane = lanes_of(tall)
    rightmost = lane < 2
    leftmost = lane >= 126

    def slab(n):
        right = pltpu.roll(turned, LANES - 2 * n, 1) if n else turned
        left = pltpu.roll(turned, 118 - 2 * n, 1)
        return jnp.where(rightmost, right, jnp.where(leftmost, left, 0.0))

    first_col, last_col = edge_ref[2] == 1, edge_ref[3] == 1
    inside = (rightmost & jnp.logical_not(last_col)) | (leftmost & jnp.logical_not(first_col))
    side_rate = slab(0)
    side_code = jnp.where(inside, slab(1), -1.0)
    side_lake = slab(2)
    side_head = slab(3)
    rate_ref[...] = signed(side_rate, side_lake > 0.5)
    code_ref[...] = side_code.astype(jnp.int32)
    stores = [
        pltpu.make_async_copy(source, into, sems.at[n + 3])
        for n, (source, into) in enumerate(((rate_ref, rate_hbm), (code_ref, code_hbm)))
    ]
    for copy in stores:
        copy.start()
    for ref, rows in ((top_ref, slice(0, 2)), (bottom_ref, slice(638, 640))):
        ref[2:4, 640:768] = side_rate[rows]
        ref[4:6, 640:768] = side_code[rows]
        ref[6:8, 640:768] = side_lake[rows]

    fetches[0].wait()
    arrived = pay_ref[pl.ds(25, RUNS, stride=RUN_ROWS), :]
    by_lane = arrived.T
    tag_ref[...] = jnp.broadcast_to(by_lane[127:128, :].astype(jnp.int32), (8, LANES))
    copy = pltpu.make_async_copy(tag_ref, tags, sems.at[5])
    copy.start()
    row = rows_of(tall)
    block = (row * 6554) >> 16
    left = (by_lane[15:16, :].astype(jnp.int32) == 2 * block + 1).astype(F32).astype(BF16)
    right = (by_lane[47:48, :].astype(jnp.int32) == 2 * block).astype(F32).astype(BF16)
    square = (LANES, LANES)
    wide = lanes_of(square)
    strips = select_dot(left, jnp.where(wide < 32, arrived, 0.0))
    strips = strips + select_dot(right, jnp.where((wide >= 32) & (wide < 64), arrived, 0.0))
    strips = jnp.where((lane & 15) == row - AGG * block, strips, 0.0)
    source = rows_of(square)
    group = source >> 4
    target = jnp.where(group < 2, 126, 0) + (group & 1)
    fold = (((source & 15) < AGG) & (group < 4) & (target == wide)).astype(F32).astype(BF16)
    depth = dot_select(strips, fold) + side_head
    depth_ref[SLABS - 1, FIRST : FIRST + 640, :] = depth
    top_ref[0:2, 640:768] = depth[0:2]
    bottom_ref[0:2, 640:768] = depth[638:640]
    copy.wait()

    def settle(s, carry):
        run = tags[0, s]
        slab = (run & 1) * 3
        row = (run >> 1) * AGG
        start = s * RUN_ROWS
        cells_ref[slab, pl.ds(row, AGG), :] = pay_ref[pl.ds(start, AGG), :]
        cells_ref[slab + 1, pl.ds(row, AGG), :] = pay_ref[pl.ds(start + AGG, AGG), :]
        last = pay_ref[pl.ds(start + 2 * AGG, 5), :]
        cells_ref[slab + 2, pl.ds(row, 5), :] = last
        cells_ref[slab + 2, pl.ds(row + 5, 5), :] = pltpu.roll(last, 64, 1)
        return carry

    lax.fori_loop(0, RUNS, settle, 0, unroll=16)
    for copy in fetches[1:]:
        copy.wait()
    picks = picks_ref[...]
    chunk = 160
    for m in range(0, 640, chunk):
        cells = jnp.concatenate([cells_ref[c, m : m + chunk, :] for c in range(SLABS)], axis=1)
        laid = dot_select(cells, picks)
        for c in range(SLABS - 1):
            columns = slice(c * LANES, (c + 1) * LANES)
            depth = laid[:, columns] + head_ref[m : m + chunk, columns]
            depth_ref[c, FIRST + m : FIRST + m + chunk, :] = depth
            if m == 0:
                top_ref[0:2, columns] = depth[0:2]
            if m == 640 - chunk:
                bottom_ref[0:2, columns] = depth[chunk - 2 :]
        rows = pl.ds(FIRST + m, chunk)
        store = pltpu.make_async_copy(depth_ref.at[:, rows, :], depth_hbm.at[:, rows, :], sems.at[6 + m // chunk])
        store.start()
        stores.append(store)
    for store in stores:
        store.wait()


def place(edges, left, right, top, bottom, payload, head):
    picks = jnp.asarray(spread_columns(), BF16)
    strip = jax.ShapeDtypeStruct((8, 768), F32)
    slabs = (SLABS, ROWS, LANES)
    side = (640, LANES)
    return pl.pallas_call(
        place_kernel,
        out_shape=(
            jax.ShapeDtypeStruct(slabs, F32),
            jax.ShapeDtypeStruct(side, F32),
            jax.ShapeDtypeStruct(side, jnp.int32),
            strip,
            strip,
        ),
        in_specs=[SMEM] + [VMEM] * 4 + [HBM] * 3,
        out_specs=(HBM, HBM, HBM, VMEM, VMEM),
        scratch_shapes=[
            pltpu.VMEM(payload.shape, F32),
            pltpu.VMEM(head.shape, F32),
            pltpu.VMEM(picks.shape, BF16),
            pltpu.VMEM(slabs, F32),
            pltpu.VMEM(side, F32),
            pltpu.VMEM(side, jnp.int32),
            pltpu.VMEM((LANES, 640), F32),
            pltpu.VMEM((SLABS, 640, LANES), F32),
            pltpu.VMEM((8, LANES), jnp.int32),
            pltpu.SMEM((8, LANES), jnp.int32),
            pltpu.SemaphoreType.DMA((10,)),
        ],
        compiler_params=params(),
        name="place",
    )(edges, left, right, top, bottom, payload, head, picks)


def rim_kernel(
    moisture_ref, conduct_ref, rain_ref, rate_hbm, code_hbm, slot_hbm, head_hbm, cols_ref, soil_ref,
    rate_ref, code_ref, slot_ref, head_ref, sems,
):
    fetches = []
    for n, (source, into) in enumerate(
        ((rate_hbm, rate_ref), (code_hbm, code_ref), (slot_hbm, slot_ref), (head_hbm, head_ref))
    ):
        for side in range(2):
            columns = pl.ds(side * 512, LANES)
            fetches.append(pltpu.make_async_copy(source.at[:, columns], into.at[side], sems.at[2 * n + side]))
    for copy in fetches:
        copy.start()
    for copy in fetches:
        copy.wait()

    def four(side):
        code = code_ref[side].astype(F32)
        lake = (slot_ref[side] < LLOC).astype(F32)
        return rate_ref[side], code, lake, head_ref[side]

    lane = lanes_of((640, LANES))
    gathered = jnp.zeros((640, LANES), F32)
    for n, first in enumerate(four(0)):
        value = pltpu.roll(first, 2 * n, 1) if n else first
        gathered = jnp.where((lane >> 1) == n, value, gathered)
    for n, last in enumerate(four(1)):
        value = pltpu.roll(last, 2 * n + 10, 1)
        gathered = jnp.where((lane >> 1) == n + 4, value, gathered)
    cols_ref[...] = gathered.T[0:16, :]

    rain = rain_ref[...]
    saturation = moisture_ref[...] / POROSITY
    squared = saturation * saturation
    drainage = conduct_ref[...] * (squared * squared)
    capacity = 10.0 * conduct_ref[0:1, :] * (1.5 - saturation[0:1])
    incoming = rain * capacity / (rain + capacity)
    for k, thickness in enumerate(LAYER_DEPTHS):
        leaving = drainage[k : k + 1]
        soil_ref[k : k + 1, :] = moisture_ref[k : k + 1, :] + TIME_STEP * (incoming - leaving) / thickness
        incoming = leaving


def rim(moisture, conduct, rainfall, rate, flow_code, lake_slot, head):
    pair = (2, 640, LANES)
    return pl.pallas_call(
        rim_kernel,
        out_shape=(jax.ShapeDtypeStruct((16, 640), F32), jax.ShapeDtypeStruct(moisture.shape, F32)),
        in_specs=[VMEM] * 3 + [HBM] * 4,
        out_specs=(VMEM,) * 2,
        scratch_shapes=[
            pltpu.VMEM(pair, F32),
            pltpu.VMEM(pair, jnp.int32),
            pltpu.VMEM(pair, jnp.int32),
            pltpu.VMEM(pair, F32),
            pltpu.SemaphoreType.DMA((8,)),
        ],
        compiler_params=params(),
        cost_estimate=pl.CostEstimate(flops=0, bytes_accessed=0, transcendentals=0),
        name="rim",
    )(moisture, conduct, rainfall.reshape(1, rainfall.shape[0]), rate, flow_code, lake_slot, head)


def static_kernel(
    rate_hbm, code_hbm, slot_hbm, rates_hbm, codes_hbm, ranges_ref, top_ref, bottom_ref,
    rate_ref, code_ref, slot_ref, rates_ref, codes_ref, bits_ref, sems,
):
    fetches = [
        pltpu.make_async_copy(source, into, sems.at[n])
        for n, (source, into) in enumerate(((rate_hbm, rate_ref), (code_hbm, code_ref), (slot_hbm, slot_ref)))
    ]
    for copy in fetches:
        copy.start()
    for copy in fetches:
        copy.wait()
    for ref, base, part in ((top_ref, 0, slice(0, 2)), (bottom_ref, 632, slice(6, 8))):
        rows = slice(base, base + 8)
        ref[...] = jnp.zeros((8, 768), F32)
        ref[2:4, 0:640] = rate_ref[rows, :][part]
        ref[4:6, 0:640] = code_ref[rows, :][part].astype(F32)
        ref[6:8, 0:640] = (slot_ref[rows, :][part] < LLOC).astype(F32)

    def center(g, carry):
        rows = pl.ds(pl.multiple_of(g * 8, 8), 8)
        into = pl.ds(pl.multiple_of(g * 8 + FIRST, 8), 8)
        low = jnp.zeros((8, LANES), jnp.int32)
        high = jnp.zeros((8, LANES), jnp.int32)
        for c in range(SLABS - 1):
            columns = slice(c * LANES, (c + 1) * LANES)
            slot = slot_ref[rows, columns]
            rates_ref[c, into, :] = signed(rate_ref[rows, columns], slot < LLOC)
            codes_ref[c, into, :] = code_ref[rows, columns]
            bit = jnp.left_shift(1, slot & 31)
            low = low | jnp.where(slot < 32, bit, 0)
            high = high | jnp.where((slot >= 32) & (slot < LLOC), bit, 0)
        for shift in (4, 2, 1):
            low = low | pltpu.roll(low, shift, 0)
            high = high | pltpu.roll(high, shift, 0)
        bits_ref[0, pl.ds(g, 1), :] = low[0:1]
        bits_ref[1, pl.ds(g, 1), :] = high[0:1]
        return carry

    lax.fori_loop(0, 80, center, 0, unroll=8)
    stores = [
        pltpu.make_async_copy(source, into, sems.at[3 + n])
        for n, (source, into) in enumerate(((rates_ref, rates_hbm), (codes_ref, codes_hbm)))
    ]
    for copy in stores:
        copy.start()
    low, high = bits_ref[0], bits_ref[1]
    for shift in (64, 32, 16, 8, 4, 2, 1):
        low = low | pltpu.roll(low, shift, 1)
        high = high | pltpu.roll(high, shift, 1)
    shape = (80, LANES)
    lane = lanes_of(shape)
    found = (jnp.right_shift(jnp.where(lane < 32, low, high), lane & 31) & 1) == 1
    group = rows_of(shape)
    begin = jnp.min(jnp.where(found, group, 80), axis=0, keepdims=True)
    end = jnp.max(jnp.where(found, group + 1, 0), axis=0, keepdims=True)
    longest = jnp.max(jnp.where(lane[0:1] < LLOC, end - begin, 0), axis=1, keepdims=True)
    ranges_ref[...] = jnp.zeros((8, LANES), jnp.int32)
    ranges_ref[0:1, :] = begin
    ranges_ref[1:2, :] = end
    ranges_ref[2:3, :] = jnp.broadcast_to(longest, (1, LANES))
    for copy in stores:
        copy.wait()


def statics(rate, flow_code, lake_slot):
    slabs = (SLABS - 1, ROWS, LANES)
    strip = jax.ShapeDtypeStruct((8, 768), F32)
    return pl.pallas_call(
        static_kernel,
        out_shape=(
            jax.ShapeDtypeStruct(slabs, F32),
            jax.ShapeDtypeStruct(slabs, jnp.int32),
            jax.ShapeDtypeStruct((8, LANES), jnp.int32),
            strip,
            strip,
        ),
        in_specs=[HBM, HBM, HBM],
        out_specs=(HBM, HBM, VMEM, VMEM, VMEM),
        scratch_shapes=[
            pltpu.VMEM(rate.shape, F32),
            pltpu.VMEM(rate.shape, jnp.int32),
            pltpu.VMEM(rate.shape, jnp.int32),
            pltpu.VMEM(slabs, F32),
            pltpu.VMEM(slabs, jnp.int32),
            pltpu.VMEM((2, 80, LANES), jnp.int32),
            pltpu.SemaphoreType.DMA((5,)),
        ],
        compiler_params=params(),
        cost_estimate=pl.CostEstimate(flops=0, bytes_accessed=0, transcendentals=0),
        name="static",
    )(rate, flow_code, lake_slot)


def leave(depth, rate):
    conveyance = rate * jnp.exp(jnp.log(depth) * (2.0 / 3.0))
    return depth * conveyance / (1.0 + conveyance)


def route_kernel(
    edge_ref, ranges, up_ref, down_ref, table_ref, depth_hbm, rates_hbm, codes_hbm, rate_hbm, code_hbm, slot_hbm,
    surface_hbm, spread_ref,
    depth_ref, rates_ref, codes_ref, slot_ref, surface_ref, leave_ref, next_ref, lake_ref, sums_ref, sems,
):
    quarters = [(0, 176), (176, 160), (336, 160), (496, 176)]

    def rows_in(source, into, n, q):
        rows = pl.ds(*quarters[q])
        return pltpu.make_async_copy(source.at[:, rows, :], into.at[:, rows, :], sems.at[4 * n + q])

    depths = [rows_in(depth_hbm, depth_ref, 0, q) for q in range(4)]
    middle, side, rows = pl.ds(0, SLABS - 1), SLABS - 1, pl.ds(FIRST, 640)
    rates = [rows_in(rates_hbm, rates_ref.at[middle], 1, q) for q in range(4)]
    side_rate = pltpu.make_async_copy(rate_hbm, rates_ref.at[side, rows, :], sems.at[15])
    codes = pltpu.make_async_copy(codes_hbm, codes_ref.at[middle], sems.at[8])
    side_code = pltpu.make_async_copy(code_hbm, codes_ref.at[side, rows, :], sems.at[16])
    slots = pltpu.make_async_copy(slot_hbm, slot_ref, sems.at[9])
    side_rate.start()
    for q in range(4):
        depths[q].start()
        rates[q].start()
    codes.start()
    side_code.start()
    slots.start()
    lane = lanes_of((8, LANES))

    def at(g):
        return pl.ds(pl.multiple_of(g * 8, 8), 8)

    def start(c, rows):
        depth = depth_ref[c, rows, :]
        leaving = leave(depth, jnp.abs(rates_ref[c, rows, :]))
        leave_ref[c, rows, :] = leaving
        depth_ref[c, rows, :] = depth - leaving

    eight = (8, LANES)
    rims = ((1, up_ref, 6, edge_ref[0] == 1), (82, down_ref, 0, edge_ref[1] == 1))

    def first(g, carry):
        rows = at(g)
        for c in range(SLABS):
            start(c, rows)
        return carry

    side_rate.wait()
    for q, (begin, end) in enumerate(((2, 22), (22, 42), (42, 62), (62, 82))):
        depths[q].wait()
        rates[q].wait()
        lax.fori_loop(begin, end, first, 0, unroll=2)
    codes.wait()
    side_code.wait()
    for g, ref, offset, outside in rims:
        rows = slice(g * 8, g * 8 + 8)
        two = slice(g * 8 + offset, g * 8 + offset + 2)
        for c in range(SLABS):
            four = ref[:, c * LANES : (c + 1) * LANES]
            depth_ref[c, rows, :] = jnp.zeros(eight, F32)
            rates_ref[c, rows, :] = jnp.ones(eight, F32)
            codes_ref[c, rows, :] = jnp.full(eight, -1, jnp.int32)
            depth_ref[c, two, :] = four[0:2]
            rates_ref[c, two, :] = jnp.where(four[6:8] > 0.5, -four[2:4], four[2:4])
            codes_ref[c, two, :] = jnp.where(outside, -1, four[4:6].astype(jnp.int32))
        first(g, 0)

    def gained(ref, g, slabs):
        east, middle, west = [], [], []
        base = g * 8
        for c in range(SLABS):
            here, above, below = (ref[c, pl.ds(base + d, 8), :] for d in (0, -1, 1))
            code, code_above, code_below = (codes_ref[c, pl.ds(base + d, 8), :] for d in (0, -1, 1))

            def pick(which, number, value):
                return jnp.where(which == number, value, 0.0)

            east.append(pick(code, 0, here) + pick(code_above, 1, above) + pick(code_below, 7, below))
            middle.append(pick(code_above, 2, above) + pick(code_below, 6, below))
            west.append(pick(code, 4, here) + pick(code_above, 3, above) + pick(code_below, 5, below))
        east = [pltpu.roll(value, 1, 1) for value in east]
        west = [pltpu.roll(value, LANES - 1, 1) for value in west]
        return [
            middle[c]
            + jnp.where(lane == 0, east[c - 1], east[c])
            + jnp.where(lane == LANES - 1, west[(c + 1) % SLABS], west[c])
            for c in range(slabs)
        ]

    def second(g, carry):
        rows = at(g)
        for c, gain in enumerate(gained(leave_ref, g, SLABS)):
            rate = rates_ref[c, rows, :]
            lake = rate < 0.0
            depth = depth_ref[c, rows, :] + gain
            kept = jnp.where(lake, 0.0, depth)
            leaving = leave(kept, jnp.abs(rate))
            next_ref[c, rows, :] = leaving
            depth_ref[c, rows, :] = kept - leaving
            if c < SLABS - 1:
                lake_ref[c, rows, :] = depth - kept
        return carry

    lax.fori_loop(1, 81, second, 0, unroll=16)
    for g in (81, 82):
        second(g, 0)

    def third(g, carry):
        rows = at(g)
        out = at(g - 2)
        for c, gain in enumerate(gained(next_ref, g, SLABS - 1)):
            depth = depth_ref[c, rows, :] + gain
            kept = jnp.where(rates_ref[c, rows, :] < 0.0, 0.0, depth)
            lake_ref[c, rows, :] += depth - kept
            surface_ref[out, c * LANES : (c + 1) * LANES] = kept
        return carry

    stores = []
    for q in range(5):
        lax.fori_loop(2 + 16 * q, 18 + 16 * q, third, 0, unroll=16)
        rows = pl.ds(128 * q, 128)
        store = pltpu.make_async_copy(surface_ref.at[rows, :], surface_hbm.at[rows, :], sems.at[10 + q])
        store.start()
        stores.append(store)
    slots.wait()
    sums_ref[...] = jnp.zeros(sums_ref.shape, F32)

    def layer(e, carry):
        def lake(slot, inner):
            g = ranges[0, slot] + e
            wanted = jnp.where(g < ranges[1, slot], slot, -1)
            g = jnp.minimum(g, 79)
            rows = at(g)
            from_rows = at(g + 2)
            into = pl.ds(pl.multiple_of(slot * 8, 8), 8)
            terms = []
            for c in range(SLABS - 1):
                mine = slot_ref[rows, c * LANES : (c + 1) * LANES] == wanted
                terms.append(jnp.where(mine, lake_ref[c, from_rows, :], 0.0))
            sums_ref[into, :] += (terms[0] + terms[1]) + (terms[2] + terms[3]) + terms[4]
            return inner

        return lax.fori_loop(0, LLOC, lake, carry, unroll=8)

    lax.fori_loop(0, ranges[2, 0], layer, 0)
    tall = (LLOC, 8 * LLOC)
    gather = ((lanes_of(tall) >> 3) == rows_of(tall)).astype(F32).astype(BF16)
    totals = jnp.sum(select_dot(gather, sums_ref[...]), axis=1, keepdims=True)
    table = table_ref[...]
    owner = (table >> 6 == rows_of((LANES, LLOC))).astype(F32).astype(BF16)
    small = (LLOC, LLOC)
    turned = jnp.where(rows_of(small) == lanes_of(small), (table & 63).astype(F32), 0.0)
    number = jnp.sum(turned, axis=1, keepdims=True).astype(jnp.int32) == lanes_of((LLOC, LANES))
    spread_ref[...] = select_dot(owner, jnp.where(number, totals, 0.0))
    for store in stores:
        store.wait()


def route(edges, ranges, up, down, depth, rates, codes, rate, code, lake_slot, lake_table):
    slabs = (SLABS, ROWS, LANES)
    slab = pltpu.VMEM(slabs, F32)
    return pl.pallas_call(
        route_kernel,
        out_shape=(jax.ShapeDtypeStruct(lake_slot.shape, F32), jax.ShapeDtypeStruct((LANES, LANES), F32)),
        in_specs=[SMEM] * 2 + [VMEM] * 3 + [HBM] * 6,
        out_specs=(HBM, VMEM),
        scratch_shapes=[
            slab,
            slab,
            pltpu.VMEM(slabs, jnp.int32),
            pltpu.VMEM(lake_slot.shape, jnp.int32),
            pltpu.VMEM(lake_slot.shape, F32),
            slab,
            slab,
            slab,
            pltpu.VMEM((8 * LLOC, LANES), F32),
            pltpu.SemaphoreType.DMA((17,)),
        ],
        compiler_params=params(),
        name="route",
    )(edges, ranges, up, down, lake_table.reshape(1, LLOC), depth, rates, codes, rate, code, lake_slot)


def pool_kernel(spread_ref, phase_ref, area_ref, crest_ref, level_ref, outflow_ref):
    inflow = jnp.sum(spread_ref[...], axis=0, keepdims=True)[:, :LLOC]
    area = area_ref[...]
    phase = phase_ref[...] + inflow / area
    excess = jnp.maximum(phase - crest_ref[...], 0.0)
    outflow = excess * jnp.sqrt(excess)
    level_ref[...] = phase - outflow / area
    outflow_ref[...] = outflow


def level_pool(spread, lake_phase, lake_area, lake_crest):
    row = jax.ShapeDtypeStruct((1, LLOC), F32)
    level, outflow = pl.pallas_call(
        pool_kernel,
        out_shape=(row, row),
        in_specs=[VMEM] * 4,
        out_specs=(VMEM,) * 2,
        compiler_params=params(),
        name="pool",
    )(spread, *(value.reshape(1, LLOC) for value in (lake_phase, lake_area, lake_crest)))
    return level.reshape(LLOC), outflow.reshape(LLOC)


def body(
    moisture, conduct, rainfall, weights, land_tile, head, rate, flow_code, lake_slot, lake_table,
    lake_phase, lake_area, lake_crest,
):
    both = ("row", "col")
    at_row, at_col = lax.axis_index("row"), lax.axis_index("col")
    edges = jnp.stack(
        [at_row == 0, at_row == lax.axis_size("row") - 1, at_col == 0, at_col == lax.axis_size("col") - 1]
    ).astype(jnp.int32)
    payload = land_payload(land_tile, moisture, conduct, rainfall, weights)
    payload, rate, flow_code, lake_slot, head, moisture = lax.optimization_barrier(
        (payload, rate, flow_code, lake_slot, head, moisture)
    )
    arrived = lax.all_to_all(
        payload.reshape(RUNS, 1, RUN_ROWS * LANES), both, split_axis=0, concat_axis=0, tiled=True
    ).reshape(RUNS * RUN_ROWS, LANES)
    cols, new_moisture = rim(moisture, conduct, rainfall, rate, flow_code, lake_slot, head)
    left = lax.ppermute(cols[8:16], "col", ring("col", 1))
    right = lax.ppermute(cols[0:8], "col", ring("col", -1))
    rates, codes, ranges, top, bottom = statics(rate, flow_code, lake_slot)
    depth, side_rate, side_code, top, bottom = place(edges, left, right, top, bottom, arrived, head)
    up = lax.ppermute(bottom, "row", ring("row", 1))
    down = lax.ppermute(top, "row", ring("row", -1))
    surface, spread = route(edges, ranges, up, down, depth, rates, codes, side_rate, side_code, lake_slot, lake_table)
    spread = lax.all_to_all(
        spread.reshape(RUNS, 1, LANES), both, split_axis=0, concat_axis=0, tiled=True
    ).reshape(RUNS, LANES)
    level, outflow = level_pool(spread, lake_phase, lake_area, lake_crest)
    return (new_moisture, surface, level, outflow)


def solution(mesh):
    blocks = P(("row", "col"))
    layers = P(None, ("row", "col"))
    cells = P("row", "col")
    in_specs = (layers, layers, blocks, layers, blocks) + (cells,) * 4 + (blocks,) * 4
    out_specs = (layers, cells, blocks, blocks)
    return jax.shard_map(body, mesh=mesh, in_specs=in_specs, out_specs=out_specs, check_vma=False)
```

```python
import jax
import jax.numpy as jnp
from jax import lax
from jax.experimental import pallas as pl
from jax.experimental.pallas import tpu as pltpu
from jax.sharding import PartitionSpec as P

AGG = 10
LLOC = 64
LANES = 128
RUNS = 128
RUN_ROWS = 26
SLABS = 6
ROWS = 672
FIRST = 16

LAYER_DEPTHS = (0.1, 0.3, 0.6, 1.0)
POROSITY = 0.45
TIME_STEP = 0.05
F32 = jnp.float32
BF16 = jnp.bfloat16
VMEM = pl.BlockSpec(memory_space=pltpu.VMEM)
HBM = pl.BlockSpec(memory_space=pltpu.HBM)
SMEM = pl.BlockSpec(memory_space=pltpu.SMEM)


def params(limit=60 * 1024 * 1024):
    return pltpu.CompilerParams(vmem_limit_bytes=limit)


def lanes_of(shape):
    return lax.broadcasted_iota(jnp.int32, shape, len(shape) - 1)


def rows_of(shape):
    return lax.broadcasted_iota(jnp.int32, shape, 0)


def split3(value):
    high = value.astype(BF16)
    rest = value - high.astype(F32)
    middle = rest.astype(BF16)
    low = (rest - middle.astype(F32)).astype(BF16)
    return high, middle, low


def select_dot(picks, value):
    return sum(jnp.dot(picks, part, preferred_element_type=F32) for part in split3(value))


def signed(rate, lake):
    return jnp.where(lake, -rate, rate)


def ring(axis, step):
    count = lax.axis_size(axis)
    return [(i, (i + step) % count) for i in range(count)]


def dot_select(value, picks, parts=3):
    return sum(jnp.dot(part, picks, preferred_element_type=F32) for part in split3(value)[:parts])


def quarter_transpose(arrays, quarter):
    rolled = []
    for d in range(4):
        skew = arrays[(3 + d) % 4]
        for m in range(3):
            skew = jnp.where(quarter == m, arrays[(m + d) % 4], skew)
        rolled.append(pltpu.roll(skew, 32 * d, 1) if d else skew)
    outs = []
    for r in range(4):
        out = rolled[(3 - r) % 4]
        for m in range(3):
            out = jnp.where(quarter == m, rolled[(m - r) % 4], out)
        outs.append(out)
    return outs


def send_kernel(
    tile_hbm, moisture_hbm, conduct_hbm, rain_hbm, weights_hbm, out_ref,
    tile_ref, moisture_ref, conduct_ref, rain_ref, slab_ref, edge_ref, sems,
):
    count = slab_ref.shape[0]

    def fetch(i):
        start = pl.multiple_of(i * LANES, LANES)
        return pltpu.make_async_copy(weights_hbm.at[:, pl.ds(start, LANES)], slab_ref.at[i], sems.at[i])

    small = [
        pltpu.make_async_copy(source, into, sems.at[count + n])
        for n, (source, into) in enumerate(
            ((tile_hbm, tile_ref), (moisture_hbm, moisture_ref), (conduct_hbm, conduct_ref), (rain_hbm, rain_ref))
        )
    ]
    for copy in small:
        copy.start()

    def begin(i, carry):
        fetch(i).start()
        return carry

    lax.fori_loop(0, count, begin, 0, unroll=4)
    for copy in small:
        copy.wait()
    lane = lanes_of((1, LANES))
    quarter = lane >> 5

    def step(i, carry):
        edges, tiles = carry
        start = pl.multiple_of(i * LANES, LANES)
        conduct = conduct_ref[0:1, pl.ds(start, LANES)]
        moisture = moisture_ref[0:1, pl.ds(start, LANES)]
        rain = rain_ref[0:1, pl.ds(start, LANES)]
        capacity = 10.0 * conduct * (1.5 - moisture / POROSITY)
        runoff = rain - rain * capacity / (rain + capacity)
        parts = [slab_ref[i, pl.ds(b, AGG, stride=AGG), :] for b in range(AGG)]
        total = sum(parts[1:], parts[0])
        mean = jnp.sum(total, axis=0, keepdims=True) * 0.01
        scale = runoff / mean
        parts = [part * scale for part in parts]
        tail = [slab_ref[i, pl.ds(first, 5, stride=AGG), :] * scale for first in (8, 9, 58, 59)]
        groups = (
            (0, AGG, quarter_transpose(parts[0:4], quarter)),
            (AGG, AGG, quarter_transpose(parts[4:8], quarter)),
            (2 * AGG, 5, quarter_transpose(tail, quarter)),
        )
        for r in range(4):
            tile = tile_ref[(4 * i + r) * 32]
            tiles = jnp.where(lane == (((0, 63, 64, 127)[r] + 2 * i) & 127), tile, tiles)
            for offset, length, outs in groups:
                out_ref[pl.ds(tile * RUN_ROWS + offset, length), :] = outs[r]
        place = ((lane & 63) == 2 * i) | ((lane & 63) == ((2 * i - 1) & 63))
        new_edges = []
        for b in range(2):
            both = jnp.where((lane & 1) == 0, parts[b], parts[8 + b])
            new_edges.append(jnp.where(place, pltpu.roll(both, 2 * i, 1), edges[b]))
        return tuple(new_edges), tiles

    zeros = jnp.zeros((AGG, LANES), F32)
    state = ((zeros, zeros), jnp.zeros((1, LANES), jnp.int32))
    group = 8

    def eight(n, carry):
        for j in range(group):
            fetch(n * group + j).wait()
        return lax.fori_loop(0, group, lambda j, inner: step(n * group + j, inner), carry, unroll=group)

    edges, tiles = lax.fori_loop(0, count // group, eight, state)
    edge_ref[...] = jnp.zeros((LANES, LANES), F32)
    edge_ref[0:AGG, :] = edges[0]
    edge_ref[16 : 16 + AGG, :] = edges[1]
    first = 2 * lane - jnp.where(lane < 64, 0, 126)
    second = jnp.where(lane < 63, 2 * lane + 5, jnp.where(lane == 127, 3, 2 * lane - 125))
    edge_ref[15:16, :] = jnp.where((lane & 1) == 0, first, second).astype(F32)
    by_run = edge_ref[...].T
    square = (LANES, LANES)
    here = (rows_of(square) == tiles).astype(F32).astype(BF16)
    by_tile = select_dot(here, by_run)
    run = by_tile[:, 15:16].astype(jnp.int32)
    wide = lanes_of(square)
    odd = (run & 1) == 1
    no_edge = jnp.where(wide == 15, -1.0, 0.0)
    row = pltpu.roll(jnp.where(odd, by_tile, no_edge), 1, 0)
    row = row + pltpu.roll(pltpu.roll(jnp.where(odd, no_edge, by_tile), LANES - 1, 0), 32, 1)
    row = row + jnp.where(wide == 127, run.astype(F32), 0.0)
    out_ref[pl.ds(25, RUNS, stride=RUN_ROWS), :] = row


def land_payload(land_tile, moisture, conduct, rainfall, weights):
    blocks = weights.shape[1]
    count = blocks // LANES
    return pl.pallas_call(
        send_kernel,
        out_shape=jax.ShapeDtypeStruct((RUNS * RUN_ROWS, LANES), F32),
        in_specs=[HBM] * 5,
        out_specs=VMEM,
        scratch_shapes=[
            pltpu.SMEM((blocks,), jnp.int32),
            pltpu.VMEM(moisture.shape, F32),
            pltpu.VMEM(conduct.shape, F32),
            pltpu.VMEM((1, blocks), F32),
            pltpu.VMEM((count, AGG * AGG, LANES), F32),
            pltpu.VMEM((LANES, LANES), F32),
            pltpu.SemaphoreType.DMA((count + 4,)),
        ],
        compiler_params=params(),
        name="land",
    )(land_tile, moisture, conduct, rainfall.reshape(1, blocks), weights)


def spread_columns():
    column = lanes_of((1, 640))
    block = (column * 6554) >> 16
    cell = column - AGG * block
    half = block >> 5
    quarter = jnp.where(cell < 8, cell & 3, cell - 8)
    source = (half * 3 + (cell >> 2)) * LANES + 32 * quarter + (block & 31)
    return (rows_of((SLABS * LANES, 640)) == source).astype(F32).astype(BF16)


def place_kernel(
    top_in, bottom_in, picks_ref, pay_ref, depth_hbm, top_ref, bottom_ref,
    depth_ref, cells_ref, tag_ref, tags, sems,
):
    arrived = pay_ref[pl.ds(25, RUNS, stride=RUN_ROWS), :]
    by_lane = arrived.T
    tag_ref[...] = jnp.broadcast_to(by_lane[127:128, :].astype(jnp.int32), (8, LANES))
    copy = pltpu.make_async_copy(tag_ref, tags, sems.at[4])
    copy.start()
    top_ref[...] = top_in[...]
    bottom_ref[...] = bottom_in[...]
    tall = (640, LANES)
    lane = lanes_of(tall)
    row = rows_of(tall)
    block = (row * 6554) >> 16
    left = (by_lane[15:16, :].astype(jnp.int32) == 2 * block + 1).astype(F32).astype(BF16)
    right = (by_lane[47:48, :].astype(jnp.int32) == 2 * block).astype(F32).astype(BF16)
    square = (LANES, LANES)
    wide = lanes_of(square)
    strips = select_dot(left, jnp.where(wide < 32, arrived, 0.0))
    strips = strips + select_dot(right, jnp.where((wide >= 32) & (wide < 64), arrived, 0.0))
    strips = jnp.where((lane & 15) == row - AGG * block, strips, 0.0)
    source = rows_of(square)
    group = source >> 4
    target = jnp.where(group < 2, 126, 0) + (group & 1)
    fold = (((source & 15) < AGG) & (group < 4) & (target == wide)).astype(F32).astype(BF16)
    depth = dot_select(strips, fold)
    depth_ref[SLABS - 1, FIRST : FIRST + 640, :] = depth
    top_ref[0:2, 640:768] += depth[0:2]
    bottom_ref[0:2, 640:768] += depth[638:640]
    picks = picks_ref[...]
    copy.wait()

    def settle(s, carry):
        run = tags[0, s]
        slab = (run & 1) * 3
        row = (run >> 1) * AGG
        start = s * RUN_ROWS
        cells_ref[slab, pl.ds(row, AGG), :] = pay_ref[pl.ds(start, AGG), :]
        cells_ref[slab + 1, pl.ds(row, AGG), :] = pay_ref[pl.ds(start + AGG, AGG), :]
        last = pay_ref[pl.ds(start + 2 * AGG, 5), :]
        cells_ref[slab + 2, pl.ds(row, 5), :] = last
        cells_ref[slab + 2, pl.ds(row + 5, 5), :] = pltpu.roll(last, 64, 1)
        return carry

    lax.fori_loop(0, RUNS, settle, 0, unroll=16)
    chunk = 160
    stores = []
    for m in range(0, 640, chunk):
        cells = jnp.concatenate([cells_ref[c, m : m + chunk, :] for c in range(SLABS)], axis=1)
        laid = dot_select(cells, picks, 2)
        for c in range(SLABS - 1):
            columns = slice(c * LANES, (c + 1) * LANES)
            depth = laid[:, columns]
            depth_ref[c, FIRST + m : FIRST + m + chunk, :] = depth
            if m == 0:
                top_ref[0:2, columns] += depth[0:2]
            if m == 640 - chunk:
                bottom_ref[0:2, columns] += depth[chunk - 2 :]
        rows = pl.ds(FIRST + m, chunk)
        store = pltpu.make_async_copy(depth_ref.at[:, rows, :], depth_hbm.at[:, rows, :], sems.at[m // chunk])
        store.start()
        stores.append(store)
    for store in stores:
        store.wait()


def place(top, bottom, picks, payload):
    strip = jax.ShapeDtypeStruct((8, 768), F32)
    slabs = (SLABS, ROWS, LANES)
    return pl.pallas_call(
        place_kernel,
        out_shape=(jax.ShapeDtypeStruct(slabs, F32), strip, strip),
        in_specs=[VMEM] * 4,
        out_specs=(HBM, VMEM, VMEM),
        scratch_shapes=[
            pltpu.VMEM(slabs, F32),
            pltpu.VMEM((SLABS, 640, LANES), F32),
            pltpu.VMEM((8, LANES), jnp.int32),
            pltpu.SMEM((8, LANES), jnp.int32),
            pltpu.SemaphoreType.DMA((5,)),
        ],
        compiler_params=params(52_500_000),
        name="place",
    )(top, bottom, picks, payload)


def rim_kernel(
    moisture_ref, conduct_ref, rain_ref, rate_hbm, code_hbm, slot_hbm, head_hbm, cols_ref, soil_ref,
    rate_ref, code_ref, slot_ref, head_ref, sems,
):
    fetches = []
    for n, (source, into) in enumerate(
        ((rate_hbm, rate_ref), (code_hbm, code_ref), (slot_hbm, slot_ref), (head_hbm, head_ref))
    ):
        for side in range(2):
            columns = pl.ds(side * 512, LANES)
            fetches.append(pltpu.make_async_copy(source.at[:, columns], into.at[side], sems.at[2 * n + side]))
    for copy in fetches:
        copy.start()
    for copy in fetches:
        copy.wait()

    def four(side):
        code = code_ref[side].astype(F32)
        lake = (slot_ref[side] < LLOC).astype(F32)
        return rate_ref[side], code, lake, head_ref[side]

    lane = lanes_of((640, LANES))
    gathered = jnp.zeros((640, LANES), F32)
    for n, first in enumerate(four(0)):
        value = pltpu.roll(first, 2 * n, 1) if n else first
        gathered = jnp.where((lane >> 1) == n, value, gathered)
    for n, last in enumerate(four(1)):
        value = pltpu.roll(last, 2 * n + 10, 1)
        gathered = jnp.where((lane >> 1) == n + 4, value, gathered)
    cols_ref[...] = gathered.T[0:16, :]

    rain = rain_ref[...]
    saturation = moisture_ref[...] / POROSITY
    squared = saturation * saturation
    drainage = conduct_ref[...] * (squared * squared)
    capacity = 10.0 * conduct_ref[0:1, :] * (1.5 - saturation[0:1])
    incoming = rain * capacity / (rain + capacity)
    for k, thickness in enumerate(LAYER_DEPTHS):
        leaving = drainage[k : k + 1]
        soil_ref[k : k + 1, :] = moisture_ref[k : k + 1, :] + TIME_STEP * (incoming - leaving) / thickness
        incoming = leaving


def rim(moisture, conduct, rainfall, rate, flow_code, lake_slot, head):
    pair = (2, 640, LANES)
    return pl.pallas_call(
        rim_kernel,
        out_shape=(jax.ShapeDtypeStruct((16, 640), F32), jax.ShapeDtypeStruct(moisture.shape, F32)),
        in_specs=[VMEM] * 3 + [HBM] * 4,
        out_specs=(VMEM,) * 2,
        scratch_shapes=[
            pltpu.VMEM(pair, F32),
            pltpu.VMEM(pair, jnp.int32),
            pltpu.VMEM(pair, jnp.int32),
            pltpu.VMEM(pair, F32),
            pltpu.SemaphoreType.DMA((8,)),
        ],
        compiler_params=params(),
        cost_estimate=pl.CostEstimate(flops=0, bytes_accessed=0, transcendentals=0),
        name="rim",
    )(moisture, conduct, rainfall.reshape(1, rainfall.shape[0]), rate, flow_code, lake_slot, head)


def static_kernel(
    rate_hbm, code_hbm, slot_hbm, head_hbm, rates_hbm, codes_hbm, ranges_ref, top_ref, bottom_ref, picks_ref,
    rate_ref, code_ref, slot_ref, head_ref, rates_ref, codes_ref, bits_ref, sems,
):
    fetches = [
        pltpu.make_async_copy(source, into, sems.at[n])
        for n, (source, into) in enumerate(
            (
                (rate_hbm, rate_ref),
                (code_hbm, code_ref),
                (slot_hbm, slot_ref),
                (head_hbm.at[0:8, :], head_ref.at[0:8, :]),
                (head_hbm.at[632:640, :], head_ref.at[8:16, :]),
            )
        )
    ]
    for copy in fetches:
        copy.start()
    picks_ref[...] = spread_columns()
    for copy in fetches:
        copy.wait()
    for ref, base, part, head in ((top_ref, 0, slice(0, 2), slice(0, 2)), (bottom_ref, 632, slice(6, 8), slice(14, 16))):
        rows = slice(base, base + 8)
        ref[...] = jnp.zeros((8, 768), F32)
        ref[0:2, 0:640] = head_ref[head, :]
        ref[2:4, 0:640] = rate_ref[rows, :][part]
        ref[4:6, 0:640] = code_ref[rows, :][part].astype(F32)
        ref[6:8, 0:640] = (slot_ref[rows, :][part] < LLOC).astype(F32)

    def center(g, carry):
        rows = pl.ds(pl.multiple_of(g * 8, 8), 8)
        into = pl.ds(pl.multiple_of(g * 8 + FIRST, 8), 8)
        low = jnp.zeros((8, LANES), jnp.int32)
        high = jnp.zeros((8, LANES), jnp.int32)
        for c in range(SLABS - 1):
            columns = slice(c * LANES, (c + 1) * LANES)
            slot = slot_ref[rows, columns]
            rates_ref[c, into, :] = signed(rate_ref[rows, columns], slot < LLOC)
            codes_ref[c, into, :] = code_ref[rows, columns]
            bit = jnp.left_shift(1, slot & 31)
            low = low | jnp.where(slot < 32, bit, 0)
            high = high | jnp.where((slot >= 32) & (slot < LLOC), bit, 0)
        for shift in (4, 2, 1):
            low = low | pltpu.roll(low, shift, 0)
            high = high | pltpu.roll(high, shift, 0)
        bits_ref[0, pl.ds(g, 1), :] = low[0:1]
        bits_ref[1, pl.ds(g, 1), :] = high[0:1]
        return carry

    lax.fori_loop(0, 80, center, 0, unroll=8)
    stores = [
        pltpu.make_async_copy(source, into, sems.at[5 + n])
        for n, (source, into) in enumerate(((rates_ref, rates_hbm), (codes_ref, codes_hbm)))
    ]
    for copy in stores:
        copy.start()
    low, high = bits_ref[0], bits_ref[1]
    for shift in (64, 32, 16, 8, 4, 2, 1):
        low = low | pltpu.roll(low, shift, 1)
        high = high | pltpu.roll(high, shift, 1)
    shape = (80, LANES)
    lane = lanes_of(shape)
    found = (jnp.right_shift(jnp.where(lane < 32, low, high), lane & 31) & 1) == 1
    group = rows_of(shape)
    begin = jnp.min(jnp.where(found, group, 80), axis=0, keepdims=True)
    end = jnp.max(jnp.where(found, group + 1, 0), axis=0, keepdims=True)
    longest = jnp.max(jnp.where(lane[0:1] < LLOC, end - begin, 0), axis=1, keepdims=True)
    ranges_ref[...] = jnp.zeros((8, LANES), jnp.int32)
    ranges_ref[0:1, :] = begin
    ranges_ref[1:2, :] = end
    ranges_ref[2:3, :] = jnp.broadcast_to(longest, (1, LANES))
    for copy in stores:
        copy.wait()


def statics(rate, flow_code, lake_slot, head):
    slabs = (SLABS - 1, ROWS, LANES)
    strip = jax.ShapeDtypeStruct((8, 768), F32)
    return pl.pallas_call(
        static_kernel,
        out_shape=(
            jax.ShapeDtypeStruct(slabs, F32),
            jax.ShapeDtypeStruct(slabs, jnp.int32),
            jax.ShapeDtypeStruct((8, LANES), jnp.int32),
            strip,
            strip,
            jax.ShapeDtypeStruct((SLABS * LANES, 640), BF16),
        ),
        in_specs=[HBM] * 4,
        out_specs=(HBM, HBM, VMEM, VMEM, VMEM, VMEM),
        scratch_shapes=[
            pltpu.VMEM(rate.shape, F32),
            pltpu.VMEM(rate.shape, jnp.int32),
            pltpu.VMEM(rate.shape, jnp.int32),
            pltpu.VMEM((16, 640), F32),
            pltpu.VMEM(slabs, F32),
            pltpu.VMEM(slabs, jnp.int32),
            pltpu.VMEM((2, 80, LANES), jnp.int32),
            pltpu.SemaphoreType.DMA((7,)),
        ],
        compiler_params=params(55000000),
        cost_estimate=pl.CostEstimate(flops=0, bytes_accessed=0, transcendentals=0),
        name="static",
    )(rate, flow_code, lake_slot, head)


def sides_kernel(
    edge_ref, left_ref, right_ref, top_in, bottom_in, rate_ref, code_ref, head_ref, top_ref, bottom_ref, turn_ref
):
    top_ref[...] = top_in[...]
    bottom_ref[...] = bottom_in[...]
    turn_ref[...] = jnp.zeros(turn_ref.shape, F32)
    turn_ref[0:8, :] = right_ref[...]
    turn_ref[8:16, :] = left_ref[...]
    turned = turn_ref[...].T
    lane = lanes_of((640, LANES))
    rightmost = lane < 2
    leftmost = lane >= 126

    def slab(n):
        right = pltpu.roll(turned, LANES - 2 * n, 1) if n else turned
        left = pltpu.roll(turned, 118 - 2 * n, 1)
        return jnp.where(rightmost, right, jnp.where(leftmost, left, 0.0))

    first_col, last_col = edge_ref[2] == 1, edge_ref[3] == 1
    inside = (rightmost & jnp.logical_not(last_col)) | (leftmost & jnp.logical_not(first_col))
    rate = slab(0)
    code = jnp.where(inside, slab(1), -1.0)
    lake = slab(2)
    rate_ref[...] = signed(rate, lake > 0.5)
    code_ref[...] = code.astype(jnp.int32)
    head = slab(3)
    head_ref[...] = head
    for ref, rows in ((top_ref, slice(0, 2)), (bottom_ref, slice(638, 640))):
        ref[0:2, 640:768] = head[rows]
        ref[2:4, 640:768] = rate[rows]
        ref[4:6, 640:768] = code[rows]
        ref[6:8, 640:768] = lake[rows]


def sides(edges, left, right, top, bottom):
    strip = jax.ShapeDtypeStruct(top.shape, F32)
    side = jax.ShapeDtypeStruct((640, LANES), F32)
    return pl.pallas_call(
        sides_kernel,
        out_shape=(side, jax.ShapeDtypeStruct(side.shape, jnp.int32), side, strip, strip),
        in_specs=[SMEM] + [VMEM] * 4,
        out_specs=(VMEM,) * 5,
        scratch_shapes=[pltpu.VMEM((LANES, 640), F32)],
        compiler_params=params(55_000_000),
        cost_estimate=pl.CostEstimate(flops=0, bytes_accessed=0, transcendentals=0),
        name="sides",
    )(edges, left, right, top, bottom)


def leave(depth, rate):
    conveyance = rate * jnp.exp(jnp.log(depth) * (2.0 / 3.0))
    return depth * conveyance / (1.0 + conveyance)


def route_kernel(
    edge_ref, ranges, up_ref, down_ref, table_ref, depth_hbm, head_hbm, rates_hbm, codes_hbm, rate_hbm, code_hbm, side_hbm, slot_hbm,
    surface_hbm, spread_ref,
    depth_ref, head_ref, rates_ref, codes_ref, slot_ref, surface_ref, leave_ref, next_ref, lake_ref, sums_ref, sems,
):
    quarters = [(0, 176), (176, 160), (336, 160), (496, 176)]

    def rows_in(source, into, n, q):
        rows = pl.ds(*quarters[q])
        return pltpu.make_async_copy(source.at[:, rows, :], into.at[:, rows, :], sems.at[4 * n + q])

    def heads_in(q):
        rows = pl.ds(160 * q, 160)
        return pltpu.make_async_copy(head_hbm.at[rows, :], head_ref.at[rows, 0:640], sems.at[17 + q])

    heads = [heads_in(q) for q in range(4)]
    depths = [rows_in(depth_hbm, depth_ref, 0, q) for q in range(4)]
    middle, side, rows = pl.ds(0, SLABS - 1), SLABS - 1, pl.ds(FIRST, 640)
    rates = [rows_in(rates_hbm, rates_ref.at[middle], 1, q) for q in range(4)]
    side_rate = pltpu.make_async_copy(rate_hbm, rates_ref.at[side, rows, :], sems.at[15])
    codes = pltpu.make_async_copy(codes_hbm, codes_ref.at[middle], sems.at[8])
    side_code = pltpu.make_async_copy(code_hbm, codes_ref.at[side, rows, :], sems.at[16])
    slots = pltpu.make_async_copy(slot_hbm, slot_ref, sems.at[9])
    side_head = pltpu.make_async_copy(side_hbm, head_ref.at[:, 640:768], sems.at[21])
    side_rate.start()
    side_head.start()
    for q in range(4):
        depths[q].start()
        heads[q].start()
        rates[q].start()
    codes.start()
    side_code.start()
    slots.start()
    lane = lanes_of((8, LANES))

    def at(g):
        return pl.ds(pl.multiple_of(g * 8, 8), 8)

    def start(c, rows, head):
        depth = depth_ref[c, rows, :] + head
        leaving = leave(depth, jnp.abs(rates_ref[c, rows, :]))
        leave_ref[c, rows, :] = leaving
        depth_ref[c, rows, :] = depth - leaving

    eight = (8, LANES)
    rims = ((1, up_ref, 6, edge_ref[0] == 1), (82, down_ref, 0, edge_ref[1] == 1))

    def first(g, carry):
        rows = at(g)
        for c in range(SLABS):
            start(c, rows, head_ref[at(g - 2), c * LANES : (c + 1) * LANES])
        return carry

    side_rate.wait()
    side_head.wait()
    for q, (begin, end) in enumerate(((2, 22), (22, 42), (42, 62), (62, 82))):
        depths[q].wait()
        heads[q].wait()
        rates[q].wait()
        lax.fori_loop(begin, end, first, 0, unroll=2)
    codes.wait()
    side_code.wait()
    for g, ref, offset, outside in rims:
        rows = slice(g * 8, g * 8 + 8)
        two = slice(g * 8 + offset, g * 8 + offset + 2)
        for c in range(SLABS):
            four = ref[:, c * LANES : (c + 1) * LANES]
            depth_ref[c, rows, :] = jnp.zeros(eight, F32)
            rates_ref[c, rows, :] = jnp.ones(eight, F32)
            codes_ref[c, rows, :] = jnp.full(eight, -1, jnp.int32)
            depth_ref[c, two, :] = four[0:2]
            rates_ref[c, two, :] = jnp.where(four[6:8] > 0.5, -four[2:4], four[2:4])
            codes_ref[c, two, :] = jnp.where(outside, -1, four[4:6].astype(jnp.int32))
            start(c, rows, 0.0)

    def gained(ref, g, slabs):
        east, middle, west = [], [], []
        base = g * 8
        for c in range(SLABS):
            here, above, below = (ref[c, pl.ds(base + d, 8), :] for d in (0, -1, 1))
            code, code_above, code_below = (codes_ref[c, pl.ds(base + d, 8), :] for d in (0, -1, 1))

            def pick(which, number, value):
                return jnp.where(which == number, value, 0.0)

            east.append(pick(code, 0, here) + pick(code_above, 1, above) + pick(code_below, 7, below))
            middle.append(pick(code_above, 2, above) + pick(code_below, 6, below))
            west.append(pick(code, 4, here) + pick(code_above, 3, above) + pick(code_below, 5, below))
        east = [pltpu.roll(value, 1, 1) for value in east]
        west = [pltpu.roll(value, LANES - 1, 1) for value in west]
        return [
            middle[c]
            + jnp.where(lane == 0, east[c - 1], east[c])
            + jnp.where(lane == LANES - 1, west[(c + 1) % SLABS], west[c])
            for c in range(slabs)
        ]

    def second(g, carry):
        rows = at(g)
        for c, gain in enumerate(gained(leave_ref, g, SLABS)):
            rate = rates_ref[c, rows, :]
            lake = rate < 0.0
            depth = depth_ref[c, rows, :] + gain
            kept = jnp.where(lake, 0.0, depth)
            leaving = leave(kept, jnp.abs(rate))
            next_ref[c, rows, :] = leaving
            depth_ref[c, rows, :] = kept - leaving
            if c < SLABS - 1:
                lake_ref[c, rows, :] = depth - kept
        return carry

    lax.fori_loop(1, 81, second, 0, unroll=16)
    for g in (81, 82):
        second(g, 0)

    def third(g, carry):
        rows = at(g)
        out = at(g - 2)
        for c, gain in enumerate(gained(next_ref, g, SLABS - 1)):
            depth = depth_ref[c, rows, :] + gain
            kept = jnp.where(rates_ref[c, rows, :] < 0.0, 0.0, depth)
            lake_ref[c, rows, :] += depth - kept
            surface_ref[out, c * LANES : (c + 1) * LANES] = kept
        return carry

    stores = []
    for q in range(5):
        lax.fori_loop(2 + 16 * q, 18 + 16 * q, third, 0, unroll=16)
        rows = pl.ds(128 * q, 128)
        store = pltpu.make_async_copy(surface_ref.at[rows, :], surface_hbm.at[rows, :], sems.at[10 + q])
        store.start()
        stores.append(store)
    slots.wait()
    sums_ref[...] = jnp.zeros(sums_ref.shape, F32)

    def layer(e, carry):
        def lake(slot, inner):
            g = ranges[0, slot] + e
            wanted = jnp.where(g < ranges[1, slot], slot, -1)
            g = jnp.minimum(g, 79)
            rows = at(g)
            from_rows = at(g + 2)
            into = pl.ds(pl.multiple_of(slot * 8, 8), 8)
            terms = []
            for c in range(SLABS - 1):
                mine = slot_ref[rows, c * LANES : (c + 1) * LANES] == wanted
                terms.append(jnp.where(mine, lake_ref[c, from_rows, :], 0.0))
            sums_ref[into, :] += (terms[0] + terms[1]) + (terms[2] + terms[3]) + terms[4]
            return inner

        return lax.fori_loop(0, LLOC, lake, carry, unroll=8)

    lax.fori_loop(0, ranges[2, 0], layer, 0)
    tall = (LLOC, 8 * LLOC)
    gather = ((lanes_of(tall) >> 3) == rows_of(tall)).astype(F32).astype(BF16)
    totals = jnp.sum(select_dot(gather, sums_ref[...]), axis=1, keepdims=True)
    table = table_ref[...]
    owner = (table >> 6 == rows_of((LANES, LLOC))).astype(F32).astype(BF16)
    small = (LLOC, LLOC)
    turned = jnp.where(rows_of(small) == lanes_of(small), (table & 63).astype(F32), 0.0)
    number = jnp.sum(turned, axis=1, keepdims=True).astype(jnp.int32) == lanes_of((LLOC, LANES))
    spread_ref[...] = select_dot(owner, jnp.where(number, totals, 0.0))
    for store in stores:
        store.wait()


def route(edges, ranges, up, down, depth, head, rates, codes, rate, code, side, lake_slot, lake_table):
    slabs = (SLABS, ROWS, LANES)
    slab = pltpu.VMEM(slabs, F32)
    return pl.pallas_call(
        route_kernel,
        out_shape=(jax.ShapeDtypeStruct(lake_slot.shape, F32), jax.ShapeDtypeStruct((LANES, LANES), F32)),
        in_specs=[SMEM] * 2 + [VMEM] * 3 + [HBM] * 8,
        out_specs=(HBM, VMEM),
        scratch_shapes=[
            slab,
            pltpu.VMEM((640, 768), F32),
            slab,
            pltpu.VMEM(slabs, jnp.int32),
            pltpu.VMEM(lake_slot.shape, jnp.int32),
            pltpu.VMEM(lake_slot.shape, F32),
            slab,
            slab,
            slab,
            pltpu.VMEM((8 * LLOC, LANES), F32),
            pltpu.SemaphoreType.DMA((22,)),
        ],
        compiler_params=params(55000000),
        name="route",
    )(edges, ranges, up, down, lake_table.reshape(1, LLOC), depth, head, rates, codes, rate, code, side, lake_slot)


def pool_kernel(spread_ref, phase_ref, area_ref, crest_ref, level_ref, outflow_ref):
    inflow = jnp.sum(spread_ref[...], axis=0, keepdims=True)[:, :LLOC]
    area = area_ref[...]
    phase = phase_ref[...] + inflow / area
    excess = jnp.maximum(phase - crest_ref[...], 0.0)
    outflow = excess * jnp.sqrt(excess)
    level_ref[...] = phase - outflow / area
    outflow_ref[...] = outflow


def level_pool(spread, lake_phase, lake_area, lake_crest):
    row = jax.ShapeDtypeStruct((1, LLOC), F32)
    level, outflow = pl.pallas_call(
        pool_kernel,
        out_shape=(row, row),
        in_specs=[VMEM] * 4,
        out_specs=(VMEM,) * 2,
        compiler_params=params(),
        name="pool",
    )(spread, *(value.reshape(1, LLOC) for value in (lake_phase, lake_area, lake_crest)))
    return level.reshape(LLOC), outflow.reshape(LLOC)


def body(
    moisture, conduct, rainfall, weights, land_tile, head, rate, flow_code, lake_slot, lake_table,
    lake_phase, lake_area, lake_crest,
):
    both = ("row", "col")
    at_row, at_col = lax.axis_index("row"), lax.axis_index("col")
    edges = jnp.stack(
        [at_row == 0, at_row == lax.axis_size("row") - 1, at_col == 0, at_col == lax.axis_size("col") - 1]
    ).astype(jnp.int32)
    payload = land_payload(land_tile, moisture, conduct, rainfall, weights)
    payload, rate, flow_code, lake_slot, head, moisture = lax.optimization_barrier(
        (payload, rate, flow_code, lake_slot, head, moisture)
    )
    arrived = lax.all_to_all(
        payload.reshape(RUNS, 1, RUN_ROWS * LANES), both, split_axis=0, concat_axis=0, tiled=True
    ).reshape(RUNS * RUN_ROWS, LANES)
    cols, new_moisture = rim(moisture, conduct, rainfall, rate, flow_code, lake_slot, head)
    left = lax.ppermute(cols[8:16], "col", ring("col", 1))
    right = lax.ppermute(cols[0:8], "col", ring("col", -1))
    rates, codes, ranges, top, bottom, picks = statics(rate, flow_code, lake_slot, head)
    side_rate, side_code, side_head, top, bottom = sides(edges, left, right, top, bottom)
    depth, top, bottom = place(top, bottom, picks, arrived)
    up = lax.ppermute(bottom, "row", ring("row", 1))
    down = lax.ppermute(top, "row", ring("row", -1))
    surface, spread = route(
        edges, ranges, up, down, depth, head, rates, codes, side_rate, side_code, side_head, lake_slot, lake_table
    )
    spread = lax.all_to_all(
        spread.reshape(RUNS, 1, LANES), both, split_axis=0, concat_axis=0, tiled=True
    ).reshape(RUNS, LANES)
    level, outflow = level_pool(spread, lake_phase, lake_area, lake_crest)
    return (new_moisture, surface, level, outflow)


def solution(mesh):
    blocks = P(("row", "col"))
    layers = P(None, ("row", "col"))
    cells = P("row", "col")
    in_specs = (layers, layers, blocks, layers, blocks) + (cells,) * 4 + (blocks,) * 4
    out_specs = (layers, cells, blocks, blocks)
    return jax.shard_map(body, mesh=mesh, in_specs=in_specs, out_specs=out_specs, check_vma=False)
```

```python
import jax
import jax.numpy as jnp
from jax import lax
from jax.experimental import pallas as pl
from jax.experimental.pallas import tpu as pltpu
from jax.sharding import PartitionSpec as P

AGG = 10
LLOC = 64
LANES = 128
RUNS = 128
RUN_ROWS = 26
SLABS = 6
ROWS = 672
FIRST = 16

LAYER_DEPTHS = (0.1, 0.3, 0.6, 1.0)
POROSITY = 0.45
TIME_STEP = 0.05
F32 = jnp.float32
BF16 = jnp.bfloat16
VMEM = pl.BlockSpec(memory_space=pltpu.VMEM)
HBM = pl.BlockSpec(memory_space=pltpu.HBM)
SMEM = pl.BlockSpec(memory_space=pltpu.SMEM)


def params(limit=60 * 1024 * 1024):
    return pltpu.CompilerParams(vmem_limit_bytes=limit)


def lanes_of(shape):
    return lax.broadcasted_iota(jnp.int32, shape, len(shape) - 1)


def rows_of(shape):
    return lax.broadcasted_iota(jnp.int32, shape, 0)


def split3(value):
    high = value.astype(BF16)
    rest = value - high.astype(F32)
    middle = rest.astype(BF16)
    low = (rest - middle.astype(F32)).astype(BF16)
    return high, middle, low


def select_dot(picks, value):
    return sum(jnp.dot(picks, part, preferred_element_type=F32) for part in split3(value))


def signed(rate, lake):
    return jnp.where(lake, -rate, rate)


def leave(depth, rate):
    conveyance = rate * jnp.exp(jnp.log(depth) * (2.0 / 3.0))
    return depth * conveyance / (1.0 + conveyance)


def ring(axis, step):
    count = lax.axis_size(axis)
    return [(i, (i + step) % count) for i in range(count)]


def dot_select(value, picks, parts=3):
    return sum(jnp.dot(part, picks, preferred_element_type=F32) for part in split3(value)[:parts])


def quarter_transpose(arrays, quarter):
    rolled = []
    for d in range(4):
        skew = arrays[(3 + d) % 4]
        for m in range(3):
            skew = jnp.where(quarter == m, arrays[(m + d) % 4], skew)
        rolled.append(pltpu.roll(skew, 32 * d, 1) if d else skew)
    outs = []
    for r in range(4):
        out = rolled[(3 - r) % 4]
        for m in range(3):
            out = jnp.where(quarter == m, rolled[(m - r) % 4], out)
        outs.append(out)
    return outs


def send_kernel(
    tile_hbm, moisture_hbm, conduct_hbm, rain_hbm, weights_hbm, out_ref,
    tile_ref, moisture_ref, conduct_ref, rain_ref, slab_ref, edge_ref, sems,
):
    count = slab_ref.shape[0]

    def fetch(i):
        start = pl.multiple_of(i * LANES, LANES)
        return pltpu.make_async_copy(weights_hbm.at[:, pl.ds(start, LANES)], slab_ref.at[i], sems.at[i])

    small = [
        pltpu.make_async_copy(source, into, sems.at[count + n])
        for n, (source, into) in enumerate(
            ((tile_hbm, tile_ref), (moisture_hbm, moisture_ref), (conduct_hbm, conduct_ref), (rain_hbm, rain_ref))
        )
    ]
    for copy in small:
        copy.start()

    def begin(i, carry):
        fetch(i).start()
        return carry

    lax.fori_loop(0, count, begin, 0, unroll=4)
    for copy in small:
        copy.wait()
    lane = lanes_of((1, LANES))
    quarter = lane >> 5

    def step(i, carry):
        edges, tiles = carry
        start = pl.multiple_of(i * LANES, LANES)
        conduct = conduct_ref[0:1, pl.ds(start, LANES)]
        moisture = moisture_ref[0:1, pl.ds(start, LANES)]
        rain = rain_ref[0:1, pl.ds(start, LANES)]
        capacity = 10.0 * conduct * (1.5 - moisture / POROSITY)
        runoff = rain - rain * capacity / (rain + capacity)
        parts = [slab_ref[i, pl.ds(b, AGG, stride=AGG), :] for b in range(AGG)]
        total = sum(parts[1:], parts[0])
        mean = jnp.sum(total, axis=0, keepdims=True) * 0.01
        scale = runoff / mean
        parts = [part * scale for part in parts]
        tail = [slab_ref[i, pl.ds(first, 5, stride=AGG), :] * scale for first in (8, 9, 58, 59)]
        groups = (
            (0, AGG, quarter_transpose(parts[0:4], quarter)),
            (AGG, AGG, quarter_transpose(parts[4:8], quarter)),
            (2 * AGG, 5, quarter_transpose(tail, quarter)),
        )
        for r in range(4):
            tile = tile_ref[(4 * i + r) * 32]
            tiles = jnp.where(lane == (((0, 63, 64, 127)[r] + 2 * i) & 127), tile, tiles)
            for offset, length, outs in groups:
                out_ref[pl.ds(tile * RUN_ROWS + offset, length), :] = outs[r]
        place = ((lane & 63) == 2 * i) | ((lane & 63) == ((2 * i - 1) & 63))
        new_edges = []
        for b in range(2):
            both = jnp.where((lane & 1) == 0, parts[b], parts[8 + b])
            new_edges.append(jnp.where(place, pltpu.roll(both, 2 * i, 1), edges[b]))
        return tuple(new_edges), tiles

    zeros = jnp.zeros((AGG, LANES), F32)
    state = ((zeros, zeros), jnp.zeros((1, LANES), jnp.int32))
    group = 8

    def eight(n, carry):
        for j in range(group):
            fetch(n * group + j).wait()
        return lax.fori_loop(0, group, lambda j, inner: step(n * group + j, inner), carry, unroll=group)

    edges, tiles = lax.fori_loop(0, count // group, eight, state)
    edge_ref[...] = jnp.zeros((LANES, LANES), F32)
    edge_ref[0:AGG, :] = edges[0]
    edge_ref[16 : 16 + AGG, :] = edges[1]
    first = 2 * lane - jnp.where(lane < 64, 0, 126)
    second = jnp.where(lane < 63, 2 * lane + 5, jnp.where(lane == 127, 3, 2 * lane - 125))
    edge_ref[15:16, :] = jnp.where((lane & 1) == 0, first, second).astype(F32)
    by_run = edge_ref[...].T
    square = (LANES, LANES)
    here = (rows_of(square) == tiles).astype(F32).astype(BF16)
    by_tile = select_dot(here, by_run)
    run = by_tile[:, 15:16].astype(jnp.int32)
    wide = lanes_of(square)
    odd = (run & 1) == 1
    no_edge = jnp.where(wide == 15, -1.0, 0.0)
    row = pltpu.roll(jnp.where(odd, by_tile, no_edge), 1, 0)
    row = row + pltpu.roll(pltpu.roll(jnp.where(odd, no_edge, by_tile), LANES - 1, 0), 32, 1)
    row = row + jnp.where(wide == 127, run.astype(F32), 0.0)
    out_ref[pl.ds(25, RUNS, stride=RUN_ROWS), :] = row


def land_payload(land_tile, moisture, conduct, rainfall, weights):
    blocks = weights.shape[1]
    count = blocks // LANES
    return pl.pallas_call(
        send_kernel,
        out_shape=jax.ShapeDtypeStruct((RUNS * RUN_ROWS, LANES), F32),
        in_specs=[HBM] * 5,
        out_specs=VMEM,
        scratch_shapes=[
            pltpu.SMEM((blocks,), jnp.int32),
            pltpu.VMEM(moisture.shape, F32),
            pltpu.VMEM(conduct.shape, F32),
            pltpu.VMEM((1, blocks), F32),
            pltpu.VMEM((count, AGG * AGG, LANES), F32),
            pltpu.VMEM((LANES, LANES), F32),
            pltpu.SemaphoreType.DMA((count + 4,)),
        ],
        compiler_params=params(),
        name="land",
    )(land_tile, moisture, conduct, rainfall.reshape(1, blocks), weights)


def spread_columns():
    column = lanes_of((1, 640))
    block = (column * 6554) >> 16
    cell = column - AGG * block
    half = block >> 5
    quarter = jnp.where(cell < 8, cell & 3, cell - 8)
    source = (half * 3 + (cell >> 2)) * LANES + 32 * quarter + (block & 31)
    return (rows_of((SLABS * LANES, 640)) == source).astype(F32).astype(BF16)


def place_kernel(
    top_in, bottom_in, picks_ref, pay_ref, depth_hbm, top_ref, bottom_ref,
    depth_ref, cells_ref, tag_ref, tags, sems,
):
    arrived = pay_ref[pl.ds(25, RUNS, stride=RUN_ROWS), :]
    by_lane = arrived.T
    tag_ref[...] = jnp.broadcast_to(by_lane[127:128, :].astype(jnp.int32), (8, LANES))
    copy = pltpu.make_async_copy(tag_ref, tags, sems.at[4])
    copy.start()
    top_ref[...] = top_in[...]
    bottom_ref[...] = bottom_in[...]
    tall = (640, LANES)
    lane = lanes_of(tall)
    row = rows_of(tall)
    block = (row * 6554) >> 16
    left = (by_lane[15:16, :].astype(jnp.int32) == 2 * block + 1).astype(F32).astype(BF16)
    right = (by_lane[47:48, :].astype(jnp.int32) == 2 * block).astype(F32).astype(BF16)
    square = (LANES, LANES)
    wide = lanes_of(square)
    strips = select_dot(left, jnp.where(wide < 32, arrived, 0.0))
    strips = strips + select_dot(right, jnp.where((wide >= 32) & (wide < 64), arrived, 0.0))
    strips = jnp.where((lane & 15) == row - AGG * block, strips, 0.0)
    source = rows_of(square)
    group = source >> 4
    target = jnp.where(group < 2, 126, 0) + (group & 1)
    fold = (((source & 15) < AGG) & (group < 4) & (target == wide)).astype(F32).astype(BF16)
    depth = dot_select(strips, fold)
    depth_ref[SLABS - 1, FIRST : FIRST + 640, :] = depth
    top_ref[0:2, 640:768] += depth[0:2]
    bottom_ref[0:2, 640:768] += depth[638:640]
    picks = picks_ref[...]
    copy.wait()

    def settle(s, carry):
        run = tags[0, s]
        slab = (run & 1) * 3
        row = (run >> 1) * AGG
        start = s * RUN_ROWS
        cells_ref[slab, pl.ds(row, AGG), :] = pay_ref[pl.ds(start, AGG), :]
        cells_ref[slab + 1, pl.ds(row, AGG), :] = pay_ref[pl.ds(start + AGG, AGG), :]
        last = pay_ref[pl.ds(start + 2 * AGG, 5), :]
        cells_ref[slab + 2, pl.ds(row, 5), :] = last
        cells_ref[slab + 2, pl.ds(row + 5, 5), :] = pltpu.roll(last, 64, 1)
        return carry

    lax.fori_loop(0, RUNS, settle, 0, unroll=16)
    chunk = 160
    stores = []
    for m in range(0, 640, chunk):
        cells = jnp.concatenate([cells_ref[c, m : m + chunk, :] for c in range(SLABS)], axis=1)
        laid = dot_select(cells, picks, 2)
        for c in range(SLABS - 1):
            columns = slice(c * LANES, (c + 1) * LANES)
            depth = laid[:, columns]
            depth_ref[c, FIRST + m : FIRST + m + chunk, :] = depth
            if m == 0:
                top_ref[0:2, columns] += depth[0:2]
            if m == 640 - chunk:
                bottom_ref[0:2, columns] += depth[chunk - 2 :]
        rows = pl.ds(FIRST + m, chunk)
        store = pltpu.make_async_copy(depth_ref.at[:, rows, :], depth_hbm.at[:, rows, :], sems.at[m // chunk])
        store.start()
        stores.append(store)
    for store in stores:
        store.wait()


def place(top, bottom, picks, payload):
    strip = jax.ShapeDtypeStruct((8, 768), F32)
    slabs = (SLABS, ROWS, LANES)
    return pl.pallas_call(
        place_kernel,
        out_shape=(jax.ShapeDtypeStruct(slabs, F32), strip, strip),
        in_specs=[VMEM] * 4,
        out_specs=(HBM, VMEM, VMEM),
        scratch_shapes=[
            pltpu.VMEM(slabs, F32),
            pltpu.VMEM((SLABS, 640, LANES), F32),
            pltpu.VMEM((8, LANES), jnp.int32),
            pltpu.SMEM((8, LANES), jnp.int32),
            pltpu.SemaphoreType.DMA((5,)),
        ],
        compiler_params=params(52_500_000),
        name="place",
    )(top, bottom, picks, payload)


def rim_kernel(
    moisture_ref, conduct_ref, rain_ref, rate_hbm, code_hbm, slot_hbm, head_hbm, cols_ref, soil_ref,
    rate_ref, code_ref, slot_ref, head_ref, sems,
):
    fetches = []
    for n, (source, into) in enumerate(
        ((rate_hbm, rate_ref), (code_hbm, code_ref), (slot_hbm, slot_ref), (head_hbm, head_ref))
    ):
        for side in range(2):
            columns = pl.ds(side * 512, LANES)
            fetches.append(pltpu.make_async_copy(source.at[:, columns], into.at[side], sems.at[2 * n + side]))
    for copy in fetches:
        copy.start()
    for copy in fetches:
        copy.wait()

    def four(side):
        code = code_ref[side].astype(F32)
        lake = (slot_ref[side] < LLOC).astype(F32)
        return rate_ref[side], code, lake, head_ref[side]

    lane = lanes_of((640, LANES))
    gathered = jnp.zeros((640, LANES), F32)
    for n, first in enumerate(four(0)):
        value = pltpu.roll(first, 2 * n, 1) if n else first
        gathered = jnp.where((lane >> 1) == n, value, gathered)
    for n, last in enumerate(four(1)):
        value = pltpu.roll(last, 2 * n + 10, 1)
        gathered = jnp.where((lane >> 1) == n + 4, value, gathered)
    cols_ref[...] = gathered.T[0:16, :]

    rain = rain_ref[...]
    saturation = moisture_ref[...] / POROSITY
    squared = saturation * saturation
    drainage = conduct_ref[...] * (squared * squared)
    capacity = 10.0 * conduct_ref[0:1, :] * (1.5 - saturation[0:1])
    incoming = rain * capacity / (rain + capacity)
    for k, thickness in enumerate(LAYER_DEPTHS):
        leaving = drainage[k : k + 1]
        soil_ref[k : k + 1, :] = moisture_ref[k : k + 1, :] + TIME_STEP * (incoming - leaving) / thickness
        incoming = leaving


def rim(moisture, conduct, rainfall, rate, flow_code, lake_slot, head):
    pair = (2, 640, LANES)
    return pl.pallas_call(
        rim_kernel,
        out_shape=(jax.ShapeDtypeStruct((16, 640), F32), jax.ShapeDtypeStruct(moisture.shape, F32)),
        in_specs=[VMEM] * 3 + [HBM] * 4,
        out_specs=(VMEM,) * 2,
        scratch_shapes=[
            pltpu.VMEM(pair, F32),
            pltpu.VMEM(pair, jnp.int32),
            pltpu.VMEM(pair, jnp.int32),
            pltpu.VMEM(pair, F32),
            pltpu.SemaphoreType.DMA((8,)),
        ],
        compiler_params=params(),
        cost_estimate=pl.CostEstimate(flops=0, bytes_accessed=0, transcendentals=0),
        name="rim",
    )(moisture, conduct, rainfall.reshape(1, rainfall.shape[0]), rate, flow_code, lake_slot, head)


def static_kernel(
    rate_hbm, code_hbm, slot_hbm, head_hbm, rates_hbm, codes_hbm, ranges_ref, top_ref, bottom_ref, picks_ref,
    rate_ref, code_ref, slot_ref, head_ref, rates_ref, codes_ref, bits_ref, sems,
):
    fetches = [
        pltpu.make_async_copy(source, into, sems.at[n])
        for n, (source, into) in enumerate(
            (
                (rate_hbm, rate_ref),
                (code_hbm, code_ref),
                (slot_hbm, slot_ref),
                (head_hbm.at[0:8, :], head_ref.at[0:8, :]),
                (head_hbm.at[632:640, :], head_ref.at[8:16, :]),
            )
        )
    ]
    for copy in fetches:
        copy.start()
    picks_ref[...] = spread_columns()
    for copy in fetches:
        copy.wait()
    for ref, base, part, head in ((top_ref, 0, slice(0, 2), slice(0, 2)), (bottom_ref, 632, slice(6, 8), slice(14, 16))):
        rows = slice(base, base + 8)
        ref[...] = jnp.zeros((8, 768), F32)
        ref[0:2, 0:640] = head_ref[head, :]
        ref[2:4, 0:640] = rate_ref[rows, :][part]
        ref[4:6, 0:640] = code_ref[rows, :][part].astype(F32)
        ref[6:8, 0:640] = (slot_ref[rows, :][part] < LLOC).astype(F32)

    def center(g, carry):
        rows = pl.ds(pl.multiple_of(g * 8, 8), 8)
        into = pl.ds(pl.multiple_of(g * 8 + FIRST, 8), 8)
        low = jnp.zeros((8, LANES), jnp.int32)
        high = jnp.zeros((8, LANES), jnp.int32)
        for c in range(SLABS - 1):
            columns = slice(c * LANES, (c + 1) * LANES)
            slot = slot_ref[rows, columns]
            rates_ref[c, into, :] = signed(rate_ref[rows, columns], slot < LLOC)
            codes_ref[c, into, :] = code_ref[rows, columns]
            bit = jnp.left_shift(1, slot & 31)
            low = low | jnp.where(slot < 32, bit, 0)
            high = high | jnp.where((slot >= 32) & (slot < LLOC), bit, 0)
        for shift in (4, 2, 1):
            low = low | pltpu.roll(low, shift, 0)
            high = high | pltpu.roll(high, shift, 0)
        bits_ref[0, pl.ds(g, 1), :] = low[0:1]
        bits_ref[1, pl.ds(g, 1), :] = high[0:1]
        return carry

    lax.fori_loop(0, 80, center, 0, unroll=8)
    stores = [
        pltpu.make_async_copy(source, into, sems.at[5 + n])
        for n, (source, into) in enumerate(((rates_ref, rates_hbm), (codes_ref, codes_hbm)))
    ]
    for copy in stores:
        copy.start()
    low, high = bits_ref[0], bits_ref[1]
    for shift in (64, 32, 16, 8, 4, 2, 1):
        low = low | pltpu.roll(low, shift, 1)
        high = high | pltpu.roll(high, shift, 1)
    shape = (80, LANES)
    lane = lanes_of(shape)
    found = (jnp.right_shift(jnp.where(lane < 32, low, high), lane & 31) & 1) == 1
    group = rows_of(shape)
    begin = jnp.min(jnp.where(found, group, 80), axis=0, keepdims=True)
    end = jnp.max(jnp.where(found, group + 1, 0), axis=0, keepdims=True)
    longest = jnp.max(jnp.where(lane[0:1] < LLOC, end - begin, 0), axis=1, keepdims=True)
    ranges_ref[...] = jnp.zeros((8, LANES), jnp.int32)
    ranges_ref[0:1, :] = begin
    ranges_ref[1:2, :] = end
    ranges_ref[2:3, :] = jnp.broadcast_to(longest, (1, LANES))
    for copy in stores:
        copy.wait()


def statics(rate, flow_code, lake_slot, head):
    slabs = (SLABS - 1, ROWS, LANES)
    strip = jax.ShapeDtypeStruct((8, 768), F32)
    return pl.pallas_call(
        static_kernel,
        out_shape=(
            jax.ShapeDtypeStruct(slabs, F32),
            jax.ShapeDtypeStruct(slabs, jnp.int32),
            jax.ShapeDtypeStruct((8, LANES), jnp.int32),
            strip,
            strip,
            jax.ShapeDtypeStruct((SLABS * LANES, 640), BF16),
        ),
        in_specs=[HBM] * 4,
        out_specs=(HBM, HBM, VMEM, VMEM, VMEM, VMEM),
        scratch_shapes=[
            pltpu.VMEM(rate.shape, F32),
            pltpu.VMEM(rate.shape, jnp.int32),
            pltpu.VMEM(rate.shape, jnp.int32),
            pltpu.VMEM((16, 640), F32),
            pltpu.VMEM(slabs, F32),
            pltpu.VMEM(slabs, jnp.int32),
            pltpu.VMEM((2, 80, LANES), jnp.int32),
            pltpu.SemaphoreType.DMA((7,)),
        ],
        compiler_params=params(55000000),
        cost_estimate=pl.CostEstimate(flops=0, bytes_accessed=0, transcendentals=0),
        name="static",
    )(rate, flow_code, lake_slot, head)


def sides_kernel(
    edge_ref, left_ref, right_ref, top_in, bottom_in, rate_ref, code_ref, head_ref, top_ref, bottom_ref, turn_ref
):
    top_ref[...] = top_in[...]
    bottom_ref[...] = bottom_in[...]
    turn_ref[...] = jnp.zeros(turn_ref.shape, F32)
    turn_ref[0:8, :] = right_ref[...]
    turn_ref[8:16, :] = left_ref[...]
    turned = turn_ref[...].T
    lane = lanes_of((640, LANES))
    rightmost = lane < 2
    leftmost = lane >= 126

    def slab(n):
        right = pltpu.roll(turned, LANES - 2 * n, 1) if n else turned
        left = pltpu.roll(turned, 118 - 2 * n, 1)
        return jnp.where(rightmost, right, jnp.where(leftmost, left, 0.0))

    first_col, last_col = edge_ref[2] == 1, edge_ref[3] == 1
    inside = (rightmost & jnp.logical_not(last_col)) | (leftmost & jnp.logical_not(first_col))
    rate = slab(0)
    code = jnp.where(inside, slab(1), -1.0)
    lake = slab(2)
    rate_ref[...] = signed(rate, lake > 0.5)
    code_ref[...] = code.astype(jnp.int32)
    head = slab(3)
    head_ref[...] = head
    for ref, rows in ((top_ref, slice(0, 2)), (bottom_ref, slice(638, 640))):
        ref[0:2, 640:768] = head[rows]
        ref[2:4, 640:768] = rate[rows]
        ref[4:6, 640:768] = code[rows]
        ref[6:8, 640:768] = lake[rows]


def sides(edges, left, right, top, bottom):
    strip = jax.ShapeDtypeStruct(top.shape, F32)
    side = jax.ShapeDtypeStruct((640, LANES), F32)
    return pl.pallas_call(
        sides_kernel,
        out_shape=(side, jax.ShapeDtypeStruct(side.shape, jnp.int32), side, strip, strip),
        in_specs=[SMEM] + [VMEM] * 4,
        out_specs=(VMEM,) * 5,
        scratch_shapes=[pltpu.VMEM((LANES, 640), F32)],
        compiler_params=params(55_000_000),
        cost_estimate=pl.CostEstimate(flops=0, bytes_accessed=0, transcendentals=0),
        name="sides",
    )(edges, left, right, top, bottom)


def open_kernel(
    depth_hbm, head_hbm, side_hbm, rates_hbm, rate_hbm, leave_hbm, stay_hbm,
    depth_ref, head_ref, rates_ref, leave_ref, sems,
):
    middle, side, center = pl.ds(0, SLABS - 1), SLABS - 1, pl.ds(FIRST, 640)
    fetches, stores = [], []
    for q in range(4):
        rows = pl.ds(FIRST + 160 * q, 160)
        from_rows = pl.ds(160 * q, 160)
        pairs = (
            (depth_hbm.at[:, rows, :], depth_ref.at[:, rows, :]),
            (rates_hbm.at[:, rows, :], rates_ref.at[middle, rows, :]),
            (head_hbm.at[from_rows, :], head_ref.at[from_rows, 0:640]),
        )
        fetches.append([pltpu.make_async_copy(*pair, sems.at[3 * q + n]) for n, pair in enumerate(pairs)])
        pairs = (
            (leave_ref.at[:, rows, :], leave_hbm.at[:, rows, :]),
            (depth_ref.at[:, rows, :], stay_hbm.at[:, rows, :]),
        )
        stores.append([pltpu.make_async_copy(*pair, sems.at[12 + 2 * q + n]) for n, pair in enumerate(pairs)])
    narrow = [
        pltpu.make_async_copy(rate_hbm, rates_ref.at[side, center, :], sems.at[20]),
        pltpu.make_async_copy(side_hbm, head_ref.at[:, 640:768], sems.at[21]),
    ]
    for copy in narrow + [copy for group in fetches for copy in group]:
        copy.start()
    for copy in narrow:
        copy.wait()

    def step(g, carry):
        rows = pl.ds(pl.multiple_of(g * 8, 8), 8)
        from_rows = pl.ds(pl.multiple_of(g * 8 - FIRST, 8), 8)
        for c in range(SLABS):
            depth = depth_ref[c, rows, :] + head_ref[from_rows, c * LANES : (c + 1) * LANES]
            leaving = leave(depth, jnp.abs(rates_ref[c, rows, :]))
            leave_ref[c, rows, :] = leaving
            depth_ref[c, rows, :] = depth - leaving
        return carry

    for q in range(4):
        for copy in fetches[q]:
            copy.wait()
        lax.fori_loop(2 + 20 * q, 22 + 20 * q, step, 0, unroll=5)
        for copy in stores[q]:
            copy.start()
    for group in stores:
        for copy in group:
            copy.wait()


def opening(depth, head, side, rates, rate):
    slab = pltpu.VMEM(depth.shape, F32)
    return pl.pallas_call(
        open_kernel,
        out_shape=(jax.ShapeDtypeStruct(depth.shape, F32),) * 2,
        in_specs=[HBM] * 5,
        out_specs=(HBM, HBM),
        scratch_shapes=[slab, pltpu.VMEM((640, 768), F32), slab, slab, pltpu.SemaphoreType.DMA((22,))],
        compiler_params=params(55_000_000),
        name="open",
    )(depth, head, side, rates, rate)


def route_kernel(
    edge_ref, ranges, up_ref, down_ref, table_ref, leave_hbm, stay_hbm, rates_hbm, codes_hbm, rate_hbm, code_hbm, slot_hbm,
    surface_hbm, spread_ref,
    leave_ref, stay_ref, rates_ref, codes_ref, slot_ref, surface_ref, next_ref, lake_ref, sums_ref, sems,
):
    middle, side, center = pl.ds(0, SLABS - 1), SLABS - 1, pl.ds(FIRST, 640)
    pairs = (
        (leave_hbm, leave_ref),
        (codes_hbm, codes_ref.at[middle]),
        (stay_hbm, stay_ref),
        (rates_hbm, rates_ref.at[middle]),
    )
    quarters = []
    for q in range(4):
        rows = pl.ds(FIRST + 160 * q, 160)
        quarters.append(
            [
                pltpu.make_async_copy(source.at[:, rows, :], into.at[:, rows, :], sems.at[4 * q + n])
                for n, (source, into) in enumerate(pairs)
            ]
        )
    narrow = [
        pltpu.make_async_copy(code_hbm, codes_ref.at[side, center, :], sems.at[16]),
        pltpu.make_async_copy(rate_hbm, rates_ref.at[side, center, :], sems.at[17]),
    ]
    slots = pltpu.make_async_copy(slot_hbm, slot_ref, sems.at[18])
    for copy in quarters[0] + narrow + quarters[1] + quarters[2] + quarters[3] + [slots]:
        copy.start()
    lane = lanes_of((8, LANES))

    def at(g):
        return pl.ds(pl.multiple_of(g * 8, 8), 8)

    eight = (8, LANES)
    for g, ref, offset, outside in ((1, up_ref, 6, edge_ref[0] == 1), (82, down_ref, 0, edge_ref[1] == 1)):
        rows = slice(g * 8, g * 8 + 8)
        two = slice(g * 8 + offset, g * 8 + offset + 2)
        for c in range(SLABS):
            four = ref[:, c * LANES : (c + 1) * LANES]
            rates_ref[c, rows, :] = jnp.ones(eight, F32)
            codes_ref[c, rows, :] = jnp.full(eight, -1, jnp.int32)
            leave_ref[c, rows, :] = jnp.zeros(eight, F32)
            stay_ref[c, rows, :] = jnp.zeros(eight, F32)
            leaving = leave(four[0:2], four[2:4])
            leave_ref[c, two, :] = leaving
            stay_ref[c, two, :] = four[0:2] - leaving
            rates_ref[c, two, :] = signed(four[2:4], four[6:8] > 0.5)
            codes_ref[c, two, :] = jnp.where(outside, -1, four[4:6].astype(jnp.int32))

    def gained(ref, g, slabs):
        east, middle, west = [], [], []
        base = g * 8
        for c in range(SLABS):
            here, above, below = (ref[c, pl.ds(base + d, 8), :] for d in (0, -1, 1))
            code, code_above, code_below = (codes_ref[c, pl.ds(base + d, 8), :] for d in (0, -1, 1))

            def pick(which, number, value):
                return jnp.where(which == number, value, 0.0)

            east.append(pick(code, 0, here) + pick(code_above, 1, above) + pick(code_below, 7, below))
            middle.append(pick(code_above, 2, above) + pick(code_below, 6, below))
            west.append(pick(code, 4, here) + pick(code_above, 3, above) + pick(code_below, 5, below))
        east = [pltpu.roll(value, 1, 1) for value in east]
        west = [pltpu.roll(value, LANES - 1, 1) for value in west]
        return [
            middle[c]
            + jnp.where(lane == 0, east[c - 1], east[c])
            + jnp.where(lane == LANES - 1, west[(c + 1) % SLABS], west[c])
            for c in range(slabs)
        ]

    def second(g, carry):
        rows = at(g)
        for c, gain in enumerate(gained(leave_ref, g, SLABS)):
            rate = rates_ref[c, rows, :]
            lake = rate < 0.0
            depth = stay_ref[c, rows, :] + gain
            kept = jnp.where(lake, 0.0, depth)
            leaving = leave(kept, jnp.abs(rate))
            next_ref[c, rows, :] = leaving
            stay_ref[c, rows, :] = kept - leaving
            if c < SLABS - 1:
                lake_ref[c, rows, :] = depth - kept
        return carry

    for q in range(4):
        for copy in quarters[q]:
            copy.wait()
        if q == 0:
            for copy in narrow:
                copy.wait()
        lax.fori_loop(1 + 20 * q, 21 + 20 * q, second, 0, unroll=20)
    for g in (81, 82):
        second(g, 0)

    def third(g, carry):
        rows = at(g)
        out = at(g - 2)
        for c, gain in enumerate(gained(next_ref, g, SLABS - 1)):
            depth = stay_ref[c, rows, :] + gain
            kept = jnp.where(rates_ref[c, rows, :] < 0.0, 0.0, depth)
            lake_ref[c, rows, :] += depth - kept
            surface_ref[out, c * LANES : (c + 1) * LANES] = kept
        return carry

    stores = []
    for q in range(5):
        lax.fori_loop(2 + 16 * q, 18 + 16 * q, third, 0, unroll=16)
        rows = pl.ds(128 * q, 128)
        store = pltpu.make_async_copy(surface_ref.at[rows, :], surface_hbm.at[rows, :], sems.at[19 + q])
        store.start()
        stores.append(store)
    slots.wait()
    sums_ref[...] = jnp.zeros(sums_ref.shape, F32)

    def layer(e, carry):
        def lake(slot, inner):
            g = ranges[0, slot] + e
            wanted = jnp.where(g < ranges[1, slot], slot, -1)
            g = jnp.minimum(g, 79)
            rows = at(g)
            from_rows = at(g + 2)
            into = pl.ds(pl.multiple_of(slot * 8, 8), 8)
            terms = []
            for c in range(SLABS - 1):
                mine = slot_ref[rows, c * LANES : (c + 1) * LANES] == wanted
                terms.append(jnp.where(mine, lake_ref[c, from_rows, :], 0.0))
            sums_ref[into, :] += (terms[0] + terms[1]) + (terms[2] + terms[3]) + terms[4]
            return inner

        return lax.fori_loop(0, LLOC, lake, carry, unroll=8)

    lax.fori_loop(0, ranges[2, 0], layer, 0)
    tall = (LLOC, 8 * LLOC)
    gather = ((lanes_of(tall) >> 3) == rows_of(tall)).astype(F32).astype(BF16)
    totals = jnp.sum(select_dot(gather, sums_ref[...]), axis=1, keepdims=True)
    table = table_ref[...]
    owner = (table >> 6 == rows_of((LANES, LLOC))).astype(F32).astype(BF16)
    small = (LLOC, LLOC)
    turned = jnp.where(rows_of(small) == lanes_of(small), (table & 63).astype(F32), 0.0)
    number = jnp.sum(turned, axis=1, keepdims=True).astype(jnp.int32) == lanes_of((LLOC, LANES))
    spread_ref[...] = select_dot(owner, jnp.where(number, totals, 0.0))
    for store in stores:
        store.wait()


def route(edges, ranges, up, down, leaving, stay, rates, codes, rate, code, lake_slot, lake_table):
    slabs = (SLABS, ROWS, LANES)
    slab = pltpu.VMEM(slabs, F32)
    return pl.pallas_call(
        route_kernel,
        out_shape=(jax.ShapeDtypeStruct(lake_slot.shape, F32), jax.ShapeDtypeStruct((LANES, LANES), F32)),
        in_specs=[SMEM] * 2 + [VMEM] * 3 + [HBM] * 7,
        out_specs=(HBM, VMEM),
        scratch_shapes=[
            slab,
            slab,
            slab,
            pltpu.VMEM(slabs, jnp.int32),
            pltpu.VMEM(lake_slot.shape, jnp.int32),
            pltpu.VMEM(lake_slot.shape, F32),
            slab,
            slab,
            pltpu.VMEM((8 * LLOC, LANES), F32),
            pltpu.SemaphoreType.DMA((24,)),
        ],
        compiler_params=params(55_000_000),
        name="route",
    )(edges, ranges, up, down, lake_table.reshape(1, LLOC), leaving, stay, rates, codes, rate, code, lake_slot)


def pool_kernel(spread_ref, phase_ref, area_ref, crest_ref, level_ref, outflow_ref):
    inflow = jnp.sum(spread_ref[...], axis=0, keepdims=True)[:, :LLOC]
    area = area_ref[...]
    phase = phase_ref[...] + inflow / area
    excess = jnp.maximum(phase - crest_ref[...], 0.0)
    outflow = excess * jnp.sqrt(excess)
    level_ref[...] = phase - outflow / area
    outflow_ref[...] = outflow


def level_pool(spread, lake_phase, lake_area, lake_crest):
    row = jax.ShapeDtypeStruct((1, LLOC), F32)
    level, outflow = pl.pallas_call(
        pool_kernel,
        out_shape=(row, row),
        in_specs=[VMEM] * 4,
        out_specs=(VMEM,) * 2,
        compiler_params=params(50_000_000),
        name="pool",
    )(spread, *(value.reshape(1, LLOC) for value in (lake_phase, lake_area, lake_crest)))
    return level.reshape(LLOC), outflow.reshape(LLOC)


def body(
    moisture, conduct, rainfall, weights, land_tile, head, rate, flow_code, lake_slot, lake_table,
    lake_phase, lake_area, lake_crest,
):
    both = ("row", "col")
    at_row, at_col = lax.axis_index("row"), lax.axis_index("col")
    edges = jnp.stack(
        [at_row == 0, at_row == lax.axis_size("row") - 1, at_col == 0, at_col == lax.axis_size("col") - 1]
    ).astype(jnp.int32)
    payload = land_payload(land_tile, moisture, conduct, rainfall, weights)
    payload, rate, flow_code, lake_slot, head, moisture = lax.optimization_barrier(
        (payload, rate, flow_code, lake_slot, head, moisture)
    )
    arrived = lax.all_to_all(
        payload.reshape(RUNS, 1, RUN_ROWS * LANES), both, split_axis=0, concat_axis=0, tiled=True
    ).reshape(RUNS * RUN_ROWS, LANES)
    cols, new_moisture = rim(moisture, conduct, rainfall, rate, flow_code, lake_slot, head)
    left = lax.ppermute(cols[8:16], "col", ring("col", 1))
    right = lax.ppermute(cols[0:8], "col", ring("col", -1))
    rates, codes, ranges, top, bottom, picks = statics(rate, flow_code, lake_slot, head)
    side_rate, side_code, side_head, top, bottom = sides(edges, left, right, top, bottom)
    depth, top, bottom = place(top, bottom, picks, arrived)
    up = lax.ppermute(bottom, "row", ring("row", 1))
    down = lax.ppermute(top, "row", ring("row", -1))
    leaving, stay = opening(depth, head, side_head, rates, side_rate)
    surface, spread = route(
        edges, ranges, up, down, leaving, stay, rates, codes, side_rate, side_code, lake_slot, lake_table
    )
    spread = lax.all_to_all(
        spread.reshape(RUNS, 1, LANES), both, split_axis=0, concat_axis=0, tiled=True
    ).reshape(RUNS, LANES)
    level, outflow = level_pool(spread, lake_phase, lake_area, lake_crest)
    return (new_moisture, surface, level, outflow)


def solution(mesh):
    blocks = P(("row", "col"))
    layers = P(None, ("row", "col"))
    cells = P("row", "col")
    in_specs = (layers, layers, blocks, layers, blocks) + (cells,) * 4 + (blocks,) * 4
    out_specs = (layers, cells, blocks, blocks)
    return jax.shard_map(body, mesh=mesh, in_specs=in_specs, out_specs=out_specs, check_vma=False)
```

```python
import jax
import jax.numpy as jnp
from jax import lax
from jax.experimental import pallas as pl
from jax.experimental.pallas import tpu as pltpu
from jax.sharding import PartitionSpec as P

AGG = 10
LLOC = 64
LANES = 128
RUNS = 128
RUN_ROWS = 26
SLABS = 6
ROWS = 672
FIRST = 16

LAYER_DEPTHS = (0.1, 0.3, 0.6, 1.0)
POROSITY = 0.45
TIME_STEP = 0.05
F32 = jnp.float32
BF16 = jnp.bfloat16
VMEM = pl.BlockSpec(memory_space=pltpu.VMEM)
HBM = pl.BlockSpec(memory_space=pltpu.HBM)
SMEM = pl.BlockSpec(memory_space=pltpu.SMEM)


def params(limit=60 * 1024 * 1024):
    return pltpu.CompilerParams(vmem_limit_bytes=limit)


def lanes_of(shape):
    return lax.broadcasted_iota(jnp.int32, shape, len(shape) - 1)


def rows_of(shape):
    return lax.broadcasted_iota(jnp.int32, shape, 0)


def split3(value):
    high = value.astype(BF16)
    rest = value - high.astype(F32)
    middle = rest.astype(BF16)
    low = (rest - middle.astype(F32)).astype(BF16)
    return high, middle, low


def select_dot(picks, value):
    return sum(jnp.dot(picks, part, preferred_element_type=F32) for part in split3(value))


def signed(rate, lake):
    return jnp.where(lake, -rate, rate)


def leave(depth, rate):
    conveyance = rate * jnp.exp(jnp.log(depth) * (2.0 / 3.0))
    return depth * conveyance / (1.0 + conveyance)


def ring(axis, step):
    count = lax.axis_size(axis)
    return [(i, (i + step) % count) for i in range(count)]


def dot_select(value, picks, parts=3):
    return sum(jnp.dot(part, picks, preferred_element_type=F32) for part in split3(value)[:parts])


def quarter_transpose(arrays, quarter):
    rolled = []
    for d in range(4):
        skew = arrays[(3 + d) % 4]
        for m in range(3):
            skew = jnp.where(quarter == m, arrays[(m + d) % 4], skew)
        rolled.append(pltpu.roll(skew, 32 * d, 1) if d else skew)
    outs = []
    for r in range(4):
        out = rolled[(3 - r) % 4]
        for m in range(3):
            out = jnp.where(quarter == m, rolled[(m - r) % 4], out)
        outs.append(out)
    return outs


def send_kernel(
    tile_hbm, moisture_hbm, conduct_hbm, rain_hbm, weights_hbm, out_ref,
    tile_ref, moisture_ref, conduct_ref, rain_ref, slab_ref, edge_ref, sems,
):
    count = slab_ref.shape[0]

    def fetch(i):
        start = pl.multiple_of(i * LANES, LANES)
        return pltpu.make_async_copy(weights_hbm.at[:, pl.ds(start, LANES)], slab_ref.at[i], sems.at[i])

    small = [
        pltpu.make_async_copy(source, into, sems.at[count + n])
        for n, (source, into) in enumerate(
            ((tile_hbm, tile_ref), (moisture_hbm, moisture_ref), (conduct_hbm, conduct_ref), (rain_hbm, rain_ref))
        )
    ]
    for copy in small:
        copy.start()

    def begin(i, carry):
        fetch(i).start()
        return carry

    lax.fori_loop(0, count, begin, 0, unroll=4)
    for copy in small:
        copy.wait()
    lane = lanes_of((1, LANES))
    quarter = lane >> 5

    def step(i, carry):
        edges, tiles = carry
        start = pl.multiple_of(i * LANES, LANES)
        conduct = conduct_ref[0:1, pl.ds(start, LANES)]
        moisture = moisture_ref[0:1, pl.ds(start, LANES)]
        rain = rain_ref[0:1, pl.ds(start, LANES)]
        capacity = 10.0 * conduct * (1.5 - moisture / POROSITY)
        runoff = rain - rain * capacity / (rain + capacity)
        parts = [slab_ref[i, pl.ds(b, AGG, stride=AGG), :] for b in range(AGG)]
        total = sum(parts[1:], parts[0])
        mean = jnp.sum(total, axis=0, keepdims=True) * 0.01
        scale = runoff / mean
        parts = [part * scale for part in parts]
        tail = [slab_ref[i, pl.ds(first, 5, stride=AGG), :] * scale for first in (8, 9, 58, 59)]
        groups = (
            (0, AGG, quarter_transpose(parts[0:4], quarter)),
            (AGG, AGG, quarter_transpose(parts[4:8], quarter)),
            (2 * AGG, 5, quarter_transpose(tail, quarter)),
        )
        for r in range(4):
            tile = tile_ref[(4 * i + r) * 32]
            tiles = jnp.where(lane == (((0, 63, 64, 127)[r] + 2 * i) & 127), tile, tiles)
            for offset, length, outs in groups:
                out_ref[pl.ds(tile * RUN_ROWS + offset, length), :] = outs[r]
        place = ((lane & 63) == 2 * i) | ((lane & 63) == ((2 * i - 1) & 63))
        new_edges = []
        for b in range(2):
            both = jnp.where((lane & 1) == 0, parts[b], parts[8 + b])
            new_edges.append(jnp.where(place, pltpu.roll(both, 2 * i, 1), edges[b]))
        return tuple(new_edges), tiles

    zeros = jnp.zeros((AGG, LANES), F32)
    state = ((zeros, zeros), jnp.zeros((1, LANES), jnp.int32))
    group = 8

    def eight(n, carry):
        for j in range(group):
            fetch(n * group + j).wait()
        return lax.fori_loop(0, group, lambda j, inner: step(n * group + j, inner), carry, unroll=group)

    edges, tiles = lax.fori_loop(0, count // group, eight, state)
    edge_ref[...] = jnp.zeros((LANES, LANES), F32)
    edge_ref[0:AGG, :] = edges[0]
    edge_ref[16 : 16 + AGG, :] = edges[1]
    first = 2 * lane - jnp.where(lane < 64, 0, 126)
    second = jnp.where(lane < 63, 2 * lane + 5, jnp.where(lane == 127, 3, 2 * lane - 125))
    edge_ref[15:16, :] = jnp.where((lane & 1) == 0, first, second).astype(F32)
    by_run = edge_ref[...].T
    square = (LANES, LANES)
    here = (rows_of(square) == tiles).astype(F32).astype(BF16)
    by_tile = select_dot(here, by_run)
    run = by_tile[:, 15:16].astype(jnp.int32)
    wide = lanes_of(square)
    odd = (run & 1) == 1
    no_edge = jnp.where(wide == 15, -1.0, 0.0)
    row = pltpu.roll(jnp.where(odd, by_tile, no_edge), 1, 0)
    row = row + pltpu.roll(pltpu.roll(jnp.where(odd, no_edge, by_tile), LANES - 1, 0), 32, 1)
    row = row + jnp.where(wide == 127, run.astype(F32), 0.0)
    out_ref[pl.ds(25, RUNS, stride=RUN_ROWS), :] = row


def land_payload(land_tile, moisture, conduct, rainfall, weights):
    blocks = weights.shape[1]
    count = blocks // LANES
    return pl.pallas_call(
        send_kernel,
        out_shape=jax.ShapeDtypeStruct((RUNS * RUN_ROWS, LANES), F32),
        in_specs=[HBM] * 5,
        out_specs=VMEM,
        scratch_shapes=[
            pltpu.SMEM((blocks,), jnp.int32),
            pltpu.VMEM(moisture.shape, F32),
            pltpu.VMEM(conduct.shape, F32),
            pltpu.VMEM((1, blocks), F32),
            pltpu.VMEM((count, AGG * AGG, LANES), F32),
            pltpu.VMEM((LANES, LANES), F32),
            pltpu.SemaphoreType.DMA((count + 4,)),
        ],
        compiler_params=params(),
        name="land",
    )(land_tile, moisture, conduct, rainfall.reshape(1, blocks), weights)


def spread_columns():
    column = lanes_of((1, 640))
    block = (column * 6554) >> 16
    cell = column - AGG * block
    half = block >> 5
    quarter = jnp.where(cell < 8, cell & 3, cell - 8)
    source = (half * 3 + (cell >> 2)) * LANES + 32 * quarter + (block & 31)
    return (rows_of((SLABS * LANES, 640)) == source).astype(F32).astype(BF16)


def place_kernel(
    top_in, bottom_in, picks_ref, pay_ref, depth_hbm, top_ref, bottom_ref,
    depth_ref, cells_ref, tag_ref, tags, sems,
):
    arrived = pay_ref[pl.ds(25, RUNS, stride=RUN_ROWS), :]
    by_lane = arrived.T
    tag_ref[...] = jnp.broadcast_to(by_lane[127:128, :].astype(jnp.int32), (8, LANES))
    copy = pltpu.make_async_copy(tag_ref, tags, sems.at[4])
    copy.start()
    top_ref[...] = top_in[...]
    bottom_ref[...] = bottom_in[...]
    tall = (640, LANES)
    lane = lanes_of(tall)
    row = rows_of(tall)
    block = (row * 6554) >> 16
    left = (by_lane[15:16, :].astype(jnp.int32) == 2 * block + 1).astype(F32).astype(BF16)
    right = (by_lane[47:48, :].astype(jnp.int32) == 2 * block).astype(F32).astype(BF16)
    square = (LANES, LANES)
    wide = lanes_of(square)
    strips = select_dot(left, jnp.where(wide < 32, arrived, 0.0))
    strips = strips + select_dot(right, jnp.where((wide >= 32) & (wide < 64), arrived, 0.0))
    strips = jnp.where((lane & 15) == row - AGG * block, strips, 0.0)
    source = rows_of(square)
    group = source >> 4
    target = jnp.where(group < 2, 126, 0) + (group & 1)
    fold = (((source & 15) < AGG) & (group < 4) & (target == wide)).astype(F32).astype(BF16)
    depth = dot_select(strips, fold)
    depth_ref[SLABS - 1, FIRST : FIRST + 640, :] = depth
    top_ref[0:2, 640:768] += depth[0:2]
    bottom_ref[0:2, 640:768] += depth[638:640]
    picks = picks_ref[...]
    copy.wait()

    def settle(s, carry):
        run = tags[0, s]
        slab = (run & 1) * 3
        row = (run >> 1) * AGG
        start = s * RUN_ROWS
        cells_ref[slab, pl.ds(row, AGG), :] = pay_ref[pl.ds(start, AGG), :]
        cells_ref[slab + 1, pl.ds(row, AGG), :] = pay_ref[pl.ds(start + AGG, AGG), :]
        last = pay_ref[pl.ds(start + 2 * AGG, 5), :]
        cells_ref[slab + 2, pl.ds(row, 5), :] = last
        cells_ref[slab + 2, pl.ds(row + 5, 5), :] = pltpu.roll(last, 64, 1)
        return carry

    lax.fori_loop(0, RUNS, settle, 0, unroll=32)
    chunk = 160
    stores = []
    for m in range(0, 640, chunk):
        cells = jnp.concatenate([cells_ref[c, m : m + chunk, :] for c in range(SLABS)], axis=1)
        laid = dot_select(cells, picks, 2)
        for c in range(SLABS - 1):
            columns = slice(c * LANES, (c + 1) * LANES)
            depth = laid[:, columns]
            depth_ref[c, FIRST + m : FIRST + m + chunk, :] = depth
            if m == 0:
                top_ref[0:2, columns] += depth[0:2]
            if m == 640 - chunk:
                bottom_ref[0:2, columns] += depth[chunk - 2 :]
        rows = pl.ds(FIRST + m, chunk)
        store = pltpu.make_async_copy(depth_ref.at[:, rows, :], depth_hbm.at[:, rows, :], sems.at[m // chunk])
        store.start()
        stores.append(store)
    for store in stores:
        store.wait()


def place(top, bottom, picks, payload):
    strip = jax.ShapeDtypeStruct((8, 768), F32)
    slabs = (SLABS, ROWS, LANES)
    return pl.pallas_call(
        place_kernel,
        out_shape=(jax.ShapeDtypeStruct(slabs, F32), strip, strip),
        in_specs=[VMEM] * 4,
        out_specs=(HBM, VMEM, VMEM),
        scratch_shapes=[
            pltpu.VMEM(slabs, F32),
            pltpu.VMEM((SLABS, 640, LANES), F32),
            pltpu.VMEM((8, LANES), jnp.int32),
            pltpu.SMEM((8, LANES), jnp.int32),
            pltpu.SemaphoreType.DMA((5,)),
        ],
        compiler_params=params(52_500_000),
        name="place",
    )(top, bottom, picks, payload)


def rim_kernel(
    moisture_ref, conduct_ref, rain_ref, rate_hbm, code_hbm, slot_hbm, head_hbm, cols_ref, soil_ref,
    rate_ref, code_ref, slot_ref, head_ref, sems,
):
    fetches = []
    for n, (source, into) in enumerate(
        ((rate_hbm, rate_ref), (code_hbm, code_ref), (slot_hbm, slot_ref), (head_hbm, head_ref))
    ):
        for side in range(2):
            columns = pl.ds(side * 512, LANES)
            fetches.append(pltpu.make_async_copy(source.at[:, columns], into.at[side], sems.at[2 * n + side]))
    for copy in fetches:
        copy.start()
    for copy in fetches:
        copy.wait()

    def four(side):
        code = code_ref[side].astype(F32)
        lake = (slot_ref[side] < LLOC).astype(F32)
        return rate_ref[side], code, lake, head_ref[side]

    lane = lanes_of((640, LANES))
    gathered = jnp.zeros((640, LANES), F32)
    for n, first in enumerate(four(0)):
        value = pltpu.roll(first, 2 * n, 1) if n else first
        gathered = jnp.where((lane >> 1) == n, value, gathered)
    for n, last in enumerate(four(1)):
        value = pltpu.roll(last, 2 * n + 10, 1)
        gathered = jnp.where((lane >> 1) == n + 4, value, gathered)
    cols_ref[...] = gathered.T[0:16, :]

    rain = rain_ref[...]
    saturation = moisture_ref[...] / POROSITY
    squared = saturation * saturation
    drainage = conduct_ref[...] * (squared * squared)
    capacity = 10.0 * conduct_ref[0:1, :] * (1.5 - saturation[0:1])
    incoming = rain * capacity / (rain + capacity)
    for k, thickness in enumerate(LAYER_DEPTHS):
        leaving = drainage[k : k + 1]
        soil_ref[k : k + 1, :] = moisture_ref[k : k + 1, :] + TIME_STEP * (incoming - leaving) / thickness
        incoming = leaving


def rim(moisture, conduct, rainfall, rate, flow_code, lake_slot, head):
    pair = (2, 640, LANES)
    return pl.pallas_call(
        rim_kernel,
        out_shape=(jax.ShapeDtypeStruct((16, 640), F32), jax.ShapeDtypeStruct(moisture.shape, F32)),
        in_specs=[VMEM] * 3 + [HBM] * 4,
        out_specs=(VMEM,) * 2,
        scratch_shapes=[
            pltpu.VMEM(pair, F32),
            pltpu.VMEM(pair, jnp.int32),
            pltpu.VMEM(pair, jnp.int32),
            pltpu.VMEM(pair, F32),
            pltpu.SemaphoreType.DMA((8,)),
        ],
        compiler_params=params(),
        cost_estimate=pl.CostEstimate(flops=0, bytes_accessed=0, transcendentals=0),
        name="rim",
    )(moisture, conduct, rainfall.reshape(1, rainfall.shape[0]), rate, flow_code, lake_slot, head)


def static_kernel(
    rate_hbm, code_hbm, slot_hbm, head_hbm, rates_hbm, codes_hbm, ranges_ref, top_ref, bottom_ref, picks_ref,
    rate_ref, code_ref, slot_ref, head_ref, rates_ref, codes_ref, bits_ref, sems,
):
    fetches = [
        pltpu.make_async_copy(source, into, sems.at[n])
        for n, (source, into) in enumerate(
            (
                (rate_hbm, rate_ref),
                (code_hbm, code_ref),
                (slot_hbm, slot_ref),
                (head_hbm.at[0:8, :], head_ref.at[0:8, :]),
                (head_hbm.at[632:640, :], head_ref.at[8:16, :]),
            )
        )
    ]
    for copy in fetches:
        copy.start()
    picks_ref[...] = spread_columns()
    for copy in fetches:
        copy.wait()
    for ref, base, part, head in ((top_ref, 0, slice(0, 2), slice(0, 2)), (bottom_ref, 632, slice(6, 8), slice(14, 16))):
        rows = slice(base, base + 8)
        ref[...] = jnp.zeros((8, 768), F32)
        ref[0:2, 0:640] = head_ref[head, :]
        ref[2:4, 0:640] = rate_ref[rows, :][part]
        ref[4:6, 0:640] = code_ref[rows, :][part].astype(F32)
        ref[6:8, 0:640] = (slot_ref[rows, :][part] < LLOC).astype(F32)

    def center(g, carry):
        rows = pl.ds(pl.multiple_of(g * 8, 8), 8)
        into = pl.ds(pl.multiple_of(g * 8 + FIRST, 8), 8)
        low = jnp.zeros((8, LANES), jnp.int32)
        high = jnp.zeros((8, LANES), jnp.int32)
        for c in range(SLABS - 1):
            columns = slice(c * LANES, (c + 1) * LANES)
            slot = slot_ref[rows, columns]
            rates_ref[c, into, :] = signed(rate_ref[rows, columns], slot < LLOC)
            codes_ref[c, into, :] = code_ref[rows, columns]
            bit = jnp.left_shift(1, slot & 31)
            low = low | jnp.where(slot < 32, bit, 0)
            high = high | jnp.where((slot >= 32) & (slot < LLOC), bit, 0)
        for shift in (4, 2, 1):
            low = low | pltpu.roll(low, shift, 0)
            high = high | pltpu.roll(high, shift, 0)
        bits_ref[0, pl.ds(g, 1), :] = low[0:1]
        bits_ref[1, pl.ds(g, 1), :] = high[0:1]
        return carry

    lax.fori_loop(0, 80, center, 0, unroll=8)
    stores = [
        pltpu.make_async_copy(source, into, sems.at[5 + n])
        for n, (source, into) in enumerate(((rates_ref, rates_hbm), (codes_ref, codes_hbm)))
    ]
    for copy in stores:
        copy.start()
    low, high = bits_ref[0], bits_ref[1]
    for shift in (64, 32, 16, 8, 4, 2, 1):
        low = low | pltpu.roll(low, shift, 1)
        high = high | pltpu.roll(high, shift, 1)
    shape = (80, LANES)
    lane = lanes_of(shape)
    found = (jnp.right_shift(jnp.where(lane < 32, low, high), lane & 31) & 1) == 1
    group = rows_of(shape)
    begin = jnp.min(jnp.where(found, group, 80), axis=0, keepdims=True)
    end = jnp.max(jnp.where(found, group + 1, 0), axis=0, keepdims=True)
    longest = jnp.max(jnp.where(lane[0:1] < LLOC, end - begin, 0), axis=1, keepdims=True)
    ranges_ref[...] = jnp.zeros((8, LANES), jnp.int32)
    ranges_ref[0:1, :] = begin
    ranges_ref[1:2, :] = end
    ranges_ref[2:3, :] = jnp.broadcast_to(longest, (1, LANES))
    for copy in stores:
        copy.wait()


def statics(rate, flow_code, lake_slot, head):
    slabs = (SLABS - 1, ROWS, LANES)
    strip = jax.ShapeDtypeStruct((8, 768), F32)
    return pl.pallas_call(
        static_kernel,
        out_shape=(
            jax.ShapeDtypeStruct(slabs, F32),
            jax.ShapeDtypeStruct(slabs, jnp.int32),
            jax.ShapeDtypeStruct((8, LANES), jnp.int32),
            strip,
            strip,
            jax.ShapeDtypeStruct((SLABS * LANES, 640), BF16),
        ),
        in_specs=[HBM] * 4,
        out_specs=(HBM, HBM, VMEM, VMEM, VMEM, VMEM),
        scratch_shapes=[
            pltpu.VMEM(rate.shape, F32),
            pltpu.VMEM(rate.shape, jnp.int32),
            pltpu.VMEM(rate.shape, jnp.int32),
            pltpu.VMEM((16, 640), F32),
            pltpu.VMEM(slabs, F32),
            pltpu.VMEM(slabs, jnp.int32),
            pltpu.VMEM((2, 80, LANES), jnp.int32),
            pltpu.SemaphoreType.DMA((7,)),
        ],
        compiler_params=params(55000000),
        cost_estimate=pl.CostEstimate(flops=0, bytes_accessed=0, transcendentals=0),
        name="static",
    )(rate, flow_code, lake_slot, head)


def sides_kernel(
    edge_ref, left_ref, right_ref, top_in, bottom_in, rate_ref, code_ref, head_ref, top_ref, bottom_ref, turn_ref
):
    top_ref[...] = top_in[...]
    bottom_ref[...] = bottom_in[...]
    turn_ref[...] = jnp.zeros(turn_ref.shape, F32)
    turn_ref[0:8, :] = right_ref[...]
    turn_ref[8:16, :] = left_ref[...]
    turned = turn_ref[...].T
    lane = lanes_of((640, LANES))
    rightmost = lane < 2
    leftmost = lane >= 126

    def slab(n):
        right = pltpu.roll(turned, LANES - 2 * n, 1) if n else turned
        left = pltpu.roll(turned, 118 - 2 * n, 1)
        return jnp.where(rightmost, right, jnp.where(leftmost, left, 0.0))

    first_col, last_col = edge_ref[2] == 1, edge_ref[3] == 1
    inside = (rightmost & jnp.logical_not(last_col)) | (leftmost & jnp.logical_not(first_col))
    rate = slab(0)
    code = jnp.where(inside, slab(1), -1.0)
    lake = slab(2)
    rate_ref[...] = signed(rate, lake > 0.5)
    code_ref[...] = code.astype(jnp.int32)
    head = slab(3)
    head_ref[...] = head
    for ref, rows in ((top_ref, slice(0, 2)), (bottom_ref, slice(638, 640))):
        ref[0:2, 640:768] = head[rows]
        ref[2:4, 640:768] = rate[rows]
        ref[4:6, 640:768] = code[rows]
        ref[6:8, 640:768] = lake[rows]


def sides(edges, left, right, top, bottom):
    strip = jax.ShapeDtypeStruct(top.shape, F32)
    side = jax.ShapeDtypeStruct((640, LANES), F32)
    return pl.pallas_call(
        sides_kernel,
        out_shape=(side, jax.ShapeDtypeStruct(side.shape, jnp.int32), side, strip, strip),
        in_specs=[SMEM] + [VMEM] * 4,
        out_specs=(VMEM,) * 5,
        scratch_shapes=[pltpu.VMEM((LANES, 640), F32)],
        compiler_params=params(55_000_000),
        cost_estimate=pl.CostEstimate(flops=0, bytes_accessed=0, transcendentals=0),
        name="sides",
    )(edges, left, right, top, bottom)


def open_kernel(
    depth_hbm, head_hbm, side_hbm, rates_hbm, rate_hbm, leave_hbm, stay_hbm,
    depth_ref, head_ref, rates_ref, leave_ref, sems,
):
    middle, side, center = pl.ds(0, SLABS - 1), SLABS - 1, pl.ds(FIRST, 640)
    fetches, stores = [], []
    for q in range(4):
        rows = pl.ds(FIRST + 160 * q, 160)
        from_rows = pl.ds(160 * q, 160)
        pairs = (
            (depth_hbm.at[:, rows, :], depth_ref.at[:, rows, :]),
            (rates_hbm.at[:, rows, :], rates_ref.at[middle, rows, :]),
            (head_hbm.at[from_rows, :], head_ref.at[from_rows, 0:640]),
        )
        fetches.append([pltpu.make_async_copy(*pair, sems.at[3 * q + n]) for n, pair in enumerate(pairs)])
        pairs = (
            (leave_ref.at[:, rows, :], leave_hbm.at[:, rows, :]),
            (depth_ref.at[:, rows, :], stay_hbm.at[:, rows, :]),
        )
        stores.append([pltpu.make_async_copy(*pair, sems.at[12 + 2 * q + n]) for n, pair in enumerate(pairs)])
    narrow = [
        pltpu.make_async_copy(rate_hbm, rates_ref.at[side, center, :], sems.at[20]),
        pltpu.make_async_copy(side_hbm, head_ref.at[:, 640:768], sems.at[21]),
    ]
    for copy in narrow + [copy for group in fetches for copy in group]:
        copy.start()
    for copy in narrow:
        copy.wait()

    def step(g, carry):
        rows = pl.ds(pl.multiple_of(g * 8, 8), 8)
        from_rows = pl.ds(pl.multiple_of(g * 8 - FIRST, 8), 8)
        for c in range(SLABS):
            depth = depth_ref[c, rows, :] + head_ref[from_rows, c * LANES : (c + 1) * LANES]
            leaving = leave(depth, jnp.abs(rates_ref[c, rows, :]))
            leave_ref[c, rows, :] = leaving
            depth_ref[c, rows, :] = depth - leaving
        return carry

    for q in range(4):
        for copy in fetches[q]:
            copy.wait()
        lax.fori_loop(2 + 20 * q, 22 + 20 * q, step, 0, unroll=5)
        for copy in stores[q]:
            copy.start()
    for group in stores:
        for copy in group:
            copy.wait()


def opening(depth, head, side, rates, rate):
    slab = pltpu.VMEM(depth.shape, F32)
    return pl.pallas_call(
        open_kernel,
        out_shape=(jax.ShapeDtypeStruct(depth.shape, F32),) * 2,
        in_specs=[HBM] * 5,
        out_specs=(HBM, HBM),
        scratch_shapes=[slab, pltpu.VMEM((640, 768), F32), slab, slab, pltpu.SemaphoreType.DMA((22,))],
        compiler_params=params(55_000_000),
        name="open",
    )(depth, head, side, rates, rate)


def route_kernel(
    edge_ref, ranges, up_ref, down_ref, table_ref, leave_hbm, stay_hbm, rates_hbm, codes_hbm, rate_hbm, code_hbm, slot_hbm,
    surface_hbm, spread_ref,
    leave_ref, stay_ref, rates_ref, codes_ref, slot_ref, surface_ref, next_ref, lake_ref, sums_ref, sems,
):
    middle, side, center = pl.ds(0, SLABS - 1), SLABS - 1, pl.ds(FIRST, 640)
    pairs = (
        (leave_hbm, leave_ref),
        (codes_hbm, codes_ref.at[middle]),
        (stay_hbm, stay_ref),
        (rates_hbm, rates_ref.at[middle]),
    )
    quarters = []
    for q in range(4):
        rows = pl.ds(FIRST + 160 * q, 160)
        quarters.append(
            [
                pltpu.make_async_copy(source.at[:, rows, :], into.at[:, rows, :], sems.at[4 * q + n])
                for n, (source, into) in enumerate(pairs)
            ]
        )
    narrow = [
        pltpu.make_async_copy(code_hbm, codes_ref.at[side, center, :], sems.at[16]),
        pltpu.make_async_copy(rate_hbm, rates_ref.at[side, center, :], sems.at[17]),
    ]
    slots = pltpu.make_async_copy(slot_hbm, slot_ref, sems.at[18])
    for copy in quarters[0] + narrow + quarters[1] + quarters[2] + quarters[3] + [slots]:
        copy.start()
    lane = lanes_of((8, LANES))

    def at(g):
        return pl.ds(pl.multiple_of(g * 8, 8), 8)

    eight = (8, LANES)
    for g, ref, offset, outside in ((1, up_ref, 6, edge_ref[0] == 1), (82, down_ref, 0, edge_ref[1] == 1)):
        rows = slice(g * 8, g * 8 + 8)
        two = slice(g * 8 + offset, g * 8 + offset + 2)
        for c in range(SLABS):
            four = ref[:, c * LANES : (c + 1) * LANES]
            rates_ref[c, rows, :] = jnp.ones(eight, F32)
            codes_ref[c, rows, :] = jnp.full(eight, -1, jnp.int32)
            leave_ref[c, rows, :] = jnp.zeros(eight, F32)
            stay_ref[c, rows, :] = jnp.zeros(eight, F32)
            leaving = leave(four[0:2], four[2:4])
            leave_ref[c, two, :] = leaving
            stay_ref[c, two, :] = four[0:2] - leaving
            rates_ref[c, two, :] = signed(four[2:4], four[6:8] > 0.5)
            codes_ref[c, two, :] = jnp.where(outside, -1, four[4:6].astype(jnp.int32))

    def gained(ref, g, slabs):
        east, middle, west = [], [], []
        base = g * 8
        for c in range(SLABS):
            here, above, below = (ref[c, pl.ds(base + d, 8), :] for d in (0, -1, 1))
            code, code_above, code_below = (codes_ref[c, pl.ds(base + d, 8), :] for d in (0, -1, 1))

            def pick(which, number, value):
                return jnp.where(which == number, value, 0.0)

            east.append(pick(code, 0, here) + pick(code_above, 1, above) + pick(code_below, 7, below))
            middle.append(pick(code_above, 2, above) + pick(code_below, 6, below))
            west.append(pick(code, 4, here) + pick(code_above, 3, above) + pick(code_below, 5, below))
        east = [pltpu.roll(value, 1, 1) for value in east]
        west = [pltpu.roll(value, LANES - 1, 1) for value in west]
        return [
            middle[c]
            + jnp.where(lane == 0, east[c - 1], east[c])
            + jnp.where(lane == LANES - 1, west[(c + 1) % SLABS], west[c])
            for c in range(slabs)
        ]

    def second(g, carry):
        rows = at(g)
        for c, gain in enumerate(gained(leave_ref, g, SLABS)):
            rate = rates_ref[c, rows, :]
            lake = rate < 0.0
            depth = stay_ref[c, rows, :] + gain
            kept = jnp.where(lake, 0.0, depth)
            leaving = leave(kept, jnp.abs(rate))
            next_ref[c, rows, :] = leaving
            stay_ref[c, rows, :] = kept - leaving
            if c < SLABS - 1:
                lake_ref[c, rows, :] = depth - kept
        return carry

    for q in range(4):
        for copy in quarters[q]:
            copy.wait()
        if q == 0:
            for copy in narrow:
                copy.wait()
        lax.fori_loop(1 + 20 * q, 21 + 20 * q, second, 0, unroll=20)
    for g in (81, 82):
        second(g, 0)

    def third(g, carry):
        rows = at(g)
        out = at(g - 2)
        for c, gain in enumerate(gained(next_ref, g, SLABS - 1)):
            depth = stay_ref[c, rows, :] + gain
            kept = jnp.where(rates_ref[c, rows, :] < 0.0, 0.0, depth)
            lake_ref[c, rows, :] += depth - kept
            surface_ref[out, c * LANES : (c + 1) * LANES] = kept
        return carry

    stores = []
    for q in range(5):
        lax.fori_loop(2 + 16 * q, 18 + 16 * q, third, 0, unroll=16)
        rows = pl.ds(128 * q, 128)
        store = pltpu.make_async_copy(surface_ref.at[rows, :], surface_hbm.at[rows, :], sems.at[19 + q])
        store.start()
        stores.append(store)
    slots.wait()
    sums_ref[...] = jnp.zeros(sums_ref.shape, F32)

    def layer(e, carry):
        def lake(slot, inner):
            g = ranges[0, slot] + e
            wanted = jnp.where(g < ranges[1, slot], slot, -1)
            g = jnp.minimum(g, 79)
            rows = at(g)
            from_rows = at(g + 2)
            into = pl.ds(pl.multiple_of(slot * 8, 8), 8)
            terms = []
            for c in range(SLABS - 1):
                mine = slot_ref[rows, c * LANES : (c + 1) * LANES] == wanted
                terms.append(jnp.where(mine, lake_ref[c, from_rows, :], 0.0))
            sums_ref[into, :] += (terms[0] + terms[1]) + (terms[2] + terms[3]) + terms[4]
            return inner

        return lax.fori_loop(0, LLOC, lake, carry, unroll=LLOC)

    lax.fori_loop(0, ranges[2, 0], layer, 0)
    tall = (LLOC, 8 * LLOC)
    gather = ((lanes_of(tall) >> 3) == rows_of(tall)).astype(F32).astype(BF16)
    totals = jnp.sum(select_dot(gather, sums_ref[...]), axis=1, keepdims=True)
    table = table_ref[...]
    owner = (table >> 6 == rows_of((LANES, LLOC))).astype(F32).astype(BF16)
    small = (LLOC, LLOC)
    turned = jnp.where(rows_of(small) == lanes_of(small), (table & 63).astype(F32), 0.0)
    number = jnp.sum(turned, axis=1, keepdims=True).astype(jnp.int32) == lanes_of((LLOC, LANES))
    spread_ref[...] = select_dot(owner, jnp.where(number, totals, 0.0))
    for store in stores:
        store.wait()


def route(edges, ranges, up, down, leaving, stay, rates, codes, rate, code, lake_slot, lake_table):
    slabs = (SLABS, ROWS, LANES)
    slab = pltpu.VMEM(slabs, F32)
    return pl.pallas_call(
        route_kernel,
        out_shape=(jax.ShapeDtypeStruct(lake_slot.shape, F32), jax.ShapeDtypeStruct((LANES, LANES), F32)),
        in_specs=[SMEM] * 2 + [VMEM] * 3 + [HBM] * 7,
        out_specs=(HBM, VMEM),
        scratch_shapes=[
            slab,
            slab,
            slab,
            pltpu.VMEM(slabs, jnp.int32),
            pltpu.VMEM(lake_slot.shape, jnp.int32),
            pltpu.VMEM(lake_slot.shape, F32),
            slab,
            slab,
            pltpu.VMEM((8 * LLOC, LANES), F32),
            pltpu.SemaphoreType.DMA((24,)),
        ],
        compiler_params=params(55_000_000),
        name="route",
    )(edges, ranges, up, down, lake_table.reshape(1, LLOC), leaving, stay, rates, codes, rate, code, lake_slot)


def pool_kernel(spread_ref, phase_ref, area_ref, crest_ref, level_ref, outflow_ref):
    inflow = jnp.sum(spread_ref[...], axis=0, keepdims=True)[:, :LLOC]
    area = area_ref[...]
    phase = phase_ref[...] + inflow / area
    excess = jnp.maximum(phase - crest_ref[...], 0.0)
    outflow = excess * jnp.sqrt(excess)
    level_ref[...] = phase - outflow / area
    outflow_ref[...] = outflow


def level_pool(spread, lake_phase, lake_area, lake_crest):
    row = jax.ShapeDtypeStruct((1, LLOC), F32)
    level, outflow = pl.pallas_call(
        pool_kernel,
        out_shape=(row, row),
        in_specs=[VMEM] * 4,
        out_specs=(VMEM,) * 2,
        compiler_params=params(50_000_000),
        name="pool",
    )(spread, *(value.reshape(1, LLOC) for value in (lake_phase, lake_area, lake_crest)))
    return level.reshape(LLOC), outflow.reshape(LLOC)


def body(
    moisture, conduct, rainfall, weights, land_tile, head, rate, flow_code, lake_slot, lake_table,
    lake_phase, lake_area, lake_crest,
):
    both = ("row", "col")
    at_row, at_col = lax.axis_index("row"), lax.axis_index("col")
    edges = jnp.stack(
        [at_row == 0, at_row == lax.axis_size("row") - 1, at_col == 0, at_col == lax.axis_size("col") - 1]
    ).astype(jnp.int32)
    payload = land_payload(land_tile, moisture, conduct, rainfall, weights)
    payload, rate, flow_code, lake_slot, head, moisture = lax.optimization_barrier(
        (payload, rate, flow_code, lake_slot, head, moisture)
    )
    arrived = lax.all_to_all(
        payload.reshape(RUNS, 1, RUN_ROWS * LANES), both, split_axis=0, concat_axis=0, tiled=True
    ).reshape(RUNS * RUN_ROWS, LANES)
    cols, new_moisture = rim(moisture, conduct, rainfall, rate, flow_code, lake_slot, head)
    left = lax.ppermute(cols[8:16], "col", ring("col", 1))
    right = lax.ppermute(cols[0:8], "col", ring("col", -1))
    rates, codes, ranges, top, bottom, picks = statics(rate, flow_code, lake_slot, head)
    side_rate, side_code, side_head, top, bottom = sides(edges, left, right, top, bottom)
    depth, top, bottom = place(top, bottom, picks, arrived)
    up = lax.ppermute(bottom, "row", ring("row", 1))
    down = lax.ppermute(top, "row", ring("row", -1))
    leaving, stay = opening(depth, head, side_head, rates, side_rate)
    surface, spread = route(
        edges, ranges, up, down, leaving, stay, rates, codes, side_rate, side_code, lake_slot, lake_table
    )
    spread = lax.all_to_all(
        spread.reshape(RUNS, 1, LANES), both, split_axis=0, concat_axis=0, tiled=True
    ).reshape(RUNS, LANES)
    level, outflow = level_pool(spread, lake_phase, lake_area, lake_crest)
    return (new_moisture, surface, level, outflow)


def solution(mesh):
    blocks = P(("row", "col"))
    layers = P(None, ("row", "col"))
    cells = P("row", "col")
    in_specs = (layers, layers, blocks, layers, blocks) + (cells,) * 4 + (blocks,) * 4
    out_specs = (layers, cells, blocks, blocks)
    return jax.shard_map(body, mesh=mesh, in_specs=in_specs, out_specs=out_specs, check_vma=False)
```

```python
import jax
import jax.numpy as jnp
from jax import lax
from jax.experimental import pallas as pl
from jax.experimental.pallas import tpu as pltpu
from jax.sharding import PartitionSpec as P

AGG = 10
LLOC = 64
LANES = 128
RUNS = 128
RUN_ROWS = 26
SLABS = 6
ROWS = 672
FIRST = 16

LAYER_DEPTHS = (0.1, 0.3, 0.6, 1.0)
POROSITY = 0.45
TIME_STEP = 0.05
F32 = jnp.float32
BF16 = jnp.bfloat16
VMEM = pl.BlockSpec(memory_space=pltpu.VMEM)
HBM = pl.BlockSpec(memory_space=pltpu.HBM)
SMEM = pl.BlockSpec(memory_space=pltpu.SMEM)


def params(limit=60 * 1024 * 1024):
    return pltpu.CompilerParams(vmem_limit_bytes=limit)


def lanes_of(shape):
    return lax.broadcasted_iota(jnp.int32, shape, len(shape) - 1)


def rows_of(shape):
    return lax.broadcasted_iota(jnp.int32, shape, 0)


def split3(value):
    high = value.astype(BF16)
    rest = value - high.astype(F32)
    middle = rest.astype(BF16)
    low = (rest - middle.astype(F32)).astype(BF16)
    return high, middle, low


def select_dot(picks, value):
    return sum(jnp.dot(picks, part, preferred_element_type=F32) for part in split3(value))


def signed(rate, lake):
    return jnp.where(lake, -rate, rate)


def leave(depth, rate):
    conveyance = rate * jnp.exp2(jnp.log2(depth) * (2.0 / 3.0))
    return depth * conveyance / (1.0 + conveyance)


def swap(axis, first):
    count = lax.axis_size(axis)
    pairs = []
    for i in range(first, first + count, 2):
        a, b = i % count, (i + 1) % count
        pairs += [(a, b), (b, a)]
    return pairs


def ring(axis, step):
    count = lax.axis_size(axis)
    return [(i, (i + step) % count) for i in range(count)]


def dot_select(value, picks, parts=3):
    return sum(jnp.dot(part, picks, preferred_element_type=F32) for part in split3(value)[:parts])


def quarter_transpose(arrays, quarter):
    rolled = []
    for d in range(4):
        skew = arrays[(3 + d) % 4]
        for m in range(3):
            skew = jnp.where(quarter == m, arrays[(m + d) % 4], skew)
        rolled.append(pltpu.roll(skew, 32 * d, 1) if d else skew)
    outs = []
    for r in range(4):
        out = rolled[(3 - r) % 4]
        for m in range(3):
            out = jnp.where(quarter == m, rolled[(m - r) % 4], out)
        outs.append(out)
    return outs


def send_kernel(
    tile_hbm, moisture_hbm, conduct_hbm, rain_hbm, weights_hbm, out_ref,
    tile_ref, moisture_ref, conduct_ref, rain_ref, slab_ref, edge_ref, sems,
):
    count = slab_ref.shape[0]

    def fetch(i):
        start = pl.multiple_of(i * LANES, LANES)
        return pltpu.make_async_copy(weights_hbm.at[:, pl.ds(start, LANES)], slab_ref.at[i], sems.at[i])

    small = [
        pltpu.make_async_copy(source, into, sems.at[count + n])
        for n, (source, into) in enumerate(
            ((tile_hbm, tile_ref), (moisture_hbm, moisture_ref), (conduct_hbm, conduct_ref), (rain_hbm, rain_ref))
        )
    ]
    for copy in small:
        copy.start()

    def begin(i, carry):
        fetch(i).start()
        return carry

    lax.fori_loop(0, count, begin, 0, unroll=4)
    for copy in small:
        copy.wait()
    lane = lanes_of((1, LANES))
    quarter = lane >> 5

    def step(i, carry):
        edges, tiles = carry
        start = pl.multiple_of(i * LANES, LANES)
        conduct = conduct_ref[0:1, pl.ds(start, LANES)]
        moisture = moisture_ref[0:1, pl.ds(start, LANES)]
        rain = rain_ref[0:1, pl.ds(start, LANES)]
        capacity = 10.0 * conduct * (1.5 - moisture / POROSITY)
        runoff = rain - rain * capacity / (rain + capacity)
        parts = [slab_ref[i, pl.ds(b, AGG, stride=AGG), :] for b in range(AGG)]
        total = sum(parts[1:], parts[0])
        mean = jnp.sum(total, axis=0, keepdims=True) * 0.01
        scale = runoff / mean
        parts = [part * scale for part in parts]
        tail = [slab_ref[i, pl.ds(first, 5, stride=AGG), :] * scale for first in (8, 9, 58, 59)]
        groups = (
            (0, AGG, quarter_transpose(parts[0:4], quarter)),
            (AGG, AGG, quarter_transpose(parts[4:8], quarter)),
            (2 * AGG, 5, quarter_transpose(tail, quarter)),
        )
        for r in range(4):
            tile = tile_ref[(4 * i + r) * 32]
            tiles = jnp.where(lane == (((0, 63, 64, 127)[r] + 2 * i) & 127), tile, tiles)
            for offset, length, outs in groups:
                out_ref[pl.ds(tile * RUN_ROWS + offset, length), :] = outs[r]
        place = ((lane & 63) == 2 * i) | ((lane & 63) == ((2 * i - 1) & 63))
        new_edges = []
        for b in range(2):
            both = jnp.where((lane & 1) == 0, parts[b], parts[8 + b])
            new_edges.append(jnp.where(place, pltpu.roll(both, 2 * i, 1), edges[b]))
        return tuple(new_edges), tiles

    zeros = jnp.zeros((AGG, LANES), F32)
    state = ((zeros, zeros), jnp.zeros((1, LANES), jnp.int32))
    group = 8

    def eight(n, carry):
        for j in range(group):
            fetch(n * group + j).wait()
        return lax.fori_loop(0, group, lambda j, inner: step(n * group + j, inner), carry, unroll=group)

    edges, tiles = lax.fori_loop(0, count // group, eight, state)
    edge_ref[...] = jnp.zeros((LANES, LANES), F32)
    edge_ref[0:AGG, :] = edges[0]
    edge_ref[16 : 16 + AGG, :] = edges[1]
    first = 2 * lane - jnp.where(lane < 64, 0, 126)
    second = jnp.where(lane < 63, 2 * lane + 5, jnp.where(lane == 127, 3, 2 * lane - 125))
    edge_ref[15:16, :] = jnp.where((lane & 1) == 0, first, second).astype(F32)
    by_run = edge_ref[...].T
    square = (LANES, LANES)
    here = (rows_of(square) == tiles).astype(F32).astype(BF16)
    by_tile = select_dot(here, by_run)
    run = by_tile[:, 15:16].astype(jnp.int32)
    wide = lanes_of(square)
    odd = (run & 1) == 1
    no_edge = jnp.where(wide == 15, -1.0, 0.0)
    row = pltpu.roll(jnp.where(odd, by_tile, no_edge), 1, 0)
    row = row + pltpu.roll(pltpu.roll(jnp.where(odd, no_edge, by_tile), LANES - 1, 0), 32, 1)
    row = row + jnp.where(wide == 127, run.astype(F32), 0.0)
    out_ref[pl.ds(25, RUNS, stride=RUN_ROWS), :] = row


def land_payload(land_tile, moisture, conduct, rainfall, weights):
    blocks = weights.shape[1]
    count = blocks // LANES
    return pl.pallas_call(
        send_kernel,
        out_shape=jax.ShapeDtypeStruct((RUNS * RUN_ROWS, LANES), F32),
        in_specs=[HBM] * 5,
        out_specs=VMEM,
        scratch_shapes=[
            pltpu.SMEM((blocks,), jnp.int32),
            pltpu.VMEM(moisture.shape, F32),
            pltpu.VMEM(conduct.shape, F32),
            pltpu.VMEM((1, blocks), F32),
            pltpu.VMEM((count, AGG * AGG, LANES), F32),
            pltpu.VMEM((LANES, LANES), F32),
            pltpu.SemaphoreType.DMA((count + 4,)),
        ],
        compiler_params=params(),
        name="land",
    )(land_tile, moisture, conduct, rainfall.reshape(1, blocks), weights)


def spread_columns():
    column = lanes_of((1, 640))
    block = (column * 6554) >> 16
    cell = column - AGG * block
    half = block >> 5
    quarter = jnp.where(cell < 8, cell & 3, cell - 8)
    source = (half * 3 + (cell >> 2)) * LANES + 32 * quarter + (block & 31)
    return (rows_of((SLABS * LANES, 640)) == source).astype(F32).astype(BF16)


def place_kernel(
    top_in, bottom_in, picks_ref, pay_ref, depth_hbm, top_ref, bottom_ref,
    depth_ref, cells_ref, tag_ref, tags, sems,
):
    arrived = pay_ref[pl.ds(25, RUNS, stride=RUN_ROWS), :]
    by_lane = arrived.T
    tag_ref[...] = jnp.broadcast_to(by_lane[127:128, :].astype(jnp.int32), (8, LANES))
    copy = pltpu.make_async_copy(tag_ref, tags, sems.at[4])
    copy.start()
    top_ref[...] = top_in[...]
    bottom_ref[...] = bottom_in[...]
    tall = (640, LANES)
    lane = lanes_of(tall)
    row = rows_of(tall)
    block = (row * 6554) >> 16
    left = (by_lane[15:16, :].astype(jnp.int32) == 2 * block + 1).astype(F32).astype(BF16)
    right = (by_lane[47:48, :].astype(jnp.int32) == 2 * block).astype(F32).astype(BF16)
    square = (LANES, LANES)
    wide = lanes_of(square)
    strips = select_dot(left, jnp.where(wide < 32, arrived, 0.0))
    strips = strips + select_dot(right, jnp.where((wide >= 32) & (wide < 64), arrived, 0.0))
    strips = jnp.where((lane & 15) == row - AGG * block, strips, 0.0)
    source = rows_of(square)
    group = source >> 4
    target = jnp.where(group < 2, 126, 0) + (group & 1)
    fold = (((source & 15) < AGG) & (group < 4) & (target == wide)).astype(F32).astype(BF16)
    depth = dot_select(strips, fold)
    depth_ref[SLABS - 1, FIRST : FIRST + 640, :] = depth
    top_ref[0:2, 640:768] += depth[0:2]
    bottom_ref[0:2, 640:768] += depth[638:640]
    picks = picks_ref[...]
    copy.wait()

    def settle(s, carry):
        run = tags[0, s]
        slab = (run & 1) * 3
        row = (run >> 1) * AGG
        start = s * RUN_ROWS
        cells_ref[slab, pl.ds(row, AGG), :] = pay_ref[pl.ds(start, AGG), :]
        cells_ref[slab + 1, pl.ds(row, AGG), :] = pay_ref[pl.ds(start + AGG, AGG), :]
        last = pay_ref[pl.ds(start + 2 * AGG, 5), :]
        cells_ref[slab + 2, pl.ds(row, 5), :] = last
        cells_ref[slab + 2, pl.ds(row + 5, 5), :] = pltpu.roll(last, 64, 1)
        return carry

    lax.fori_loop(0, RUNS, settle, 0, unroll=32)
    chunk = 160
    stores = []
    for m in range(0, 640, chunk):
        cells = jnp.concatenate([cells_ref[c, m : m + chunk, :] for c in range(SLABS)], axis=1)
        laid = dot_select(cells, picks, 2)
        for c in range(SLABS - 1):
            columns = slice(c * LANES, (c + 1) * LANES)
            depth = laid[:, columns]
            depth_ref[c, FIRST + m : FIRST + m + chunk, :] = depth
            if m == 0:
                top_ref[0:2, columns] += depth[0:2]
            if m == 640 - chunk:
                bottom_ref[0:2, columns] += depth[chunk - 2 :]
        rows = pl.ds(FIRST + m, chunk)
        store = pltpu.make_async_copy(depth_ref.at[:, rows, :], depth_hbm.at[:, rows, :], sems.at[m // chunk])
        store.start()
        stores.append(store)
    for store in stores:
        store.wait()


def place(top, bottom, picks, payload):
    strip = jax.ShapeDtypeStruct((8, 768), F32)
    slabs = (SLABS, ROWS, LANES)
    return pl.pallas_call(
        place_kernel,
        out_shape=(jax.ShapeDtypeStruct(slabs, F32), strip, strip),
        in_specs=[VMEM] * 4,
        out_specs=(HBM, VMEM, VMEM),
        scratch_shapes=[
            pltpu.VMEM(slabs, F32),
            pltpu.VMEM((SLABS, 640, LANES), F32),
            pltpu.VMEM((8, LANES), jnp.int32),
            pltpu.SMEM((8, LANES), jnp.int32),
            pltpu.SemaphoreType.DMA((5,)),
        ],
        compiler_params=params(52_500_000),
        name="place",
    )(top, bottom, picks, payload)


def rim_kernel(
    moisture_ref, conduct_ref, rain_ref, rate_hbm, code_hbm, slot_hbm, head_hbm, cols_ref, soil_ref,
    rate_ref, code_ref, slot_ref, head_ref, sems,
):
    fetches = []
    for n, (source, into) in enumerate(
        ((rate_hbm, rate_ref), (code_hbm, code_ref), (slot_hbm, slot_ref), (head_hbm, head_ref))
    ):
        for side in range(2):
            columns = pl.ds(side * 512, LANES)
            fetches.append(pltpu.make_async_copy(source.at[:, columns], into.at[side], sems.at[2 * n + side]))
    for copy in fetches:
        copy.start()
    for copy in fetches:
        copy.wait()

    def four(side):
        code = code_ref[side].astype(F32)
        lake = (slot_ref[side] < LLOC).astype(F32)
        return rate_ref[side], code, lake, head_ref[side]

    lane = lanes_of((640, LANES))
    gathered = jnp.zeros((640, LANES), F32)
    for n, first in enumerate(four(0)):
        value = pltpu.roll(first, 2 * n, 1) if n else first
        gathered = jnp.where((lane >> 1) == n, value, gathered)
    for n, last in enumerate(four(1)):
        value = pltpu.roll(last, 2 * n + 10, 1)
        gathered = jnp.where((lane >> 1) == n + 4, value, gathered)
    cols_ref[...] = gathered.T[0:16, :]

    rain = rain_ref[...]
    saturation = moisture_ref[...] / POROSITY
    squared = saturation * saturation
    drainage = conduct_ref[...] * (squared * squared)
    capacity = 10.0 * conduct_ref[0:1, :] * (1.5 - saturation[0:1])
    incoming = rain * capacity / (rain + capacity)
    for k, thickness in enumerate(LAYER_DEPTHS):
        leaving = drainage[k : k + 1]
        soil_ref[k : k + 1, :] = moisture_ref[k : k + 1, :] + TIME_STEP * (incoming - leaving) / thickness
        incoming = leaving


def rim(moisture, conduct, rainfall, rate, flow_code, lake_slot, head):
    pair = (2, 640, LANES)
    return pl.pallas_call(
        rim_kernel,
        out_shape=(jax.ShapeDtypeStruct((16, 640), F32), jax.ShapeDtypeStruct(moisture.shape, F32)),
        in_specs=[VMEM] * 3 + [HBM] * 4,
        out_specs=(VMEM,) * 2,
        scratch_shapes=[
            pltpu.VMEM(pair, F32),
            pltpu.VMEM(pair, jnp.int32),
            pltpu.VMEM(pair, jnp.int32),
            pltpu.VMEM(pair, F32),
            pltpu.SemaphoreType.DMA((8,)),
        ],
        compiler_params=params(),
        cost_estimate=pl.CostEstimate(flops=0, bytes_accessed=0, transcendentals=0),
        name="rim",
    )(moisture, conduct, rainfall.reshape(1, rainfall.shape[0]), rate, flow_code, lake_slot, head)


def static_kernel(
    rate_hbm, code_hbm, slot_hbm, head_hbm, rates_hbm, codes_hbm, ranges_ref, top_ref, bottom_ref, picks_ref,
    rate_ref, code_ref, slot_ref, head_ref, rates_ref, codes_ref, bits_ref, sems,
):
    fetches = [
        pltpu.make_async_copy(source, into, sems.at[n])
        for n, (source, into) in enumerate(
            (
                (rate_hbm, rate_ref),
                (code_hbm, code_ref),
                (slot_hbm, slot_ref),
                (head_hbm.at[0:8, :], head_ref.at[0:8, :]),
                (head_hbm.at[632:640, :], head_ref.at[8:16, :]),
            )
        )
    ]
    for copy in fetches:
        copy.start()
    picks_ref[...] = spread_columns()
    for copy in fetches:
        copy.wait()
    for ref, base, part, head in ((top_ref, 0, slice(0, 2), slice(0, 2)), (bottom_ref, 632, slice(6, 8), slice(14, 16))):
        rows = slice(base, base + 8)
        ref[...] = jnp.zeros((8, 768), F32)
        ref[0:2, 0:640] = head_ref[head, :]
        ref[2:4, 0:640] = rate_ref[rows, :][part]
        ref[4:6, 0:640] = code_ref[rows, :][part].astype(F32)
        ref[6:8, 0:640] = (slot_ref[rows, :][part] < LLOC).astype(F32)

    def center(g, carry):
        rows = pl.ds(pl.multiple_of(g * 8, 8), 8)
        into = pl.ds(pl.multiple_of(g * 8 + FIRST, 8), 8)
        low = jnp.zeros((8, LANES), jnp.int32)
        high = jnp.zeros((8, LANES), jnp.int32)
        for c in range(SLABS - 1):
            columns = slice(c * LANES, (c + 1) * LANES)
            slot = slot_ref[rows, columns]
            rates_ref[c, into, :] = signed(rate_ref[rows, columns], slot < LLOC)
            codes_ref[c, into, :] = code_ref[rows, columns]
            bit = jnp.left_shift(1, slot & 31)
            low = low | jnp.where(slot < 32, bit, 0)
            high = high | jnp.where((slot >= 32) & (slot < LLOC), bit, 0)
        for shift in (4, 2, 1):
            low = low | pltpu.roll(low, shift, 0)
            high = high | pltpu.roll(high, shift, 0)
        bits_ref[0, pl.ds(g, 1), :] = low[0:1]
        bits_ref[1, pl.ds(g, 1), :] = high[0:1]
        return carry

    lax.fori_loop(0, 80, center, 0, unroll=8)
    stores = [
        pltpu.make_async_copy(source, into, sems.at[5 + n])
        for n, (source, into) in enumerate(((rates_ref, rates_hbm), (codes_ref, codes_hbm)))
    ]
    for copy in stores:
        copy.start()
    low, high = bits_ref[0], bits_ref[1]
    for shift in (64, 32, 16, 8, 4, 2, 1):
        low = low | pltpu.roll(low, shift, 1)
        high = high | pltpu.roll(high, shift, 1)
    shape = (80, LANES)
    lane = lanes_of(shape)
    found = (jnp.right_shift(jnp.where(lane < 32, low, high), lane & 31) & 1) == 1
    group = rows_of(shape)
    begin = jnp.min(jnp.where(found, group, 80), axis=0, keepdims=True)
    end = jnp.max(jnp.where(found, group + 1, 0), axis=0, keepdims=True)
    longest = jnp.max(jnp.where(lane[0:1] < LLOC, end - begin, 0), axis=1, keepdims=True)
    ranges_ref[...] = jnp.zeros((8, LANES), jnp.int32)
    ranges_ref[0:1, :] = begin
    ranges_ref[1:2, :] = end
    ranges_ref[2:3, :] = jnp.broadcast_to(longest, (1, LANES))
    for copy in stores:
        copy.wait()


def statics(rate, flow_code, lake_slot, head):
    slabs = (SLABS - 1, ROWS, LANES)
    strip = jax.ShapeDtypeStruct((8, 768), F32)
    return pl.pallas_call(
        static_kernel,
        out_shape=(
            jax.ShapeDtypeStruct(slabs, F32),
            jax.ShapeDtypeStruct(slabs, jnp.int32),
            jax.ShapeDtypeStruct((8, LANES), jnp.int32),
            strip,
            strip,
            jax.ShapeDtypeStruct((SLABS * LANES, 640), BF16),
        ),
        in_specs=[HBM] * 4,
        out_specs=(HBM, HBM, VMEM, VMEM, VMEM, VMEM),
        scratch_shapes=[
            pltpu.VMEM(rate.shape, F32),
            pltpu.VMEM(rate.shape, jnp.int32),
            pltpu.VMEM(rate.shape, jnp.int32),
            pltpu.VMEM((16, 640), F32),
            pltpu.VMEM(slabs, F32),
            pltpu.VMEM(slabs, jnp.int32),
            pltpu.VMEM((2, 80, LANES), jnp.int32),
            pltpu.SemaphoreType.DMA((7,)),
        ],
        compiler_params=params(55000000),
        cost_estimate=pl.CostEstimate(flops=0, bytes_accessed=0, transcendentals=0),
        name="static",
    )(rate, flow_code, lake_slot, head)


def sides_kernel(
    edge_ref, left_ref, right_ref, top_in, bottom_in, rate_ref, code_ref, head_ref, top_ref, bottom_ref, turn_ref
):
    top_ref[...] = top_in[...]
    bottom_ref[...] = bottom_in[...]
    turn_ref[...] = jnp.zeros(turn_ref.shape, F32)
    turn_ref[0:8, :] = right_ref[...]
    turn_ref[8:16, :] = left_ref[...]
    turned = turn_ref[...].T
    lane = lanes_of((640, LANES))
    rightmost = lane < 2
    leftmost = lane >= 126

    def slab(n):
        right = pltpu.roll(turned, LANES - 2 * n, 1) if n else turned
        left = pltpu.roll(turned, 118 - 2 * n, 1)
        return jnp.where(rightmost, right, jnp.where(leftmost, left, 0.0))

    first_col, last_col = edge_ref[2] == 1, edge_ref[3] == 1
    inside = (rightmost & jnp.logical_not(last_col)) | (leftmost & jnp.logical_not(first_col))
    rate = slab(0)
    code = jnp.where(inside, slab(1), -1.0)
    lake = slab(2)
    rate_ref[...] = signed(rate, lake > 0.5)
    code_ref[...] = code.astype(jnp.int32)
    head = slab(3)
    head_ref[...] = head
    for ref, rows in ((top_ref, slice(0, 2)), (bottom_ref, slice(638, 640))):
        ref[0:2, 640:768] = head[rows]
        ref[2:4, 640:768] = rate[rows]
        ref[4:6, 640:768] = code[rows]
        ref[6:8, 640:768] = lake[rows]


def sides(edges, left, right, top, bottom):
    strip = jax.ShapeDtypeStruct(top.shape, F32)
    side = jax.ShapeDtypeStruct((640, LANES), F32)
    return pl.pallas_call(
        sides_kernel,
        out_shape=(side, jax.ShapeDtypeStruct(side.shape, jnp.int32), side, strip, strip),
        in_specs=[SMEM] + [VMEM] * 4,
        out_specs=(VMEM,) * 5,
        scratch_shapes=[pltpu.VMEM((LANES, 640), F32)],
        compiler_params=params(55_000_000),
        cost_estimate=pl.CostEstimate(flops=0, bytes_accessed=0, transcendentals=0),
        name="sides",
    )(edges, left, right, top, bottom)


def open_kernel(
    depth_hbm, head_hbm, side_hbm, rates_hbm, rate_hbm, leave_hbm, stay_hbm,
    depth_ref, head_ref, rates_ref, leave_ref, sems,
):
    middle, side, center = pl.ds(0, SLABS - 1), SLABS - 1, pl.ds(FIRST, 640)
    fetches, stores = [], []
    for q in range(4):
        rows = pl.ds(FIRST + 160 * q, 160)
        from_rows = pl.ds(160 * q, 160)
        pairs = (
            (depth_hbm.at[:, rows, :], depth_ref.at[:, rows, :]),
            (rates_hbm.at[:, rows, :], rates_ref.at[middle, rows, :]),
            (head_hbm.at[from_rows, :], head_ref.at[from_rows, 0:640]),
        )
        fetches.append([pltpu.make_async_copy(*pair, sems.at[3 * q + n]) for n, pair in enumerate(pairs)])
        pairs = (
            (leave_ref.at[:, rows, :], leave_hbm.at[:, rows, :]),
            (depth_ref.at[:, rows, :], stay_hbm.at[:, rows, :]),
        )
        stores.append([pltpu.make_async_copy(*pair, sems.at[12 + 2 * q + n]) for n, pair in enumerate(pairs)])
    narrow = [
        pltpu.make_async_copy(rate_hbm, rates_ref.at[side, center, :], sems.at[20]),
        pltpu.make_async_copy(side_hbm, head_ref.at[:, 640:768], sems.at[21]),
    ]
    for copy in narrow + [copy for group in fetches for copy in group]:
        copy.start()
    for copy in narrow:
        copy.wait()

    def step(g, carry):
        rows = pl.ds(pl.multiple_of(g * 8, 8), 8)
        from_rows = pl.ds(pl.multiple_of(g * 8 - FIRST, 8), 8)
        for c in range(SLABS):
            depth = depth_ref[c, rows, :] + head_ref[from_rows, c * LANES : (c + 1) * LANES]
            leaving = leave(depth, jnp.abs(rates_ref[c, rows, :]))
            leave_ref[c, rows, :] = leaving
            depth_ref[c, rows, :] = depth - leaving
        return carry

    for q in range(4):
        for copy in fetches[q]:
            copy.wait()
        lax.fori_loop(2 + 20 * q, 22 + 20 * q, step, 0, unroll=10)
        for copy in stores[q]:
            copy.start()
    for group in stores:
        for copy in group:
            copy.wait()


def opening(depth, head, side, rates, rate):
    slab = pltpu.VMEM(depth.shape, F32)
    return pl.pallas_call(
        open_kernel,
        out_shape=(jax.ShapeDtypeStruct(depth.shape, F32),) * 2,
        in_specs=[HBM] * 5,
        out_specs=(HBM, HBM),
        scratch_shapes=[slab, pltpu.VMEM((640, 768), F32), slab, slab, pltpu.SemaphoreType.DMA((22,))],
        compiler_params=params(55_000_000),
        name="open",
    )(depth, head, side, rates, rate)


def route_kernel(
    edge_ref, ranges, up_ref, down_ref, table_ref, leave_hbm, stay_hbm, rates_hbm, codes_hbm, rate_hbm, code_hbm, slot_hbm,
    surface_hbm, spread_ref,
    leave_ref, stay_ref, rates_ref, codes_ref, slot_ref, surface_ref, next_ref, lake_ref, sums_ref, sems,
):
    middle, side, center = pl.ds(0, SLABS - 1), SLABS - 1, pl.ds(FIRST, 640)
    pairs = (
        (leave_hbm, leave_ref),
        (codes_hbm, codes_ref.at[middle]),
        (stay_hbm, stay_ref),
        (rates_hbm, rates_ref.at[middle]),
    )
    quarters = []
    for q in range(4):
        rows = pl.ds(FIRST + 160 * q, 160)
        quarters.append(
            [
                pltpu.make_async_copy(source.at[:, rows, :], into.at[:, rows, :], sems.at[4 * q + n])
                for n, (source, into) in enumerate(pairs)
            ]
        )
    narrow = [
        pltpu.make_async_copy(code_hbm, codes_ref.at[side, center, :], sems.at[16]),
        pltpu.make_async_copy(rate_hbm, rates_ref.at[side, center, :], sems.at[17]),
    ]
    slots = pltpu.make_async_copy(slot_hbm, slot_ref, sems.at[18])
    for copy in quarters[0] + narrow + quarters[1] + quarters[2] + quarters[3] + [slots]:
        copy.start()
    lane = lanes_of((8, LANES))

    def at(g):
        return pl.ds(pl.multiple_of(g * 8, 8), 8)

    eight = (8, LANES)
    for g, ref, offset, outside in ((1, up_ref, 6, edge_ref[0] == 1), (82, down_ref, 0, edge_ref[1] == 1)):
        rows = slice(g * 8, g * 8 + 8)
        two = slice(g * 8 + offset, g * 8 + offset + 2)
        for c in range(SLABS):
            four = ref[:, c * LANES : (c + 1) * LANES]
            rates_ref[c, rows, :] = jnp.ones(eight, F32)
            codes_ref[c, rows, :] = jnp.full(eight, -1, jnp.int32)
            leave_ref[c, rows, :] = jnp.zeros(eight, F32)
            stay_ref[c, rows, :] = jnp.zeros(eight, F32)
            leaving = leave(four[0:2], four[2:4])
            leave_ref[c, two, :] = leaving
            stay_ref[c, two, :] = four[0:2] - leaving
            rates_ref[c, two, :] = signed(four[2:4], four[6:8] > 0.5)
            codes_ref[c, two, :] = jnp.where(outside, -1, four[4:6].astype(jnp.int32))

    def gained(ref, g, slabs):
        east, middle, west = [], [], []
        base = g * 8
        for c in range(SLABS):
            here, above, below = (ref[c, pl.ds(base + d, 8), :] for d in (0, -1, 1))
            code, code_above, code_below = (codes_ref[c, pl.ds(base + d, 8), :] for d in (0, -1, 1))

            def pick(which, number, value):
                return jnp.where(which == number, value, 0.0)

            east.append(pick(code, 0, here) + pick(code_above, 1, above) + pick(code_below, 7, below))
            middle.append(pick(code_above, 2, above) + pick(code_below, 6, below))
            west.append(pick(code, 4, here) + pick(code_above, 3, above) + pick(code_below, 5, below))
        east = [pltpu.roll(value, 1, 1) for value in east]
        west = [pltpu.roll(value, LANES - 1, 1) for value in west]
        return [
            middle[c]
            + jnp.where(lane == 0, east[c - 1], east[c])
            + jnp.where(lane == LANES - 1, west[(c + 1) % SLABS], west[c])
            for c in range(slabs)
        ]

    def second(g, carry):
        rows = at(g)
        for c, gain in enumerate(gained(leave_ref, g, SLABS)):
            rate = rates_ref[c, rows, :]
            lake = rate < 0.0
            depth = stay_ref[c, rows, :] + gain
            kept = jnp.where(lake, 0.0, depth)
            leaving = leave(kept, jnp.abs(rate))
            next_ref[c, rows, :] = leaving
            stay_ref[c, rows, :] = kept - leaving
            if c < SLABS - 1:
                lake_ref[c, rows, :] = depth - kept
        return carry

    for q in range(4):
        for copy in quarters[q]:
            copy.wait()
        if q == 0:
            for copy in narrow:
                copy.wait()
        lax.fori_loop(1 + 20 * q, 21 + 20 * q, second, 0, unroll=20)
    for g in (81, 82):
        second(g, 0)

    def third(g, carry):
        rows = at(g)
        out = at(g - 2)
        for c, gain in enumerate(gained(next_ref, g, SLABS - 1)):
            depth = stay_ref[c, rows, :] + gain
            kept = jnp.where(rates_ref[c, rows, :] < 0.0, 0.0, depth)
            lake_ref[c, rows, :] += depth - kept
            surface_ref[out, c * LANES : (c + 1) * LANES] = kept
        return carry

    stores = []
    for q in range(5):
        lax.fori_loop(2 + 16 * q, 18 + 16 * q, third, 0, unroll=16)
        rows = pl.ds(128 * q, 128)
        store = pltpu.make_async_copy(surface_ref.at[rows, :], surface_hbm.at[rows, :], sems.at[19 + q])
        store.start()
        stores.append(store)
    slots.wait()
    sums_ref[...] = jnp.zeros(sums_ref.shape, F32)

    def layer(e, carry):
        def lake(slot, inner):
            g = ranges[0, slot] + e
            wanted = jnp.where(g < ranges[1, slot], slot, -1)
            g = jnp.minimum(g, 79)
            rows = at(g)
            from_rows = at(g + 2)
            into = pl.ds(pl.multiple_of(slot * 8, 8), 8)
            terms = []
            for c in range(SLABS - 1):
                mine = slot_ref[rows, c * LANES : (c + 1) * LANES] == wanted
                terms.append(jnp.where(mine, lake_ref[c, from_rows, :], 0.0))
            sums_ref[into, :] += (terms[0] + terms[1]) + (terms[2] + terms[3]) + terms[4]
            return inner

        return lax.fori_loop(0, LLOC, lake, carry, unroll=LLOC)

    lax.fori_loop(0, ranges[2, 0], layer, 0)
    tall = (LLOC, 8 * LLOC)
    gather = ((lanes_of(tall) >> 3) == rows_of(tall)).astype(F32).astype(BF16)
    totals = jnp.sum(select_dot(gather, sums_ref[...]), axis=1, keepdims=True)
    table = table_ref[...]
    owner = (table >> 6 == rows_of((LANES, LLOC))).astype(F32).astype(BF16)
    small = (LLOC, LLOC)
    turned = jnp.where(rows_of(small) == lanes_of(small), (table & 63).astype(F32), 0.0)
    number = jnp.sum(turned, axis=1, keepdims=True).astype(jnp.int32) == lanes_of((LLOC, LANES))
    spread_ref[...] = select_dot(owner, jnp.where(number, totals, 0.0))
    for store in stores:
        store.wait()


def route(edges, ranges, up, down, leaving, stay, rates, codes, rate, code, lake_slot, lake_table):
    slabs = (SLABS, ROWS, LANES)
    slab = pltpu.VMEM(slabs, F32)
    return pl.pallas_call(
        route_kernel,
        out_shape=(jax.ShapeDtypeStruct(lake_slot.shape, F32), jax.ShapeDtypeStruct((LANES, LANES), F32)),
        in_specs=[SMEM] * 2 + [VMEM] * 3 + [HBM] * 7,
        out_specs=(HBM, VMEM),
        scratch_shapes=[
            slab,
            slab,
            slab,
            pltpu.VMEM(slabs, jnp.int32),
            pltpu.VMEM(lake_slot.shape, jnp.int32),
            pltpu.VMEM(lake_slot.shape, F32),
            slab,
            slab,
            pltpu.VMEM((8 * LLOC, LANES), F32),
            pltpu.SemaphoreType.DMA((24,)),
        ],
        compiler_params=params(55_000_000),
        name="route",
    )(edges, ranges, up, down, lake_table.reshape(1, LLOC), leaving, stay, rates, codes, rate, code, lake_slot)


def pool_kernel(spread_ref, phase_ref, area_ref, crest_ref, level_ref, outflow_ref):
    inflow = jnp.sum(spread_ref[...], axis=0, keepdims=True)[:, :LLOC]
    area = area_ref[...]
    phase = phase_ref[...] + inflow / area
    excess = jnp.maximum(phase - crest_ref[...], 0.0)
    outflow = excess * jnp.sqrt(excess)
    level_ref[...] = phase - outflow / area
    outflow_ref[...] = outflow


def level_pool(spread, lake_phase, lake_area, lake_crest):
    row = jax.ShapeDtypeStruct((1, LLOC), F32)
    level, outflow = pl.pallas_call(
        pool_kernel,
        out_shape=(row, row),
        in_specs=[VMEM] * 4,
        out_specs=(VMEM,) * 2,
        compiler_params=params(50_000_000),
        name="pool",
    )(spread, *(value.reshape(1, LLOC) for value in (lake_phase, lake_area, lake_crest)))
    return level.reshape(LLOC), outflow.reshape(LLOC)


def body(
    moisture, conduct, rainfall, weights, land_tile, head, rate, flow_code, lake_slot, lake_table,
    lake_phase, lake_area, lake_crest,
):
    both = ("row", "col")
    at_row, at_col = lax.axis_index("row"), lax.axis_index("col")
    edges = jnp.stack(
        [at_row == 0, at_row == lax.axis_size("row") - 1, at_col == 0, at_col == lax.axis_size("col") - 1]
    ).astype(jnp.int32)
    payload = land_payload(land_tile, moisture, conduct, rainfall, weights)
    payload, rate, flow_code, lake_slot, head, moisture = lax.optimization_barrier(
        (payload, rate, flow_code, lake_slot, head, moisture)
    )
    arrived = lax.all_to_all(
        payload.reshape(RUNS, 1, RUN_ROWS * LANES), both, split_axis=0, concat_axis=0, tiled=True
    ).reshape(RUNS * RUN_ROWS, LANES)
    cols, new_moisture = rim(moisture, conduct, rainfall, rate, flow_code, lake_slot, head)
    left = lax.ppermute(cols[8:16], "col", ring("col", 1))
    right = lax.ppermute(cols[0:8], "col", ring("col", -1))
    rates, codes, ranges, top, bottom, picks = statics(rate, flow_code, lake_slot, head)
    side_rate, side_code, side_head, top, bottom = sides(edges, left, right, top, bottom)
    depth, top, bottom = place(top, bottom, picks, arrived)
    even = at_row % 2 == 0
    near = lax.ppermute(jnp.where(even, bottom, top), "row", swap("row", 0))
    far = lax.ppermute(jnp.where(even, top, bottom), "row", swap("row", 1))
    up = jnp.where(even, far, near)
    down = jnp.where(even, near, far)
    leaving, stay = opening(depth, head, side_head, rates, side_rate)
    surface, spread = route(
        edges, ranges, up, down, leaving, stay, rates, codes, side_rate, side_code, lake_slot, lake_table
    )
    spread = lax.all_to_all(
        spread.reshape(RUNS, 1, LANES), both, split_axis=0, concat_axis=0, tiled=True
    ).reshape(RUNS, LANES)
    level, outflow = level_pool(spread, lake_phase, lake_area, lake_crest)
    return (new_moisture, surface, level, outflow)


def solution(mesh):
    blocks = P(("row", "col"))
    layers = P(None, ("row", "col"))
    cells = P("row", "col")
    in_specs = (layers, layers, blocks, layers, blocks) + (cells,) * 4 + (blocks,) * 4
    out_specs = (layers, cells, blocks, blocks)
    return jax.shard_map(body, mesh=mesh, in_specs=in_specs, out_specs=out_specs, check_vma=False)
```
